32 devices in a mesh: gx: 2 (over core), gy: 4 (over y, x), gz: 4 (over z).
Axes of the slice: x: 2, y: 2, z: 4, core: 2. Of those that a mesh axis runs over, the one named last changes fastest.
Arguments:
- features: float32 [4, 8, 4, 128, 128], P('gx', 'gy', 'gz'), may hold values from -6 to 6
- positions: float32 [4, 8, 4, 3, 128], P('gx', 'gy', 'gz'), may hold values from 0 to 1
- counts: int32 [4, 8, 4], P('gx', 'gy', 'gz'), may hold values from 64 to 128, as said below
- waves: int32 [3, 2048], replicated, may hold values from -8 to 8
- filter_table: float32 [2048, 128], replicated, may hold values from -6 to 6
- w_value: float32 [128, 128], replicated, may hold values from -0.5 to 0.5
- w_charge: float32 [128, 128], replicated, may hold values from -0.5 to 0.5
- radial_mix: float32 [8, 128], replicated, may hold values from -2 to 2
- w_hidden: float32 [128, 256], replicated, may hold values from -0.5 to 0.5
- w_out: float32 [256, 128], replicated, may hold values from -0.375 to 0.375
Outputs:
- updated: float32 [4, 8, 4, 128, 128], P('gx', 'gy', 'gz')
The draws below stay inside these ranges and needn't reach their ends.
Inputs may be any that keep to these rules, and one draw needn't show every extreme that they name: `counts`: slots below a cell's count hold atoms, the others are padding.
All inputs are finite; a program needn't handle non-finite values.
Results may differ from the reference program's by a relative error of at most 0.0001.
Values sent between devices are 32-bit elements; how exact they have to be, the bound alone decides.
No kernel may reach another device: no remote copies, remote signals or barrier semaphores. Data moves between devices by JAX's collectives and lax.ppermute only.
A program may use at most 64 MiB of HBM per device.

```python
import math
import jax
import jax.numpy as jnp
from jax import lax

C = 128
K = 2048
B = 8
F = 256
A = 128
NCX = 4
NCY = 8
NCZ = 4


def draw_counts(key, part):
    cell_total = NCX * NCY * NCZ
    key_fill, key_top, key_low = jax.random.split(jax.random.fold_in(key, 11), 3)
    filled = jax.random.randint(key_fill, (cell_total,), A // 2, A + 1, dtype=jnp.int32)
    top_cell = jax.random.randint(key_top, (), 0, cell_total, dtype=jnp.int32)
    low_cell = (top_cell + 1 + jax.random.randint(key_low, (), 0, cell_total - 1, dtype=jnp.int32)) % cell_total
    cell_ids = jnp.arange(cell_total, dtype=jnp.int32)
    filled = jnp.where(cell_ids == top_cell, A, filled)
    filled = jnp.where(cell_ids == low_cell, A // 2, filled)
    return filled.reshape((NCX, NCY, NCZ))


def touch_ends(values, own_key, smallest, top_value):
    place = [jax.random.randint(jax.random.fold_in(own_key, axis), (), 0, length) for axis, length in enumerate(values.shape)]
    longest = values.shape.index(max(values.shape))
    next_to = place[:longest] + [(place[longest] + 1) % values.shape[longest]] + place[longest + 1:]
    return values.at[tuple(place)].set(smallest).at[tuple(next_to)].set(top_value)


def levels(rng, extent, shards, low, largest):
    def one(axis_at, shards_of):
        draws = jax.random.uniform(jax.random.fold_in(jax.random.fold_in(rng, 6), axis_at), (shards_of,), jnp.float32, low / len(shards), largest / len(shards))
        return jnp.repeat(jnp.exp(draws), extent[axis_at] // shards_of).reshape((-1,) + (1,) * (len(extent) - axis_at - 1))

    factor_of = one(*shards[0])
    for cut in shards[1:]:
        factor_of = factor_of * one(*cut)
    return factor_of


def bell_draw(rng, dims, deviation, reach, cuts=(), held_as=jnp.bfloat16):
    drawn = jax.random.normal(rng, dims, jnp.float32) * deviation
    if len(cuts) > 0:
        drawn = levels(rng, dims, cuts, -0.22, 0.18) * drawn
    return jnp.clip(drawn, min=-reach, max=reach).astype(held_as)


def setup_inputs(seed: int = 0) -> dict:
    key_list = jax.random.split(jax.random.key(seed), 11)
    return {
        "features": bell_draw(key_list[0], (NCX, NCY, NCZ, C, A), 1.0, 6.0, ((0, 2), (1, 4), (2, 4)), jnp.float32),
        "positions": jnp.clip(1.0 * jax.random.uniform(key_list[1], (NCX, NCY, NCZ, 3, A), jnp.float32) ** levels(key_list[1], (NCX, NCY, NCZ, 3, A), ((0, 2), (1, 4), (2, 4)), -0.2, 0.2), 0.0, 1.0),
        "counts": draw_counts(jax.random.fold_in(key_list[10], 71), 0),
        "waves": touch_ends(jax.random.randint(key_list[3], (3, K), -8, 9), jax.random.fold_in(key_list[3], 1), -8, 8).astype(jnp.int32),
        "filter_table": bell_draw(key_list[4], (K, C), 1.0, 6.0, (), jnp.float32),
        "w_value": bell_draw(key_list[5], (C, C), C ** -0.5, 0.5, (), jnp.float32),
        "w_charge": bell_draw(key_list[6], (C, C), C ** -0.5, 0.5, (), jnp.float32),
        "radial_mix": bell_draw(key_list[7], (B, C), B ** -0.5, 2.0, (), jnp.float32),
        "w_hidden": bell_draw(key_list[8], (C, F), C ** -0.5, 0.5, (), jnp.float32),
        "w_out": bell_draw(key_list[9], (F, C), F ** -0.5, 0.375, (), jnp.float32),
    }


highest = lax.Precision.HIGHEST
cut_radius = 1.0
message_scale = 0.125

def radial_kernel(own_pos, nearby_pos, shift, self_pair):
    offsets = shift[:, None, None] + nearby_pos[..., :, None, :] - own_pos[..., :, :, None]
    squared = lax.optimization_barrier(jnp.sum(offsets * offsets, axis=-3))
    distance = jnp.sqrt(squared)
    envelope = jnp.square(jnp.maximum(1.0 - squared / (cut_radius * cut_radius), 0.0))
    envelope = envelope * (1.0 - self_pair * jnp.eye(A, dtype=jnp.float32))
    centres = jnp.arange(B, dtype=jnp.float32) * (cut_radius / (B - 1))
    scaled = (distance[..., None, :, :] - centres[:, None, None]) * ((B - 1) / cut_radius)
    return jnp.exp(-scaled * scaled) * envelope[..., None, :, :]

def pair_term(own_pos, nearby, shift, self_pair, radial_mix):
    channels = nearby.shape[-2] - 3
    kernel = radial_kernel(own_pos, nearby[..., channels:, :], shift, self_pair)
    weighted = radial_mix[:, :, None] * nearby[..., None, :channels, :]
    return jnp.einsum('...bij,...bcj->...ci', kernel, weighted, precision=highest)

def short_range(values, positions, radial_mix):
    packed = jnp.concatenate([values, positions], axis=3)
    summed = jnp.zeros_like(values)
    for step in range(27):
        moves = (step // 9 - 1, step // 3 % 3 - 1, step % 3 - 1)
        nearby = jnp.roll(packed, (-moves[0], -moves[1], -moves[2]), axis=(0, 1, 2))
        shift = jnp.array(moves, dtype=jnp.float32)
        self_pair = 1.0 if step == 13 else 0.0
        pair_sum = lax.map(lambda slab_pair: pair_term(slab_pair[0], slab_pair[1], shift, self_pair, radial_mix), (positions, nearby))
        summed = summed + pair_sum
    return summed

def plane_waves(frac_x, frac_y, frac_z, waves):
    expand = (waves.shape[1],) + (1,) * frac_x.ndim
    wave_float = waves.astype(jnp.float32)
    angle = wave_float[0].reshape(expand) * frac_x + wave_float[1].reshape(expand) * frac_y + wave_float[2].reshape(expand) * frac_z
    angle = angle * (2.0 * math.pi)
    return (jnp.cos(angle), jnp.sin(angle))

def slab_waves(slab_index, slab_pos, waves):
    rows_y = jnp.arange(NCY, dtype=jnp.float32)[:, None, None]
    rows_z = jnp.arange(NCZ, dtype=jnp.float32)[None, :, None]
    frac_x = (slab_index.astype(jnp.float32) + slab_pos[:, :, 0, :]) / NCX
    frac_y = (rows_y + slab_pos[:, :, 1, :]) / NCY
    frac_z = (rows_z + slab_pos[:, :, 2, :]) / NCZ
    return plane_waves(frac_x, frac_y, frac_z, waves)

def long_range(charges, positions, waves, filter_table):
    slab_ids = jnp.arange(NCX, dtype=jnp.int32)

    def accumulate(summed, inputs):
        cosine, sine = slab_waves(inputs[0], inputs[1], waves)
        real_part = jnp.einsum('kyza,yzca->kc', cosine, inputs[2], precision=highest)
        imag_part = jnp.einsum('kyza,yzca->kc', sine, inputs[2], precision=highest)
        return (summed + jnp.stack([real_part, imag_part]), None)
    factors, unused = lax.scan(accumulate, jnp.zeros((2, K, C), jnp.float32), (slab_ids, positions, charges))
    normalizer = 1.0 / math.sqrt(NCX * NCY * NCZ * A)
    filtered = factors * normalizer * filter_table[None]

    def slab_potential(inputs):
        cosine, sine = slab_waves(inputs[0], inputs[1], waves)
        first = jnp.einsum('kc,kyza->yzca', filtered[0], cosine, precision=highest)
        second = jnp.einsum('kc,kyza->yzca', filtered[1], sine, precision=highest)
        return (first + second) * (1.0 / math.sqrt(K))
    return lax.map(slab_potential, (slab_ids, positions))

def reference(features, positions, counts, waves, filter_table, w_value, w_charge, radial_mix, w_hidden, w_out):
    slot_ids = lax.broadcasted_iota(jnp.int32, (NCX, NCY, NCZ, A), 3)
    present = (slot_ids < counts[..., None]).astype(jnp.float32)[..., None, :]
    values = jnp.einsum('dc,xyzda->xyzca', w_value, features, precision=highest) * present
    charges = jnp.einsum('dc,xyzda->xyzca', w_charge, features, precision=highest) * present
    messages = short_range(values, positions, radial_mix)
    potentials = long_range(charges, positions, waves, filter_table)
    mixed = features + message_scale * messages + potentials
    hidden = jax.nn.silu(jnp.einsum('cf,xyzca->xyzfa', w_hidden, mixed, precision=highest))
    return (mixed + jnp.einsum('fc,xyzfa->xyzca', w_out, hidden, precision=highest)) * present
```

```python
import functools
import math

import numpy as np

import jax
import jax.numpy as jnp
from jax import lax
from jax.experimental import pallas as pl
from jax.experimental.pallas import tpu as pltpu
from jax.sharding import PartitionSpec as P


HIGH = lax.Precision.HIGH
message_scale = 0.125
bf16 = jnp.bfloat16
f32 = jnp.float32
VMEM_LIMIT = 56 * 1024 * 1024


def ring(block, axis, step):
    count = lax.axis_size(axis)
    step = step % count
    if step == 0:
        return block
    return lax.ppermute(block, axis, [(i, (i + step) % count) for i in range(count)])


def split(x):
    high = x.astype(bf16)
    low = (x - high.astype(f32)).astype(bf16)
    return high, low


def whole():
    return pl.BlockSpec(memory_space=pltpu.VMEM)


def params():
    return pltpu.CompilerParams(vmem_limit_bytes=VMEM_LIMIT)


SIN = [math.pi ** (2 * n + 1) * (-1) ** n / math.factorial(2 * n + 1) for n in range(7)]
COS = [math.pi ** (2 * n) * (-1) ** n / math.factorial(2 * n) for n in range(7)]


def poly(coefficients, t):
    acc = jnp.full_like(t, coefficients[-1])
    for c in coefficients[-2::-1]:
        acc = acc * t + c
    return acc


def turns(u):
    u = u - jnp.round(u)
    t = u * u
    twice_sine = poly([2.0 * c for c in SIN], t) * u
    cosine = poly(COS, t)
    return 1.0 - 0.5 * twice_sine * twice_sine, twice_sine * cosine


def factor_kernel(count, rows_of, *refs):
    waves_ref = refs[0]
    blocks = refs[1 : 1 + count]
    factor_ref, high_ref, low_ref, weight_ref = refs[1 + count :]
    cells, _, slots = blocks[0].shape
    channels = factor_ref.shape[-1]
    waves_here = waves_ref.shape[0]

    @pl.when(pl.program_id(0) == 0)
    def _():
        for n, block in enumerate(blocks):
            for cell in range(cells):
                at = (n * cells + cell) * slots
                high, low = split(block[cell, :channels, :].T)
                weight_ref[at : at + slots, :channels] = high
                weight_ref[at : at + slots, channels:] = low

    wave_x = waves_ref[:, 0:1]
    wave_y = waves_ref[:, 1:2]
    wave_z = waves_ref[:, 2:3]
    for n, block in enumerate(blocks):
        for cell in range(cells):
            at = (n * cells + cell) * slots
            frac = block[cell, rows_of : rows_of + 3, :]
            u = wave_x * frac[0:1] + wave_y * frac[1:2] + wave_z * frac[2:3]
            cosine, sine = turns(u)
            high, low = split(cosine)
            high_ref[:waves_here, at : at + slots] = high
            low_ref[:waves_here, at : at + slots] = low
            high, low = split(sine)
            high_ref[waves_here:, at : at + slots] = high
            low_ref[waves_here:, at : at + slots] = low
    both = jnp.dot(high_ref[...], weight_ref[...], preferred_element_type=f32)
    both = both + jnp.dot(low_ref[...], weight_ref[...], preferred_element_type=f32)
    factor_ref[...] = both[:, :channels] + both[:, channels:]


def partial_factors(waves, blocks, channels, frac_row):
    total = waves.shape[0]
    chunk = math.gcd(total, 128)
    cells, rows, slots = blocks[0].shape
    atoms = len(blocks) * cells * slots
    return pl.pallas_call(
        functools.partial(factor_kernel, len(blocks), frac_row),
        grid=(total // chunk,),
        in_specs=[pl.BlockSpec((chunk, 3), lambda j: (j, 0))] + [whole()] * len(blocks),
        out_specs=[
            pl.BlockSpec((2 * chunk, channels), lambda j: (j, 0)),
            pl.BlockSpec((2 * chunk, atoms), lambda j: (j, 0)),
            pl.BlockSpec((2 * chunk, atoms), lambda j: (j, 0)),
        ],
        out_shape=[
            jax.ShapeDtypeStruct((2 * total, channels), f32),
            jax.ShapeDtypeStruct((2 * total, atoms), bf16),
            jax.ShapeDtypeStruct((2 * total, atoms), bf16),
        ],
        scratch_shapes=[pltpu.VMEM((atoms, 2 * channels), bf16)],
        compiler_params=params(),
        cost_estimate=pl.CostEstimate(
            flops=60 * total * atoms, bytes_accessed=8 * total * atoms, transcendentals=0
        ),
        name="factors",
    )(waves, *blocks)


def filter_kernel(*refs):
    parts, (weight_ref, table_ref, out_ref) = refs[:-3], refs[-3:]
    summed = parts[0][...]
    for part in parts[1:]:
        summed = summed + part[...]
    projected = jnp.dot(summed, weight_ref[...], precision=HIGH, preferred_element_type=f32)
    out_ref[...] = projected * table_ref[...]


def filtered_piece(parts, w_charge, table):
    return pl.pallas_call(
        filter_kernel,
        in_specs=[whole()] * (len(parts) + 2),
        out_specs=whole(),
        out_shape=jax.ShapeDtypeStruct(table.shape, f32),
        compiler_params=params(),
        name="filter",
    )(*parts, w_charge, table)


def potential_kernel(groups, pieces, index_ref, *refs):
    held = refs[:groups]
    high_ref, low_ref = refs[groups : groups + 2]
    outs = refs[groups + 2 : -2]
    ordered_ref, turned_ref = refs[-2:]
    step = pl.program_id(0)
    channels = ordered_ref.shape[-1]
    piece = held[0].shape[0] // pieces

    @pl.when(step == 0)
    def _():
        for group in range(groups):
            for n in range(pieces):
                at = pl.multiple_of(index_ref[group * pieces + n] * piece, piece)
                ordered_ref[pl.ds(at, piece), :] = held[group][n * piece : (n + 1) * piece, :]
        high, low = split(ordered_ref[...].T)
        turned_ref[:channels, :] = high
        turned_ref[channels:, :] = low

    both = jnp.dot(turned_ref[...], high_ref[...], preferred_element_type=f32)
    third = jnp.dot(turned_ref[:channels, :], low_ref[...], preferred_element_type=f32)
    potential = both[:channels] + both[channels:] + third
    for n, out in enumerate(outs):

        @pl.when(step == n)
        def _(out=out):
            cells, _, slots = out.shape
            for cell in range(cells):
                out[cell] = potential[:, cell * slots : (cell + 1) * slots]


def potentials_of(index, held, pieces, high, low, cells, slots):
    rows, atoms = high.shape
    channels = held[0].shape[-1]
    count = atoms // (cells * slots)
    span = cells * slots
    return pl.pallas_call(
        functools.partial(potential_kernel, len(held), pieces),
        grid_spec=pltpu.PrefetchScalarGridSpec(
            num_scalar_prefetch=1,
            grid=(count,),
            in_specs=[pl.BlockSpec(h.shape, lambda j, index: (0, 0)) for h in held]
            + [pl.BlockSpec((rows, span), lambda j, index: (0, j))] * 2,
            out_specs=[pl.BlockSpec((cells, channels, slots), lambda j, index: (0, 0, 0))] * count,
            scratch_shapes=[
                pltpu.VMEM((rows, channels), f32),
                pltpu.VMEM((2 * channels, rows), bf16),
            ],
        ),
        out_shape=[jax.ShapeDtypeStruct((cells, channels, slots), f32)] * count,
        compiler_params=params(),
        cost_estimate=pl.CostEstimate(
            flops=6 * rows * atoms * channels, bytes_accessed=4 * rows * atoms, transcendentals=0
        ),
        name="potentials",
    )(index, *held, high, low)


def message_kernel(
    basis, own_z, step_ref, own_ref, ext_ref, mix_ref, value_ref, out_ref,
    cell_ref, own_col_ref, left_ref, right_ref,
):
    step = pl.program_id(0)
    across, along, planes, _, slots = ext_ref.shape
    channels = value_ref.shape[0]
    place_x = step_ref[0, step]
    place_y = step_ref[1, step]
    plane = step_ref[2, step]
    shift_z = step_ref[3, step].astype(f32)
    own = step_ref[4, step]
    first = step_ref[5, step]

    @pl.when(step == 0)
    def _():
        def turn(n, carry):
            x = n // (along * planes)
            y = (n // planes) % along
            z = n % planes
            high, low = split(ext_ref[x, y, z, :channels, :].T)
            cell_ref[n, :, :channels] = high
            cell_ref[n, :, channels:] = low
            return carry

        lax.fori_loop(0, across * along * planes, turn, 0)

    for axis in range(3):
        row = own_ref[own, channels + axis : channels + axis + 1, :]
        own_col_ref[axis] = jnp.broadcast_to(row, (slots, slots)).T

    near = []
    for n in range(9):
        move_x, move_y = n // 3 - 1, n % 3 - 1
        x = place_x + 1 + move_x
        y = place_y + 1 + move_y
        row = (x * along + y) * planes + plane
        cell = cell_ref[row]
        right_ref[n * slots : (n + 1) * slots, :] = cell
        right_ref[(9 + n) * slots : (10 + n) * slots, :] = cell
        at = ext_ref[x, y, plane, channels : channels + 3, :]
        near.append((at[0:1] + float(move_x), at[1:2] + float(move_y), at[2:3] + shift_z))

    tile = 16

    def rows(m, carry):
        at = pl.multiple_of(m * tile, tile)
        own_x = own_col_ref[0, pl.ds(at, tile), :]
        own_y = own_col_ref[1, pl.ds(at, tile), :]
        own_z_pos = own_col_ref[2, pl.ds(at, tile), :]
        for n in range(9):
            dx = near[n][0] - own_x
            dy = near[n][1] - own_y
            dz = near[n][2] - own_z_pos
            squared = dx * dx + dy * dy + dz * dz
            distance = squared * lax.rsqrt(jnp.maximum(squared, 1e-30))
            envelope = jnp.maximum(1.0 - squared, 0.0)
            term = envelope * envelope * jnp.exp(squared * (-float((basis - 1) ** 2)))
            ratio = jnp.exp(distance * (2.0 * (basis - 1)))
            if own_z and n == 4:
                i = lax.broadcasted_iota(jnp.int32, (tile, slots), 0) + at
                j = lax.broadcasted_iota(jnp.int32, (tile, slots), 1)
                same = jnp.logical_and(i == j, step_ref[3, step] == 0)
                term = jnp.where(same, 0.0, term)
            for b in range(basis):
                if b > 0:
                    term = term * ratio
                high, low = split(term)
                left_ref[pl.ds(b * slots + at, tile), n * slots : (n + 1) * slots] = high
                left_ref[pl.ds(b * slots + at, tile), (9 + n) * slots : (10 + n) * slots] = low
        return carry

    lax.fori_loop(0, slots // tile, rows, 0)
    both = jnp.dot(left_ref[...], right_ref[...], preferred_element_type=f32)
    gathered = both[:, :channels] + both[:, channels:]
    projected = jnp.dot(gathered, value_ref[...], precision=HIGH, preferred_element_type=f32)
    message = projected[:slots] * mix_ref[0:1, :]
    for b in range(1, basis):
        message = message + projected[b * slots : (b + 1) * slots] * mix_ref[b : b + 1, :]
    message = message.T

    @pl.when(first == 1)
    def _():
        out_ref[0] = message

    @pl.when(first == 0)
    def _():
        out_ref[0] += message


def pair_messages(steps, own_z, own, ext, mix, w_value):
    cells, _, slots = own.shape
    basis, channels = mix.shape
    across, along, planes = ext.shape[:3]
    count = steps.shape[1]
    return pl.pallas_call(
        functools.partial(message_kernel, basis, own_z),
        grid_spec=pltpu.PrefetchScalarGridSpec(
            num_scalar_prefetch=1,
            grid=(count,),
            in_specs=[whole()] * 4,
            out_specs=pl.BlockSpec((1, channels, slots), lambda s, steps: (steps[4, s], 0, 0)),
            scratch_shapes=[
                pltpu.VMEM((across * along * planes, slots, 2 * channels), bf16),
                pltpu.VMEM((3, slots, slots), f32),
                pltpu.VMEM((basis * slots, 18 * slots), bf16),
                pltpu.VMEM((18 * slots, 2 * channels), bf16),
            ],
        ),
        out_shape=jax.ShapeDtypeStruct((cells, channels, slots), f32),
        compiler_params=params(),
        cost_estimate=pl.CostEstimate(
            flops=count * 8 * basis * slots * 9 * slots * channels, bytes_accessed=1 << 20,
            transcendentals=0,
        ),
        name="messages",
    )(jnp.asarray(steps), own, ext, mix, w_value)


def visits(cells_x, cells_y, cells_z, inside):
    table, seen = [], set()
    for x in range(cells_x):
        for y in range(cells_y):
            for z in range(cells_z):
                own = (x * cells_y + y) * cells_z + z
                for shift in (-1, 0, 1):
                    plane = z + shift
                    here = 0 <= plane < cells_z
                    if here != inside:
                        continue
                    if not here:
                        plane = 0 if plane < 0 else 1
                    table.append((x, y, plane, shift, own, int(own not in seen)))
                    seen.add(own)
    return np.array(table, np.int32).T.copy()


def mlp_kernel(count, *refs):
    counts_ref, feature_ref = refs[:2]
    messages = refs[2:4]
    potentials = refs[4 : 4 + count]
    hidden_ref, back_ref, out_ref = refs[4 + count :]
    cells, channels, slots = feature_ref.shape
    columns = []
    for cell in range(cells):
        mixed = feature_ref[cell] + message_scale * (messages[0][cell] + messages[1][cell])
        for potential in potentials:
            mixed = mixed + potential[cell]
        columns.append(mixed)
    mixed = jnp.concatenate(columns, axis=1)
    inner = jnp.dot(hidden_ref[...].T, mixed, precision=HIGH, preferred_element_type=f32)
    hidden = inner * jax.nn.sigmoid(inner)
    updated = mixed + jnp.dot(back_ref[...].T, hidden, precision=HIGH, preferred_element_type=f32)
    slot = lax.broadcasted_iota(jnp.int32, (channels, slots), 1)
    for cell in range(cells):
        part = updated[:, cell * slots : (cell + 1) * slots]
        out_ref[cell] = jnp.where(slot < counts_ref[cell], part, 0.0)


def atom_mlp(counts, features, messages, potentials, w_hidden, w_out):
    return pl.pallas_call(
        functools.partial(mlp_kernel, len(potentials)),
        in_specs=[pl.BlockSpec(memory_space=pltpu.SMEM)]
        + [whole()] * (5 + len(potentials)),
        out_specs=whole(),
        out_shape=jax.ShapeDtypeStruct(features.shape, f32),
        compiler_params=params(),
        name="atom_mlp",
    )(counts, features, *messages, *potentials, w_hidden, w_out)


def along_y(block, low, high):
    return jnp.concatenate([low, block, high], axis=1)


def with_x(block):
    low = ring(block[-1:], "gx", 1)
    high = ring(block[:1], "gx", -1)
    return jnp.concatenate([low, block, high], axis=0)


def shards(
    features, positions, counts, waves, filter_table, w_value, w_charge, radial_mix, w_hidden, w_out
):
    cells_x, cells_y, cells_z, channels, slots = features.shape
    basis = radial_mix.shape[0]
    total_waves = waves.shape[1]
    size_x, size_y, size_z = (lax.axis_size(a) for a in ("gx", "gy", "gz"))
    at_x, at_y, at_z = (lax.axis_index(a) for a in ("gx", "gy", "gz"))
    grid = (cells_x * size_x, cells_y * size_y, cells_z * size_z)
    cells = cells_x * cells_y * cells_z

    shape = (cells_x, cells_y, cells_z, 1, slots)
    occupied = lax.broadcasted_iota(jnp.int32, shape, 4) < counts[..., None, None]
    fractions = []
    for axis, (at, here) in enumerate(((at_x, cells_x), (at_y, cells_y), (at_z, cells_z))):
        cell = lax.broadcasted_iota(jnp.int32, shape, axis) + at * here
        fractions.append((cell.astype(f32) + positions[..., axis : axis + 1, :]) / grid[axis])
    packed = jnp.concatenate(
        [jnp.where(occupied, features, 0.0), positions] + fractions + [jnp.zeros_like(fractions[0])] * 2,
        axis=3,
    )
    rows = packed.shape[3]

    gathered = [packed] + [ring(packed, "gy", s) for s in range(1, size_y)]
    below_z = ring(packed, "gz", 1)[:, :, -1:]
    above_z = ring(packed, "gz", -1)[:, :, :1]

    share = total_waves // size_y
    own_waves = lax.dynamic_slice_in_dim(waves, at_y * share, share, 1).astype(f32).T
    flat = [block.reshape(cells, rows, slots) for block in gathered]
    factors, high, low = partial_factors(own_waves, flat, channels, channels + 3)

    half = factors.shape[0] // size_x
    summed = lax.dynamic_slice_in_dim(factors, at_x * half, half, 0)
    for s in range(1, size_x):
        other = lax.rem(at_x + s, size_x)
        summed = summed + ring(lax.dynamic_slice_in_dim(factors, other * half, half, 0), "gx", s)
    piece = half // size_z
    parts = [lax.dynamic_slice_in_dim(summed, at_z * piece, piece, 0)]
    for s in range(1, size_z):
        other = lax.rem(at_z + s, size_z)
        parts.append(ring(lax.dynamic_slice_in_dim(summed, other * piece, piece, 0), "gz", s))
    scale = 1.0 / math.sqrt(grid[0] * grid[1] * grid[2] * slots) / math.sqrt(total_waves)
    chunk = math.gcd(share, 128)
    table = lax.dynamic_slice_in_dim(filter_table, at_y * share, share, 0) * scale
    table = jnp.broadcast_to(
        table.reshape(share // chunk, 1, chunk, channels), (share // chunk, 2, chunk, channels)
    ).reshape(2 * share, channels)
    table = lax.dynamic_slice_in_dim(table, at_x * half + at_z * piece, piece, 0)
    filtered = filtered_piece(parts, w_charge, table)

    held_z = jnp.concatenate([filtered] + [ring(filtered, "gz", s) for s in range(1, size_z)], axis=0)
    held = [held_z] + [ring(held_z, "gx", s) for s in range(1, size_x)]
    index = jnp.stack(
        [
            lax.rem(at_x - s + size_x, size_x) * size_z + lax.rem(at_z - t + size_z, size_z)
            for s in range(size_x)
            for t in range(size_z)
        ]
    ).astype(jnp.int32)

    own = packed.reshape(cells, rows, slots)
    plane = with_x(along_y(packed, gathered[1 % size_y][:, -1:], gathered[-1 % size_y][:, :1]))
    sides = jnp.concatenate([below_z, above_z], axis=2)
    sides = along_y(sides, ring(sides[:, -1:], "gy", 1), ring(sides[:, :1], "gy", -1))
    sides = with_x(sides)
    squares = jnp.arange(basis, dtype=f32) ** 2
    mix = radial_mix * jnp.exp(-squares)[:, None]
    near = pair_messages(visits(cells_x, cells_y, cells_z, True), True, own, plane, mix, w_value)
    far = pair_messages(visits(cells_x, cells_y, cells_z, False), False, own, sides, mix, w_value)

    found = potentials_of(index, held, held_z.shape[0] // piece, high, low, cells, slots)
    returned = [found[0]] + [ring(found[s], "gy", -s) for s in range(1, size_y)]

    updated = atom_mlp(
        counts.reshape(cells), features.reshape(cells, channels, slots), [near, far], returned,
        w_hidden, w_out,
    )
    return updated.reshape(features.shape)


def solution(mesh):
    placed = (
        P("gx", "gy", "gz", None, None),
        P("gx", "gy", "gz", None, None),
        P("gx", "gy", "gz"),
        P(),
        P(),
        P(),
        P(),
        P(),
        P(),
        P(),
    )
    return jax.shard_map(
        shards,
        mesh=mesh,
        in_specs=placed,
        out_specs=P("gx", "gy", "gz", None, None),
        check_vma=False,
    )
```

```python
import functools
import math

import numpy as np

import jax
import jax.numpy as jnp
from jax import lax
from jax.experimental import pallas as pl
from jax.experimental.pallas import tpu as pltpu
from jax.sharding import PartitionSpec as P


HIGH = lax.Precision.HIGH
message_scale = 0.125
bf16 = jnp.bfloat16
f32 = jnp.float32
VMEM_LIMIT = 28 * 1024 * 1024


LOG2E = math.log2(math.e)


def partner(i, step, count):
    return i ^ step


def exchange(block, axis, step):
    count = lax.axis_size(axis)
    pairs = [(i, partner(i, step, count)) for i in range(count)]
    return lax.ppermute(block, axis, pairs)


def is_even(axis):
    if lax.axis_size(axis) % 2:
        return jnp.bool_(True)
    return lax.rem(lax.axis_index(axis), 2) == 0


def neighbours(low, high, axis, same=False):
    count = lax.axis_size(axis)
    if count == 1:
        return low, high
    if count % 2:
        up = lax.ppermute(low, axis, [(i, (i - 1) % count) for i in range(count)])
        down = lax.ppermute(high, axis, [(i, (i + 1) % count) for i in range(count)])
        return up, down
    even = is_even(axis)
    first = high if same else jnp.where(even, high, low)
    second = low if same else jnp.where(even, low, high)
    one = [(i, i ^ 1) for i in range(count)]
    two = [(i, (i + 1 if i % 2 else i - 1) % count) for i in range(count)]
    return lax.ppermute(first, axis, one), lax.ppermute(second, axis, two)


def below_above(low, high, axis):
    first, second = neighbours(low, high, axis)
    even = is_even(axis)
    return jnp.where(even, second, first), jnp.where(even, first, second)


def split(x):
    high = x.astype(bf16)
    low = (x - high.astype(f32)).astype(bf16)
    return high, low


def whole():
    return pl.BlockSpec(memory_space=pltpu.VMEM)


def params():
    return pltpu.CompilerParams(vmem_limit_bytes=VMEM_LIMIT)


def pack_kernel(grid, place_ref, counts_ref, feature_ref, position_ref, out_ref):
    cells, channels, slots = feature_ref.shape
    slot = lax.broadcasted_iota(jnp.int32, (channels, slots), 1)
    blank = jnp.zeros((2, slots), f32)
    for cell in range(cells):
        out_ref[cell, :channels, :] = jnp.where(slot < counts_ref[cell], feature_ref[cell], 0.0)
        at = position_ref[cell]
        rows = [at]
        for axis in range(3):
            here = place_ref[cell * 3 + axis].astype(f32)
            rows.append((at[axis : axis + 1] + here) * (1.0 / grid[axis]))
        out_ref[cell, channels:, :] = jnp.concatenate(rows + [blank], axis=0)


def pack(grid, place, counts, features, positions):
    cells, channels, slots = features.shape
    smem = pl.BlockSpec(memory_space=pltpu.SMEM)
    return pl.pallas_call(
        functools.partial(pack_kernel, grid),
        in_specs=[smem, smem, whole(), whole()],
        out_specs=whole(),
        out_shape=jax.ShapeDtypeStruct((cells, channels + 8, slots), f32),
        compiler_params=params(),
        name="pack",
    )(place, counts, features, positions)


def fitted(function, terms):
    t = 0.125 * (1.0 + np.cos(np.pi * (np.arange(terms) + 0.5) / terms))
    solved = np.linalg.solve(np.vander(t, terms, increasing=True), function(np.sqrt(t)))
    return [float(c) for c in solved]


SIN = fitted(lambda u: 2.0 * np.sin(np.pi * u) / u, 5)
COS = fitted(lambda u: np.cos(np.pi * u), 5)


def poly(coefficients, t):
    acc = t * coefficients[-1] + coefficients[-2]
    for c in coefficients[-3::-1]:
        acc = acc * t + c
    return acc


def turns(u):
    u = u - jnp.round(u)
    t = u * u
    twice_sine = poly(SIN, t) * u
    cosine = poly(COS, t)
    return 1.0 - 0.5 * twice_sine * twice_sine, twice_sine * cosine


def factor_kernel(parts, chunk, first, at_ref, waves_ref, block_ref, *refs):
    before = refs[: 0 if first else parts]
    refs = refs[len(before) :]
    after, wave_ref, weight_ref = refs[:parts], refs[parts], refs[parts + 1]
    cells, _, slots = block_ref.shape
    channels = after[0].shape[-1]
    span = cells * slots
    total = waves_ref.shape[0]
    for cell in range(cells):
        high, low = split(block_ref[cell, :channels, :])
        for at in (cell * slots, span + cell * slots):
            weight_ref[:channels, at : at + slots] = high
            weight_ref[channels:, at : at + slots] = low

    def some(j, carry):
        here = pl.multiple_of(j * chunk, chunk)
        wave_x = waves_ref[pl.ds(here, chunk), 0:1]
        wave_y = waves_ref[pl.ds(here, chunk), 1:2]
        wave_z = waves_ref[pl.ds(here, chunk), 2:3]
        row = pl.multiple_of(j * 2 * chunk, 2 * chunk)
        for cell in range(cells):
            at = cell * slots
            frac = block_ref[cell, channels + 3 : channels + 6, :]
            u = wave_x * frac[0:1] + wave_y * frac[1:2] + wave_z * frac[2:3]
            cosine, sine = turns(u)
            high, low = split(cosine)
            wave_ref[pl.ds(row, chunk), at : at + slots] = high
            wave_ref[pl.ds(row, chunk), span + at : span + at + slots] = low
            high, low = split(sine)
            wave_ref[pl.ds(row + chunk, chunk), at : at + slots] = high
            wave_ref[pl.ds(row + chunk, chunk), span + at : span + at + slots] = low
        both = lax.dot_general(
            wave_ref[pl.ds(row, 2 * chunk), :], weight_ref[...], (((1,), (1,)), ((), ())),
            preferred_element_type=f32,
        )
        both = both[:, :channels] + both[:, channels:]
        per_part = total // chunk // parts
        part = lax.rem(j // per_part - at_ref[0] + parts, parts)
        row = pl.multiple_of(lax.rem(j, per_part) * 2 * chunk, 2 * chunk)
        for n in range(parts):

            @pl.when(part == n)
            def _(n=n):
                if first:
                    after[n][pl.ds(row, 2 * chunk), :] = both
                else:
                    after[n][pl.ds(row, 2 * chunk), :] = before[n][pl.ds(row, 2 * chunk), :] + both

        return carry

    lax.fori_loop(0, total // chunk, some, 0)


def partial_factors(at, waves, block, before, parts):
    total = waves.shape[0]
    chunk = math.gcd(total // parts, 128)
    cells, rows, slots = block.shape
    channels = rows - 8
    span = cells * slots
    out = [jax.ShapeDtypeStruct((2 * total // parts, channels), f32)] * parts
    return pl.pallas_call(
        functools.partial(factor_kernel, parts, chunk, not before),
        in_specs=[pl.BlockSpec(memory_space=pltpu.SMEM)] + [whole()] * (2 + len(before)),
        out_specs=[whole()] * (parts + 1),
        out_shape=out + [jax.ShapeDtypeStruct((2 * total, 2 * span), bf16)],
        scratch_shapes=[pltpu.VMEM((2 * channels, 2 * span), bf16)],
        compiler_params=params(),
        cost_estimate=pl.CostEstimate(
            flops=8 * total * span * channels, bytes_accessed=8 * total * span, transcendentals=0
        ),
        name="factors",
    )(at, waves, block, *before)


def filter_kernel(*refs):
    parts, (weight_ref, table_ref, out_ref) = refs[:-3], refs[-3:]
    summed = parts[0][...]
    for part in parts[1:]:
        summed = summed + part[...]
    projected = jnp.dot(summed, weight_ref[...], precision=HIGH, preferred_element_type=f32)
    out_ref[...] = projected * table_ref[...]


def filtered_piece(parts, w_charge, table):
    return pl.pallas_call(
        filter_kernel,
        in_specs=[whole()] * (len(parts) + 2),
        out_specs=whole(),
        out_shape=jax.ShapeDtypeStruct(table.shape, f32),
        compiler_params=params(),
        name="filter",
    )(*parts, w_charge, table)


def potential_kernel(groups, pieces, blocks, index_ref, *refs):
    held = refs[:groups]
    waves = refs[groups : groups + blocks]
    outs = refs[groups + blocks : -2]
    ordered_ref, turned_ref = refs[-2:]
    channels = ordered_ref.shape[-1]
    piece = held[0].shape[0] // pieces
    for group in range(groups):
        for n in range(pieces):
            at = pl.multiple_of(index_ref[group * pieces + n] * piece, piece)
            ordered_ref[pl.ds(at, piece), :] = held[group][n * piece : (n + 1) * piece, :]
    high, low = split(ordered_ref[...].T)
    turned_ref[:channels, :] = high
    turned_ref[channels:, :] = low
    for wave_ref, out in zip(waves, outs):
        cells, _, slots = out.shape
        span = cells * slots
        both = jnp.dot(turned_ref[...], wave_ref[:, :span], preferred_element_type=f32)
        third = jnp.dot(turned_ref[:channels, :], wave_ref[:, span:], preferred_element_type=f32)
        potential = both[:channels] + both[channels:] + third
        for cell in range(cells):
            out[cell] = potential[:, cell * slots : (cell + 1) * slots]


def potentials_of(index, held, pieces, waves, cells, slots):
    rows = waves[0].shape[0]
    channels = held[0].shape[-1]
    return pl.pallas_call(
        functools.partial(potential_kernel, len(held), pieces, len(waves)),
        in_specs=[pl.BlockSpec(memory_space=pltpu.SMEM)] + [whole()] * (len(held) + len(waves)),
        out_specs=[whole()] * len(waves),
        scratch_shapes=[
            pltpu.VMEM((rows, channels), f32),
            pltpu.VMEM((2 * channels, rows), bf16),
        ],
        out_shape=[jax.ShapeDtypeStruct((cells, channels, slots), f32)] * len(waves),
        compiler_params=params(),
        cost_estimate=pl.CostEstimate(
            flops=6 * rows * len(waves) * cells * slots * channels,
            bytes_accessed=4 * rows * len(waves) * cells * slots, transcendentals=0,
        ),
        name="potentials",
    )(index, *held, *waves)


def message_kernel(
    basis, own_plane, step_ref, own_ref, ext_ref, mix_ref, value_ref, out_ref,
    cell_ref, own_col_ref, acc_ref, mixed_ref, left_0, left_1, left_2, right_0, right_1, right_2,
):
    count = step_ref.shape[1]
    cells = own_ref.shape[0]
    across, along, planes, _, slots = ext_ref.shape
    channels = value_ref.shape[0]
    lefts, rights = (left_0, left_1, left_2), (right_0, right_1, right_2)

    def turn(n, carry):
        x = n // (along * planes)
        y = (n // planes) % along
        z = n % planes
        high, low = split(ext_ref[x, y, z, :channels, :])
        cell_ref[n, :channels, :] = high
        cell_ref[n, channels:, :] = low
        return carry

    lax.fori_loop(0, across * along * planes, turn, 0, unroll=4)
    for b in range(basis):
        high, low = split(value_ref[...] * mix_ref[b : b + 1, :])
        mixed_ref[b * channels : (b + 1) * channels, :channels] = high
        mixed_ref[b * channels : (b + 1) * channels, channels:] = low
    for cell in range(cells):
        columns = own_ref[cell, channels : channels + 8, :].T
        for axis in range(3):
            own_col_ref[cell, axis] = jnp.broadcast_to(columns[:, axis : axis + 1], (slots, slots))

    def fill(step, move):
        place_x = step_ref[0, step] + 1 + (move - 1)
        place_y = step_ref[1, step]
        plane = step_ref[2, step]
        shift_z = step_ref[3, step].astype(f32)
        left, right = lefts[move], rights[move]
        own = step_ref[4, step]
        near = []
        for n in range(3):
            cell = cell_ref[(place_x * along + place_y + n) * planes + plane]
            right[:, n * slots : (n + 1) * slots] = cell
            right[:, (3 + n) * slots : (4 + n) * slots] = cell
            at = ext_ref[place_x, place_y + n, plane, channels : channels + 3, :]
            near.append((at[0:1] + float(move - 1), at[1:2] + float(n - 1), at[2:3] + shift_z))
        tile = 16
        for m in range(slots // tile):
            at = m * tile
            own_x = own_col_ref[own, 0, at : at + tile, :]
            own_y = own_col_ref[own, 1, at : at + tile, :]
            own_z = own_col_ref[own, 2, at : at + tile, :]
            for n in range(3):
                dx = near[n][0] - own_x
                dy = near[n][1] - own_y
                dz = near[n][2] - own_z
                squared = dx * dx + dy * dy + dz * dz
                distance = squared * lax.rsqrt(jnp.maximum(squared, 1e-30))
                envelope = jnp.maximum(1.0 - squared, 0.0)
                term = envelope * envelope * jnp.exp2(squared * (-float((basis - 1) ** 2) * LOG2E))
                ratio = jnp.exp2(distance * (2.0 * (basis - 1) * LOG2E))
                if own_plane and move == 1 and n == 1:
                    i = lax.broadcasted_iota(jnp.int32, (tile, slots), 0) + at
                    j = lax.broadcasted_iota(jnp.int32, (tile, slots), 1)
                    same = jnp.logical_and(i == j, step_ref[3, step] == 0)
                    term = jnp.where(same, 0.0, term)
                for b in range(basis):
                    if b > 0:
                        term = term * ratio
                    high, low = split(term)
                    row = b * slots + at
                    left[row : row + tile, n * slots : (n + 1) * slots] = high
                    left[row : row + tile, (3 + n) * slots : (4 + n) * slots] = low

    def product(move):
        return lax.dot_general(
            lefts[move][...], rights[move][...], (((1,), (1,)), ((), ())), preferred_element_type=f32
        )

    def finish(own):
        gathered = acc_ref[:, :channels] + acc_ref[:, channels:]
        wide = jnp.concatenate([gathered[b * slots : (b + 1) * slots] for b in range(basis)], axis=1)
        high, low = split(wide)
        both = jnp.dot(high, mixed_ref[...], preferred_element_type=f32)
        both = both + jnp.dot(low, mixed_ref[...], preferred_element_type=f32)
        out_ref[own] = (both[:, :channels] + both[:, channels:]).T

    fill(0, 0)

    def visit(step, carry):
        fresh = step_ref[5, step] == 1
        acc_ref[...] = jnp.where(fresh, 0.0, acc_ref[...]) + product(0)
        fill(step, 1)
        acc_ref[...] += product(1)
        fill(step, 2)
        acc_ref[...] += product(2)
        fill(jnp.minimum(step + 1, count - 1), 0)

        @pl.when(step_ref[6, step] == 1)
        def _():
            finish(step_ref[4, step])

        return carry

    lax.fori_loop(0, count, visit, 0)


def pair_messages(steps, own_plane, own, ext, mix, w_value):
    cells, _, slots = own.shape
    basis, channels = mix.shape
    across, along, planes = ext.shape[:3]
    count = steps.shape[1]
    return pl.pallas_call(
        functools.partial(message_kernel, basis, own_plane),
        in_specs=[pl.BlockSpec(memory_space=pltpu.SMEM)] + [whole()] * 4,
        out_specs=whole(),
        scratch_shapes=[
            pltpu.VMEM((across * along * planes, 2 * channels, slots), bf16),
            pltpu.VMEM((cells, 3, slots, slots), f32),
            pltpu.VMEM((basis * slots, 2 * channels), f32),
            pltpu.VMEM((basis * channels, 2 * channels), bf16),
        ]
        + [pltpu.VMEM((basis * slots, 6 * slots), bf16)] * 3
        + [pltpu.VMEM((2 * channels, 6 * slots), bf16)] * 3,
        out_shape=jax.ShapeDtypeStruct((cells, channels, slots), f32),
        compiler_params=params(),
        cost_estimate=pl.CostEstimate(
            flops=count * 8 * basis * slots * 9 * slots * channels, bytes_accessed=1 << 20,
            transcendentals=0,
        ),
        name="messages",
    )(steps, own, ext, mix, w_value)
def visits(cells_x, cells_y, cells_z, inside):
    table = []
    for x in range(cells_x):
        for y in range(cells_y):
            for z in range(cells_z):
                own = (x * cells_y + y) * cells_z + z
                for shift in (-1, 0, 1):
                    plane = z + shift
                    if (0 <= plane < cells_z) != inside:
                        continue
                    if not inside:
                        plane = 0 if shift > 0 else 1
                    table.append([x, y, plane, shift, own, 1, 1])
    for one, after in zip(table, table[1:]):
        if one[4] == after[4]:
            one[6] = after[5] = 0
    return np.array(table, np.int32).T.copy()


def mlp_kernel(count, *refs):
    counts_ref, feature_ref = refs[:2]
    messages = refs[2:4]
    potentials = refs[4 : 4 + count]
    hidden_ref, back_ref, out_ref = refs[4 + count :]
    cells, channels, slots = feature_ref.shape
    columns = []
    for cell in range(cells):
        mixed = feature_ref[cell] + message_scale * (messages[0][cell] + messages[1][cell])
        for potential in potentials:
            mixed = mixed + potential[cell]
        columns.append(mixed)
    mixed = jnp.concatenate(columns, axis=1)
    inner = jnp.dot(hidden_ref[...].T, mixed, precision=HIGH, preferred_element_type=f32)
    hidden = inner * jax.nn.sigmoid(inner)
    updated = mixed + jnp.dot(back_ref[...].T, hidden, precision=HIGH, preferred_element_type=f32)
    slot = lax.broadcasted_iota(jnp.int32, (channels, slots), 1)
    for cell in range(cells):
        part = updated[:, cell * slots : (cell + 1) * slots]
        out_ref[cell] = jnp.where(slot < counts_ref[cell], part, 0.0)


def atom_mlp(counts, features, messages, potentials, w_hidden, w_out):
    return pl.pallas_call(
        functools.partial(mlp_kernel, len(potentials)),
        in_specs=[pl.BlockSpec(memory_space=pltpu.SMEM)]
        + [whole()] * (5 + len(potentials)),
        out_specs=whole(),
        out_shape=jax.ShapeDtypeStruct(features.shape, f32),
        compiler_params=params(),
        name="atom_mlp",
    )(counts, features, *messages, *potentials, w_hidden, w_out)


def with_x(block):
    below, above = below_above(block[:1], block[-1:], "gx")
    return jnp.concatenate([below, block, above], axis=0)


def shards(
    features, positions, counts, waves, filter_table, w_value, w_charge, radial_mix, w_hidden, w_out
):
    cells_x, cells_y, cells_z, channels, slots = features.shape
    basis = radial_mix.shape[0]
    total_waves = waves.shape[1]
    size_x, size_y, size_z = (lax.axis_size(a) for a in ("gx", "gy", "gz"))
    at_x, at_y, at_z = (lax.axis_index(a) for a in ("gx", "gy", "gz"))
    grid = (cells_x * size_x, cells_y * size_y, cells_z * size_z)
    cells = cells_x * cells_y * cells_z
    flat_counts = counts.reshape(cells)
    flat_features = features.reshape(cells, channels, slots)

    offsets = np.array(
        [(x, y, z) for x in range(cells_x) for y in range(cells_y) for z in range(cells_z)], np.int32
    )
    base = jnp.stack([at_x * cells_x, at_y * cells_y, at_z * cells_z]).astype(jnp.int32)
    own = pack(
        grid, (base + offsets).reshape(-1), flat_counts, flat_features,
        positions.reshape(cells, 3, slots),
    )
    rows = own.shape[1]
    packed = own.reshape(cells_x, cells_y, cells_z, rows, slots)

    gathered = [own] + [exchange(own, "gy", s) for s in range(1, size_y)]
    sides = neighbours(packed[:, :, :1], packed[:, :, -1:], "gz", same=cells_z == 1)

    share = total_waves // size_y
    own_waves = lax.dynamic_slice_in_dim(waves, at_y * share, share, 1).astype(f32).T
    parts, tables = (), []
    for block in gathered:
        *parts, table = partial_factors(at_x.reshape(1), own_waves, block, parts, size_x)
        tables.append(table)

    half = 2 * share // size_x
    summed = parts[0]
    for s in range(1, size_x):
        other = partner(at_x, s, size_x)
        to = parts[1]
        for n in range(2, size_x):
            to = jnp.where(lax.rem(other - at_x + size_x, size_x) == n, parts[n], to)
        summed = summed + exchange(to, "gx", s)
    piece = half // size_z
    pieces = [lax.dynamic_slice_in_dim(summed, at_z * piece, piece, 0)]
    for s in range(1, size_z):
        other = partner(at_z, s, size_z)
        pieces.append(exchange(lax.dynamic_slice_in_dim(summed, other * piece, piece, 0), "gz", s))
    scale = 1.0 / math.sqrt(grid[0] * grid[1] * grid[2] * slots) / math.sqrt(total_waves)
    chunk = math.gcd(share // size_x, 128)
    table = lax.dynamic_slice_in_dim(filter_table, at_y * share, share, 0) * scale
    table = jnp.broadcast_to(
        table.reshape(share // chunk, 1, chunk, channels), (share // chunk, 2, chunk, channels)
    ).reshape(2 * share, channels)
    table = lax.dynamic_slice_in_dim(table, at_x * half + at_z * piece, piece, 0)
    filtered = filtered_piece(pieces, w_charge, table)

    held_z = jnp.concatenate(
        [filtered] + [exchange(filtered, "gz", s) for s in range(1, size_z)], axis=0
    )
    held = [held_z] + [exchange(held_z, "gx", s) for s in range(1, size_x)]
    ranks_x = [at_x] + [partner(at_x, s, size_x) for s in range(1, size_x)]
    ranks_z = [at_z] + [partner(at_z, s, size_z) for s in range(1, size_z)]
    index = jnp.stack([x * size_z + z for x in ranks_x for z in ranks_z]).astype(jnp.int32)

    def of_y(rank, edge):
        found = None
        for s in range(size_y):
            source = at_y if s == 0 else partner(at_y, s, size_y)
            possible = any(
                (i if s == 0 else partner(i, s, size_y)) == (i + rank) % size_y for i in range(size_y)
            )
            if not possible:
                continue
            block = gathered[s].reshape(packed.shape)[:, edge]
            wanted = source == lax.rem(at_y + rank + size_y, size_y)
            found = block if found is None else jnp.where(wanted, block, found)
        return found

    plane = with_x(jnp.concatenate([of_y(-1, slice(-1, None)), packed, of_y(1, slice(0, 1))], axis=1))
    low, high = (
        jnp.concatenate([side[:, edge] for side in sides], axis=2)
        for edge in (slice(0, 1), slice(-1, None))
    )
    low, high, filtered = lax.optimization_barrier((low, high, filtered))
    below, above = below_above(low, high, "gy")
    around = with_x(jnp.concatenate([below, jnp.concatenate(sides, axis=2), above], axis=1))

    mix = radial_mix * np.exp(-np.arange(basis, dtype=np.float64) ** 2).astype(np.float32)[:, None]
    inner = jnp.asarray(visits(cells_x, cells_y, cells_z, True))
    outer = jnp.asarray(visits(cells_x, cells_y, cells_z, False))
    outer = outer.at[2].set(jnp.where(is_even("gz"), outer[2], 1 - outer[2]))
    near = pair_messages(inner, True, own, plane, mix, w_value)
    far = pair_messages(outer, False, own, around, mix, w_value)

    found = potentials_of(index, held, held_z.shape[0] // piece, tables, cells, slots)
    returned = [found[0]] + [exchange(found[s], "gy", s) for s in range(1, size_y)]

    updated = atom_mlp(flat_counts, flat_features, [near, far], returned, w_hidden, w_out)
    return updated.reshape(features.shape)


def solution(mesh):
    placed = (
        P("gx", "gy", "gz", None, None),
        P("gx", "gy", "gz", None, None),
        P("gx", "gy", "gz"),
        P(),
        P(),
        P(),
        P(),
        P(),
        P(),
        P(),
    )
    return jax.shard_map(
        shards,
        mesh=mesh,
        in_specs=placed,
        out_specs=P("gx", "gy", "gz", None, None),
        check_vma=False,
    )
```

```python
import functools
import math

import numpy as np

import jax
import jax.numpy as jnp
from jax import lax
from jax.experimental import pallas as pl
from jax.experimental.pallas import tpu as pltpu
from jax.sharding import PartitionSpec as P


HIGH = lax.Precision.HIGH
message_scale = 0.125
bf16 = jnp.bfloat16
f32 = jnp.float32
VMEM_LIMIT = 28 * 1024 * 1024


LOG2E = math.log2(math.e)


def partner(i, step, count):
    return i ^ step


def exchange(block, axis, step):
    count = lax.axis_size(axis)
    pairs = [(i, partner(i, step, count)) for i in range(count)]
    return lax.ppermute(block, axis, pairs)


def is_even(axis):
    if lax.axis_size(axis) % 2:
        return jnp.bool_(True)
    return lax.rem(lax.axis_index(axis), 2) == 0


def neighbours(low, high, axis, same=False):
    count = lax.axis_size(axis)
    if count == 1:
        return low, high
    if count % 2:
        up = lax.ppermute(low, axis, [(i, (i - 1) % count) for i in range(count)])
        down = lax.ppermute(high, axis, [(i, (i + 1) % count) for i in range(count)])
        return up, down
    even = is_even(axis)
    first = high if same else jnp.where(even, high, low)
    second = low if same else jnp.where(even, low, high)
    one = [(i, i ^ 1) for i in range(count)]
    two = [(i, (i + 1 if i % 2 else i - 1) % count) for i in range(count)]
    return lax.ppermute(first, axis, one), lax.ppermute(second, axis, two)


def below_above(low, high, axis):
    first, second = neighbours(low, high, axis)
    even = is_even(axis)
    return jnp.where(even, second, first), jnp.where(even, first, second)


def split(x):
    high = x.astype(bf16)
    low = (x - high.astype(f32)).astype(bf16)
    return high, low


def whole():
    return pl.BlockSpec(memory_space=pltpu.VMEM)


def params():
    return pltpu.CompilerParams(vmem_limit_bytes=VMEM_LIMIT)


def place_of(cell, shape):
    return cell // (shape[1] * shape[2]), cell // shape[2] % shape[1], cell % shape[2]


def pack_kernel(shape, grid, counts_ref, feature_ref, position_ref, out_ref):
    cells, channels, slots = feature_ref.shape
    slot = lax.broadcasted_iota(jnp.int32, (channels, slots), 1)
    blank = jnp.zeros((2, slots), f32)
    base = [lax.axis_index(axis) * here for axis, here in zip(("gx", "gy", "gz"), shape)]
    for cell in range(cells):
        x, y, z = place_of(cell, shape)
        held = slot < counts_ref[x, z, y]
        out_ref[cell, :channels, :] = jnp.where(held, feature_ref[cell], 0.0)
        at = [position_ref[3 * cell + axis] for axis in range(3)]
        rows = list(at)
        for axis, offset in enumerate((x, y, z)):
            rows.append((at[axis] + (base[axis] + offset).astype(f32)) * (1.0 / grid[axis]))
        out_ref[cell, channels:, :] = jnp.concatenate(rows + [blank], axis=0)


def pack(shape, grid, counts, features, positions):
    cells, channels, slots = features.shape
    return pl.pallas_call(
        functools.partial(pack_kernel, shape, grid),
        in_specs=[pl.BlockSpec(memory_space=pltpu.SMEM), whole(), whole()],
        out_specs=whole(),
        out_shape=jax.ShapeDtypeStruct((cells, channels + 8, slots), f32),
        compiler_params=params(),
        name="pack",
    )(counts, features, positions)


def fitted(function, terms):
    t = 0.125 * (1.0 + np.cos(np.pi * (np.arange(terms) + 0.5) / terms))
    solved = np.linalg.solve(np.vander(t, terms, increasing=True), function(np.sqrt(t)))
    return [float(c) for c in solved]


SIN = fitted(lambda u: 2.0 * np.sin(np.pi * u) / u, 5)
COS = fitted(lambda u: np.cos(np.pi * u), 5)


def poly(coefficients, t):
    acc = t * coefficients[-1] + coefficients[-2]
    for c in coefficients[-3::-1]:
        acc = acc * t + c
    return acc


def turns(u):
    u = u - jnp.round(u)
    t = u * u
    twice_sine = poly(SIN, t) * u
    cosine = poly(COS, t)
    return 1.0 - 0.5 * twice_sine * twice_sine, twice_sine * cosine


def factor_kernel(parts, chunk, first, waves_ref, block_ref, *refs):
    before = refs[: 0 if first else parts]
    refs = refs[len(before) :]
    after, wave_ref, weight_ref, column_ref = refs[:parts], refs[parts], refs[parts + 1], refs[parts + 2]
    cells, _, slots = block_ref.shape
    channels = after[0].shape[-1]
    span = cells * slots
    total = wave_ref.shape[0] // 2
    at_x = lax.axis_index("gx")
    begin = pl.multiple_of(lax.axis_index("gy") * total, total)
    rows = waves_ref[:, pl.ds(begin, total)].astype(f32)
    column_ref[...] = jnp.concatenate([rows, jnp.zeros((5, total), f32)], axis=0).T
    for cell in range(cells):
        high, low = split(block_ref[cell, :channels, :])
        for at in (cell * slots, span + cell * slots):
            weight_ref[:channels, at : at + slots] = high
            weight_ref[channels:, at : at + slots] = low

    def some(j, carry):
        here = pl.multiple_of(j * chunk, chunk)
        wave_x = column_ref[pl.ds(here, chunk), 0:1]
        wave_y = column_ref[pl.ds(here, chunk), 1:2]
        wave_z = column_ref[pl.ds(here, chunk), 2:3]
        row = pl.multiple_of(j * 2 * chunk, 2 * chunk)
        for cell in range(cells):
            at = cell * slots
            frac = block_ref[cell, channels + 3 : channels + 6, :]
            u = wave_x * frac[0:1] + wave_y * frac[1:2] + wave_z * frac[2:3]
            cosine, sine = turns(u)
            high, low = split(cosine)
            wave_ref[pl.ds(row, chunk), at : at + slots] = high
            wave_ref[pl.ds(row, chunk), span + at : span + at + slots] = low
            high, low = split(sine)
            wave_ref[pl.ds(row + chunk, chunk), at : at + slots] = high
            wave_ref[pl.ds(row + chunk, chunk), span + at : span + at + slots] = low
        both = lax.dot_general(
            wave_ref[pl.ds(row, 2 * chunk), :], weight_ref[...], (((1,), (1,)), ((), ())),
            preferred_element_type=f32,
        )
        both = both[:, :channels] + both[:, channels:]
        per_part = total // chunk // parts
        part = lax.rem(j // per_part - at_x + parts, parts)
        row = pl.multiple_of(lax.rem(j, per_part) * 2 * chunk, 2 * chunk)
        for n in range(parts):

            @pl.when(part == n)
            def _(n=n):
                if first:
                    after[n][pl.ds(row, 2 * chunk), :] = both
                else:
                    after[n][pl.ds(row, 2 * chunk), :] = before[n][pl.ds(row, 2 * chunk), :] + both

        return carry

    lax.fori_loop(0, total // chunk, some, 0)


def partial_factors(waves, total, chunk, block, before, parts):
    cells, rows, slots = block.shape
    channels = rows - 8
    span = cells * slots
    out = [jax.ShapeDtypeStruct((2 * total // parts, channels), f32)] * parts
    return pl.pallas_call(
        functools.partial(factor_kernel, parts, chunk, not before),
        in_specs=[whole()] * (2 + len(before)),
        out_specs=[whole()] * (parts + 1),
        out_shape=out + [jax.ShapeDtypeStruct((2 * total, 2 * span), bf16)],
        input_output_aliases={2 + n: n for n in range(len(before))},
        scratch_shapes=[pltpu.VMEM((2 * channels, 2 * span), bf16), pltpu.VMEM((total, 8), f32)],
        compiler_params=params(),
        cost_estimate=pl.CostEstimate(
            flops=8 * total * span * channels, bytes_accessed=8 * total * span, transcendentals=0
        ),
        name="factors",
    )(waves, block, *before)


def filter_kernel(scale, block_ref, *refs):
    parts, (weight_ref, table_ref, out_ref) = refs[:-3], refs[-3:]
    summed = parts[0][...]
    for part in parts[1:]:
        summed = summed + part[...]
    projected = jnp.dot(summed, weight_ref[...], precision=HIGH, preferred_element_type=f32)
    table = table_ref[...] * scale
    for n in range(0, summed.shape[0], table.shape[0]):
        out_ref[n : n + table.shape[0], :] = projected[n : n + table.shape[0]] * table


def filtered_piece(scale, block, chunk, parts, w_charge, table):
    rows, channels = parts[0].shape
    fixed = pl.BlockSpec((rows, channels), lambda i, block: (0, 0))
    return pl.pallas_call(
        functools.partial(filter_kernel, scale),
        grid_spec=pltpu.PrefetchScalarGridSpec(
            num_scalar_prefetch=1,
            grid=(1,),
            in_specs=[fixed] * len(parts)
            + [
                pl.BlockSpec(w_charge.shape, lambda i, block: (0, 0)),
                pl.BlockSpec((chunk, channels), lambda i, block: (block[0], 0)),
            ],
            out_specs=fixed,
        ),
        out_shape=jax.ShapeDtypeStruct((rows, channels), f32),
        compiler_params=params(),
        name="filter",
    )(block, *parts, w_charge, table)


def potential_kernel(groups, pieces, blocks, *refs):
    held = refs[:groups]
    waves = refs[groups : groups + blocks]
    outs = refs[groups + blocks : -2]
    ordered_ref, turned_ref = refs[-2:]
    channels = ordered_ref.shape[-1]
    piece = held[0].shape[0] // pieces
    for group in range(groups):
        for n in range(pieces):
            rank_x = partner(lax.axis_index("gx"), group, groups)
            rank_z = partner(lax.axis_index("gz"), n, pieces)
            at = pl.multiple_of((rank_x * pieces + rank_z) * piece, piece)
            ordered_ref[pl.ds(at, piece), :] = held[group][n * piece : (n + 1) * piece, :]
    high, low = split(ordered_ref[...].T)
    turned_ref[:channels, :] = high
    turned_ref[channels:, :] = low
    for wave_ref, out in zip(waves, outs):
        cells, _, slots = out.shape
        span = cells * slots
        both = jnp.dot(turned_ref[...], wave_ref[:, :span], preferred_element_type=f32)
        third = jnp.dot(turned_ref[:channels, :], wave_ref[:, span:], preferred_element_type=f32)
        potential = both[:channels] + both[channels:] + third
        for cell in range(cells):
            out[cell] = potential[:, cell * slots : (cell + 1) * slots]


def potentials_of(held, pieces, waves, cells, slots):
    rows = waves[0].shape[0]
    channels = held[0].shape[-1]
    return pl.pallas_call(
        functools.partial(potential_kernel, len(held), pieces, len(waves)),
        in_specs=[whole()] * (len(held) + len(waves)),
        out_specs=[whole()] * len(waves),
        scratch_shapes=[
            pltpu.VMEM((rows, channels), f32),
            pltpu.VMEM((2 * channels, rows), bf16),
        ],
        out_shape=[jax.ShapeDtypeStruct((cells, channels, slots), f32)] * len(waves),
        compiler_params=params(),
        cost_estimate=pl.CostEstimate(
            flops=6 * rows * len(waves) * cells * slots * channels,
            bytes_accessed=4 * rows * len(waves) * cells * slots, transcendentals=0,
        ),
        name="potentials",
    )(*held, *waves)


def message_kernel(
    basis, sources, table, own_plane, step_ref, own_ref, mix_ref, value_ref, *refs
):
    blocks, out_ref = refs[:sources], refs[sources]
    cell_ref, at_ref, own_col_ref, acc_ref, mixed_ref = refs[sources + 1 : sources + 6]
    left_0, left_1, left_2, right_0, right_1, right_2 = refs[sources + 6 :]
    count = step_ref.shape[1]
    cells = own_ref.shape[0]
    slots = own_ref.shape[-1]
    along, planes = len(table[0]), len(table[0][0])
    channels = value_ref.shape[0]
    lefts, rights = (left_0, left_1, left_2), (right_0, right_1, right_2)

    for x, columns in enumerate(table):
        for y, column in enumerate(columns):
            for z, choices in enumerate(column):
                n = (x * along + y) * planes + z
                (_, source, index), others = choices[0], choices[1:]
                block = blocks[source][index]
                for condition, source, index in others:
                    block = jnp.where(condition(), blocks[source][index], block)
                high, low = split(block[:channels])
                cell_ref[n, :channels, :] = high
                cell_ref[n, channels:, :] = low
                at_ref[n] = block[channels:]
    for b in range(basis):
        high, low = split(value_ref[...] * (mix_ref[b : b + 1, :] * math.exp(-b * b)))
        mixed_ref[b * channels : (b + 1) * channels, :channels] = high
        mixed_ref[b * channels : (b + 1) * channels, channels:] = low
    for cell in range(cells):
        columns = own_ref[cell, channels : channels + 8, :].T
        for axis in range(3):
            own_col_ref[cell, axis] = jnp.broadcast_to(columns[:, axis : axis + 1], (slots, slots))

    def fill(step, move):
        place_x = step_ref[0, step] + 1 + (move - 1)
        place_y = step_ref[1, step]
        plane = step_ref[2, step]
        if not own_plane:
            plane = jnp.where(is_even("gz"), plane, 1 - plane)
        shift_z = step_ref[3, step].astype(f32)
        left, right = lefts[move], rights[move]
        own = step_ref[4, step]
        near = []
        for n in range(3):
            number = (place_x * along + place_y + n) * planes + plane
            cell = cell_ref[number]
            right[:, n * slots : (n + 1) * slots] = cell
            right[:, (3 + n) * slots : (4 + n) * slots] = cell
            at = at_ref[number]
            near.append((at[0:1] + float(move - 1), at[1:2] + float(n - 1), at[2:3] + shift_z))
        tile = 16
        for m in range(slots // tile):
            at = m * tile
            own_x = own_col_ref[own, 0, at : at + tile, :]
            own_y = own_col_ref[own, 1, at : at + tile, :]
            own_z = own_col_ref[own, 2, at : at + tile, :]
            for n in range(3):
                dx = near[n][0] - own_x
                dy = near[n][1] - own_y
                dz = near[n][2] - own_z
                squared = dx * dx + dy * dy + dz * dz
                distance = squared * lax.rsqrt(jnp.maximum(squared, 1e-30))
                envelope = jnp.maximum(1.0 - squared, 0.0)
                term = envelope * envelope * jnp.exp2(squared * (-float((basis - 1) ** 2) * LOG2E))
                ratio = jnp.exp2(distance * (2.0 * (basis - 1) * LOG2E))
                if own_plane and move == 1 and n == 1:
                    i = lax.broadcasted_iota(jnp.int32, (tile, slots), 0) + at
                    j = lax.broadcasted_iota(jnp.int32, (tile, slots), 1)
                    same = jnp.logical_and(i == j, step_ref[3, step] == 0)
                    term = jnp.where(same, 0.0, term)
                for b in range(basis):
                    if b > 0:
                        term = term * ratio
                    high, low = split(term)
                    row = b * slots + at
                    left[row : row + tile, n * slots : (n + 1) * slots] = high
                    left[row : row + tile, (3 + n) * slots : (4 + n) * slots] = low

    def product(move):
        return lax.dot_general(
            lefts[move][...], rights[move][...], (((1,), (1,)), ((), ())), preferred_element_type=f32
        )

    def finish(own):
        gathered = acc_ref[:, :channels] + acc_ref[:, channels:]
        wide = jnp.concatenate([gathered[b * slots : (b + 1) * slots] for b in range(basis)], axis=1)
        high, low = split(wide)
        both = jnp.dot(high, mixed_ref[...], preferred_element_type=f32)
        both = both + jnp.dot(low, mixed_ref[...], preferred_element_type=f32)
        out_ref[own] = (both[:, :channels] + both[:, channels:]).T

    fill(0, 0)

    def visit(step, carry):
        fresh = step_ref[5, step] == 1
        acc_ref[...] = jnp.where(fresh, 0.0, acc_ref[...]) + product(0)
        fill(step, 1)
        acc_ref[...] += product(1)
        fill(step, 2)
        acc_ref[...] += product(2)
        fill(jnp.minimum(step + 1, count - 1), 0)

        @pl.when(step_ref[6, step] == 1)
        def _():
            finish(step_ref[4, step])

        return carry

    lax.fori_loop(0, count, visit, 0)


def pair_messages(steps, own_plane, own, blocks, table, mix, w_value):
    cells, _, slots = own.shape
    basis, channels = mix.shape
    around = len(table) * len(table[0]) * len(table[0][0])
    count = steps.shape[1]
    return pl.pallas_call(
        functools.partial(message_kernel, basis, len(blocks), table, own_plane),
        in_specs=[pl.BlockSpec(memory_space=pltpu.SMEM)] + [whole()] * (3 + len(blocks)),
        out_specs=whole(),
        scratch_shapes=[
            pltpu.VMEM((around, 2 * channels, slots), bf16),
            pltpu.VMEM((around, 8, slots), f32),
            pltpu.VMEM((cells, 3, slots, slots), f32),
            pltpu.VMEM((basis * slots, 2 * channels), f32),
            pltpu.VMEM((basis * channels, 2 * channels), bf16),
        ]
        + [pltpu.VMEM((basis * slots, 6 * slots), bf16)] * 3
        + [pltpu.VMEM((2 * channels, 6 * slots), bf16)] * 3,
        out_shape=jax.ShapeDtypeStruct((cells, channels, slots), f32),
        compiler_params=params(),
        cost_estimate=pl.CostEstimate(
            flops=count * 8 * basis * slots * 9 * slots * channels, bytes_accessed=1 << 20,
            transcendentals=0,
        ),
        name="messages",
    )(steps, own, mix, w_value, *blocks)
def visits(cells_x, cells_y, cells_z, inside):
    table = []
    for x in range(cells_x):
        for y in range(cells_y):
            for z in range(cells_z):
                own = (x * cells_y + y) * cells_z + z
                for shift in (-1, 0, 1):
                    plane = z + shift
                    if (0 <= plane < cells_z) != inside:
                        continue
                    if not inside:
                        plane = 0 if shift > 0 else 1
                    table.append([x, y, plane, shift, own, 1, 1])
    for one, after in zip(table, table[1:]):
        if one[4] == after[4]:
            one[6] = after[5] = 0
    return np.array(table, np.int32).T.copy()


def mlp_kernel(count, shape, *refs):
    counts_ref, feature_ref = refs[:2]
    messages = refs[2:4]
    potentials = refs[4 : 4 + count]
    hidden_ref, back_ref, out_ref = refs[4 + count :]
    cells, channels, slots = feature_ref.shape
    columns = []
    for cell in range(cells):
        mixed = feature_ref[cell] + message_scale * (messages[0][cell] + messages[1][cell])
        for potential in potentials:
            mixed = mixed + potential[cell]
        columns.append(mixed)
    mixed = jnp.concatenate(columns, axis=1)
    inner = jnp.dot(hidden_ref[...].T, mixed, precision=HIGH, preferred_element_type=f32)
    hidden = inner * jax.nn.sigmoid(inner)
    updated = mixed + jnp.dot(back_ref[...].T, hidden, precision=HIGH, preferred_element_type=f32)
    slot = lax.broadcasted_iota(jnp.int32, (channels, slots), 1)
    for cell in range(cells):
        part = updated[:, cell * slots : (cell + 1) * slots]
        x, y, z = place_of(cell, shape)
        out_ref[cell] = jnp.where(slot < counts_ref[x, z, y], part, 0.0)


def atom_mlp(shape, counts, features, messages, potentials, w_hidden, w_out):
    return pl.pallas_call(
        functools.partial(mlp_kernel, len(potentials), shape),
        in_specs=[pl.BlockSpec(memory_space=pltpu.SMEM)]
        + [whole()] * (5 + len(potentials)),
        out_specs=whole(),
        out_shape=jax.ShapeDtypeStruct(features.shape, f32),
        compiler_params=params(),
        name="atom_mlp",
    )(counts, features, *messages, *potentials, w_hidden, w_out)


def next_in_x(block, shape):
    size = lax.axis_size("gx")
    if size == 2:
        other = exchange(block, "gx", 1)
        return (other, shape[0] - 1), (other, 0)
    wide = block.reshape(shape + block.shape[1:])
    below, above = below_above(wide[:1], wide[-1:], "gx")
    return tuple((side.reshape((-1,) + block.shape[1:]), 0) for side in (below, above))


class Sources:
    def __init__(self):
        self.arrays = []

    def add(self, array):
        for n, held in enumerate(self.arrays):
            if held is array:
                return n
        self.arrays.append(array)
        return len(self.arrays) - 1

    def columns(self, block, shape):
        below, above = next_in_x(block, shape)
        inside = [(self.add(block), x) for x in range(shape[0])]
        return [(self.add(below[0]), below[1])] + inside + [(self.add(above[0]), above[1])]


def always():
    return True


def shards(
    features, positions, counts, waves, filter_table, w_value, w_charge, radial_mix, w_hidden, w_out
):
    shape = cells_x, cells_y, cells_z = features.shape[:3]
    channels, slots = features.shape[3:]
    total_waves = waves.shape[1]
    size_x, size_y, size_z = (lax.axis_size(a) for a in ("gx", "gy", "gz"))
    at_x, at_y, at_z = (lax.axis_index(a) for a in ("gx", "gy", "gz"))
    grid = (cells_x * size_x, cells_y * size_y, cells_z * size_z)
    cells = cells_x * cells_y * cells_z
    some_counts = jnp.transpose(counts, (0, 2, 1))
    flat_features = features.reshape(cells, channels, slots)

    own = pack(shape, grid, some_counts, flat_features, positions.reshape(cells * 3, 1, slots))
    rows = own.shape[1]
    packed = own.reshape(shape + (rows, slots))

    gathered = [own] + [exchange(own, "gy", s) for s in range(1, size_y)]
    if cells_z == 1:
        sides = neighbours(own, own, "gz", same=True)
    else:
        flat = (cells_x * cells_y, rows, slots)
        sides = neighbours(packed[:, :, 0].reshape(flat), packed[:, :, -1].reshape(flat), "gz")

    share = total_waves // size_y
    half = 2 * share // size_x
    piece = half // size_z
    chunk = min(piece, share // size_x)
    parts, tables = (), []
    for block in gathered:
        *parts, table = partial_factors(waves, share, chunk, block, parts, size_x)
        tables.append(table)

    summed = parts[0]
    for s in range(1, size_x):
        other = partner(at_x, s, size_x)
        to = parts[1]
        for n in range(2, size_x):
            to = jnp.where(lax.rem(other - at_x + size_x, size_x) == n, parts[n], to)
        summed = summed + exchange(to, "gx", s)
    value_near, summed = lax.optimization_barrier((w_value, summed))
    pieces = [lax.dynamic_slice_in_dim(summed, at_z * piece, piece, 0)]
    for s in range(1, size_z):
        other = partner(at_z, s, size_z)
        pieces.append(exchange(lax.dynamic_slice_in_dim(summed, other * piece, piece, 0), "gz", s))

    sources = Sources()

    def reaches(step, rank):
        return any(partner(i, step, size_y) == (i + rank) % size_y for i in range(size_y))

    columns = {
        step: sources.columns(block, shape)
        for step, block in enumerate(gathered)
        if any(reaches(step, rank) for rank in (-1, 0, 1))
    }

    def at_rank(step, rank):
        def condition():
            at = lax.axis_index("gy")
            return partner(at, step, size_y) == (at + rank) % size_y

        return condition

    def choices(x, y, z):
        rank = -1 if y < 0 else 1 if y == cells_y else 0
        y = y % cells_y
        found = []
        for step in columns:
            if reaches(step, rank):
                source, from_x = columns[step][x + 1]
                found.append((at_rank(step, rank), source, (from_x * cells_y + y) * cells_z + z))
        return found

    table = [
        [[choices(x, y, z) for z in range(cells_z)] for y in range(-1, cells_y + 1)]
        for x in range(-1, cells_x + 1)
    ]
    inner = jnp.asarray(visits(cells_x, cells_y, cells_z, True))
    near = pair_messages(inner, True, own, sources.arrays, table, radial_mix, value_near)

    scale = 1.0 / math.sqrt(grid[0] * grid[1] * grid[2] * slots) / math.sqrt(total_waves)
    rank = at_x * size_z + at_z
    block = at_y * (share // chunk) + (rank * piece) // (2 * chunk)
    charge, near = lax.optimization_barrier((w_charge, near))
    filtered = filtered_piece(scale, block.reshape(1), chunk, pieces, charge, filter_table)

    held_z = [filtered] + [exchange(filtered, "gz", s) for s in range(1, size_z)]
    started = held_z[min(1, size_z - 1)]
    held_z = jnp.concatenate(held_z, axis=0)
    held = [held_z] + [exchange(held_z, "gx", s) for s in range(1, size_x)]

    low, high = (
        jnp.concatenate(
            [side[n : n + 1] for n in range(y, cells_x * cells_y, cells_y) for side in sides], axis=0
        )
        for y in (0, cells_y - 1)
    )
    low, high, started = lax.optimization_barrier((low, high, started))
    edges = neighbours(low, high, "gy")
    sources = Sources()
    flat = (cells_x, cells_y, 1)
    side_columns = [sources.columns(side, flat) for side in sides]
    edge_columns = [sources.columns(edge, (cells_x, 1, 2)) for edge in edges]

    def choices(x, y, z):
        if 0 <= y < cells_y:
            source, from_x = side_columns[z][x + 1]
            return [(always, source, from_x * cells_y + y)]
        found = []
        for n, columns in enumerate(edge_columns):
            source, from_x = columns[x + 1]
            first_is_here = y == cells_y
            condition = (lambda: is_even("gy")) if (n == 0) == first_is_here else (
                lambda: jnp.logical_not(is_even("gy"))
            )
            found.append((condition, source, from_x * 2 + z))
        return found

    table = [
        [[choices(x, y, z) for z in range(2)] for y in range(-1, cells_y + 1)]
        for x in range(-1, cells_x + 1)
    ]
    found = potentials_of(held, held_z.shape[0] // piece, tables, cells, slots)
    value_far, *found = lax.optimization_barrier((w_value, *found))
    returned = [found[0]] + [exchange(found[s], "gy", s) for s in range(1, size_y)]
    outer = jnp.asarray(visits(cells_x, cells_y, cells_z, False))
    far = pair_messages(outer, False, own, sources.arrays, table, radial_mix, value_far)

    updated = atom_mlp(
        shape, some_counts, flat_features, [near, far], returned, w_hidden, w_out
    )
    return updated.reshape(features.shape)


def solution(mesh):
    placed = (
        P("gx", "gy", "gz", None, None),
        P("gx", "gy", "gz", None, None),
        P("gx", "gy", "gz"),
        P(),
        P(),
        P(),
        P(),
        P(),
        P(),
        P(),
    )
    return jax.shard_map(
        shards,
        mesh=mesh,
        in_specs=placed,
        out_specs=P("gx", "gy", "gz", None, None),
        check_vma=False,
    )
```

```python
import functools
import math

import numpy as np

import jax
import jax.numpy as jnp
from jax import lax
from jax.experimental import pallas as pl
from jax.experimental.pallas import tpu as pltpu
from jax.sharding import PartitionSpec as P


HIGH = lax.Precision.HIGH
message_scale = 0.125
bf16 = jnp.bfloat16
f32 = jnp.float32
VMEM_LIMIT = 28 * 1024 * 1024


LOG2E = math.log2(math.e)


def partner(i, step, count):
    return i ^ step


def exchange(block, axis, step):
    count = lax.axis_size(axis)
    pairs = [(i, partner(i, step, count)) for i in range(count)]
    return lax.ppermute(block, axis, pairs)


def is_even(axis):
    if lax.axis_size(axis) % 2:
        return jnp.bool_(True)
    return lax.rem(lax.axis_index(axis), 2) == 0


def neighbours(low, high, axis, same=False):
    count = lax.axis_size(axis)
    if count == 1:
        return low, high
    if count % 2:
        up = lax.ppermute(low, axis, [(i, (i - 1) % count) for i in range(count)])
        down = lax.ppermute(high, axis, [(i, (i + 1) % count) for i in range(count)])
        return up, down
    even = is_even(axis)
    first = high if same else jnp.where(even, high, low)
    second = low if same else jnp.where(even, low, high)
    one = [(i, i ^ 1) for i in range(count)]
    two = [(i, (i + 1 if i % 2 else i - 1) % count) for i in range(count)]
    return lax.ppermute(first, axis, one), lax.ppermute(second, axis, two)


def below_above(low, high, axis):
    first, second = neighbours(low, high, axis)
    even = is_even(axis)
    return jnp.where(even, second, first), jnp.where(even, first, second)


def split(x):
    high = x.astype(bf16)
    low = (x - high.astype(f32)).astype(bf16)
    return high, low


def whole():
    return pl.BlockSpec(memory_space=pltpu.VMEM)


def params():
    return pltpu.CompilerParams(vmem_limit_bytes=VMEM_LIMIT)


def place_of(cell, shape):
    return cell // (shape[1] * shape[2]), cell // shape[2] % shape[1], cell % shape[2]


def pack_kernel(shape, grid, counts_hbm, feature_hbm, position_hbm, out_ref, counts_ref, feature_ref, position_ref, sems):
    cells, channels, slots = feature_ref.shape
    copies = [
        pltpu.make_async_copy(counts_hbm, counts_ref, sems.at[0]),
        pltpu.make_async_copy(position_hbm, position_ref, sems.at[1]),
        pltpu.make_async_copy(feature_hbm, feature_ref, sems.at[2]),
    ]
    for copy in copies:
        copy.start()
    for copy in copies:
        copy.wait()
    slot = lax.broadcasted_iota(jnp.int32, (channels, slots), 1)
    for cell in range(cells):
        place = place_of(cell, shape)
        held = slot < counts_ref[place[0], place[2], place[1]]
        out_ref[cell, :channels, :] = jnp.where(held, feature_ref[cell], 0.0)
        at = [position_ref[3 * cell + axis] for axis in range(3)]
        rows = list(at)
        for axis, name in enumerate(("gx", "gy", "gz")):
            here = lax.axis_index(name) * shape[axis] + place[axis]
            rows.append((at[axis] + here.astype(f32)) * (1.0 / grid[axis]))
        out_ref[cell, channels:, :] = jnp.concatenate(rows + [jnp.zeros((2, slots), f32)], axis=0)


def pack(shape, grid, counts, features, positions):
    cells, channels, slots = features.shape
    return pl.pallas_call(
        functools.partial(pack_kernel, shape, grid),
        in_specs=[pl.BlockSpec(memory_space=pltpu.HBM)] * 3,
        out_specs=whole(),
        out_shape=jax.ShapeDtypeStruct((cells, channels + 8, slots), f32),
        scratch_shapes=[
            pltpu.SMEM(counts.shape, jnp.int32),
            pltpu.VMEM(features.shape, f32),
            pltpu.VMEM(positions.shape, f32),
            pltpu.SemaphoreType.DMA((3,)),
        ],
        compiler_params=params(),
        name="pack",
    )(counts, features, positions)


def fitted(function, terms):
    t = 0.125 * (1.0 + np.cos(np.pi * (np.arange(terms) + 0.5) / terms))
    solved = np.linalg.solve(np.vander(t, terms, increasing=True), function(np.sqrt(t)))
    return [float(c) for c in solved]


SIN = fitted(lambda u: math.sqrt(2.0) * np.sin(np.pi * u) / u, 5)
COS = fitted(lambda u: math.sqrt(2.0) * np.cos(np.pi * u), 5)


def poly(coefficients, t):
    acc = t * coefficients[-1] + coefficients[-2]
    for c in coefficients[-3::-1]:
        acc = acc * t + c
    return acc


def turns(u):
    u = u - jnp.round(u)
    t = u * u
    sine = poly(SIN, t) * u
    cosine = poly(COS, t)
    return 1.0 - sine * sine, sine * cosine


def factor_kernel(parts, chunk, first, waves_ref, block_ref, *refs):
    before = refs[: 0 if first else parts]
    refs = refs[len(before) :]
    after, wave_ref, weight_ref, column_ref = refs[:parts], refs[parts], refs[parts + 1], refs[parts + 2]
    cells, _, slots = block_ref.shape
    channels = after[0].shape[-1]
    span = cells * slots
    total = wave_ref.shape[0] // 2
    at_x = lax.axis_index("gx")
    begin = pl.multiple_of(lax.axis_index("gy") * total, total)
    rows = waves_ref[:, pl.ds(begin, total)].astype(f32)
    column_ref[...] = jnp.concatenate([rows, jnp.zeros((5, total), f32)], axis=0).T
    for cell in range(cells):
        high, low = split(block_ref[cell, :channels, :])
        for at in (cell * slots, span + cell * slots):
            weight_ref[:channels, at : at + slots] = high
            weight_ref[channels:, at : at + slots] = low

    def some(j, carry):
        here = pl.multiple_of(j * chunk, chunk)
        wave_x = column_ref[pl.ds(here, chunk), 0:1]
        wave_y = column_ref[pl.ds(here, chunk), 1:2]
        wave_z = column_ref[pl.ds(here, chunk), 2:3]
        row = pl.multiple_of(j * 2 * chunk, 2 * chunk)
        for cell in range(cells):
            at = cell * slots
            frac = block_ref[cell, channels + 3 : channels + 6, :]
            u = wave_x * frac[0:1] + wave_y * frac[1:2] + wave_z * frac[2:3]
            cosine, sine = turns(u)
            high, low = split(cosine)
            wave_ref[pl.ds(row, chunk), at : at + slots] = high
            wave_ref[pl.ds(row, chunk), span + at : span + at + slots] = low
            high, low = split(sine)
            wave_ref[pl.ds(row + chunk, chunk), at : at + slots] = high
            wave_ref[pl.ds(row + chunk, chunk), span + at : span + at + slots] = low
        return carry

    lax.fori_loop(0, total // chunk, some, 0)
    half = 2 * total // parts
    for n in range(parts):
        row = pl.multiple_of(lax.rem(at_x + n, parts) * half, half)
        both = lax.dot_general(
            wave_ref[pl.ds(row, half), :], weight_ref[...], (((1,), (1,)), ((), ())),
            preferred_element_type=f32,
        )
        both = both[:, :channels] + both[:, channels:]
        after[n][...] = both if first else before[n][...] + both


def partial_factors(waves, total, chunk, block, before, parts):
    cells, rows, slots = block.shape
    channels = rows - 8
    span = cells * slots
    out = [jax.ShapeDtypeStruct((2 * total // parts, channels), f32)] * parts
    return pl.pallas_call(
        functools.partial(factor_kernel, parts, chunk, not before),
        in_specs=[whole()] * (2 + len(before)),
        out_specs=[whole()] * (parts + 1),
        out_shape=out + [jax.ShapeDtypeStruct((2 * total, 2 * span), bf16)],
        input_output_aliases={2 + n: n for n in range(len(before))},
        scratch_shapes=[pltpu.VMEM((2 * channels, 2 * span), bf16), pltpu.VMEM((total, 8), f32)],
        compiler_params=params(),
        cost_estimate=pl.CostEstimate(
            flops=8 * total * span * channels, bytes_accessed=8 * total * span, transcendentals=0
        ),
        name="factors",
    )(waves, block, *before)


def filter_kernel(scale, block_ref, *refs):
    parts, (weight_ref, table_ref, out_ref) = refs[:-3], refs[-3:]
    summed = parts[0][...]
    for part in parts[1:]:
        summed = summed + part[...]
    projected = jnp.dot(summed, weight_ref[...], precision=HIGH, preferred_element_type=f32)
    table = table_ref[...] * scale
    for n in range(0, summed.shape[0], table.shape[0]):
        out_ref[n : n + table.shape[0], :] = projected[n : n + table.shape[0]] * table


def filtered_piece(scale, block, chunk, parts, w_charge, table):
    rows, channels = parts[0].shape
    fixed = pl.BlockSpec((rows, channels), lambda i, block: (0, 0))
    return pl.pallas_call(
        functools.partial(filter_kernel, scale),
        grid_spec=pltpu.PrefetchScalarGridSpec(
            num_scalar_prefetch=1,
            grid=(1,),
            in_specs=[fixed] * len(parts)
            + [
                pl.BlockSpec(w_charge.shape, lambda i, block: (0, 0)),
                pl.BlockSpec((chunk, channels), lambda i, block: (block[0], 0)),
            ],
            out_specs=fixed,
        ),
        out_shape=jax.ShapeDtypeStruct((rows, channels), f32),
        compiler_params=params(),
        name="filter",
    )(block, *parts, w_charge, table)


def potential_kernel(groups, pieces, blocks, *refs):
    held = refs[:groups]
    waves = refs[groups : groups + blocks]
    outs = refs[groups + blocks : -2]
    ordered_ref, turned_ref = refs[-2:]
    channels = ordered_ref.shape[-1]
    piece = held[0].shape[0] // pieces
    for group in range(groups):
        for n in range(pieces):
            rank_x = partner(lax.axis_index("gx"), group, groups)
            rank_z = partner(lax.axis_index("gz"), n, pieces)
            at = pl.multiple_of((rank_x * pieces + rank_z) * piece, piece)
            ordered_ref[pl.ds(at, piece), :] = held[group][n * piece : (n + 1) * piece, :]
    high, low = split(ordered_ref[...].T)
    turned_ref[:channels, :] = high
    turned_ref[channels:, :] = low
    for wave_ref, out in zip(waves, outs):
        cells, _, slots = out.shape
        span = cells * slots
        both = jnp.dot(turned_ref[...], wave_ref[:, :span], preferred_element_type=f32)
        third = jnp.dot(turned_ref[:channels, :], wave_ref[:, span:], preferred_element_type=f32)
        potential = both[:channels] + both[channels:] + third
        for cell in range(cells):
            out[cell] = potential[:, cell * slots : (cell + 1) * slots]


def potentials_of(held, pieces, waves, cells, slots):
    rows = waves[0].shape[0]
    channels = held[0].shape[-1]
    return pl.pallas_call(
        functools.partial(potential_kernel, len(held), pieces, len(waves)),
        in_specs=[whole()] * (len(held) + len(waves)),
        out_specs=[whole()] * len(waves),
        scratch_shapes=[
            pltpu.VMEM((rows, channels), f32),
            pltpu.VMEM((2 * channels, rows), bf16),
        ],
        out_shape=[jax.ShapeDtypeStruct((cells, channels, slots), f32)] * len(waves),
        compiler_params=params(),
        cost_estimate=pl.CostEstimate(
            flops=6 * rows * len(waves) * cells * slots * channels,
            bytes_accessed=4 * rows * len(waves) * cells * slots, transcendentals=0,
        ),
        name="potentials",
    )(*held, *waves)


def message_kernel(
    basis, sources, table, last, step_ref, own_ref, mix_ref, value_ref, *refs
):
    blocks, refs = refs[:sources], refs[sources:]
    if last:
        before_ref, out_ref, cell_ref, at_ref, own_col_ref, acc_ref, mixed_ref, wide_ref = refs[:8]
    else:
        out_ref, cell_ref, at_ref, own_col_ref, acc_ref = refs[:5]
    left_0, left_1, left_2, right_0, right_1, right_2 = refs[-6:]
    count = step_ref.shape[1]
    cells = own_ref.shape[0]
    slots = own_ref.shape[-1]
    along, planes = len(table[0]), len(table[0][0])
    channels = value_ref.shape[0]
    lefts, rights = (left_0, left_1, left_2), (right_0, right_1, right_2)

    for x, columns in enumerate(table):
        for y, column in enumerate(columns):
            for z, choices in enumerate(column):
                n = (x * along + y) * planes + z
                (_, source, index), others = choices[0], choices[1:]
                block = blocks[source][index]
                for condition, source, index in others:
                    block = jnp.where(condition(), blocks[source][index], block)
                high, low = split(block[:channels])
                cell_ref[n, :channels, :] = high
                cell_ref[n, channels:, :] = low
                at_ref[n] = block[channels:]
    for b in range(basis) if last else ():
        high, low = split(value_ref[...] * (mix_ref[b : b + 1, :] * math.exp(-b * b)))
        mixed_ref[b * channels : (b + 1) * channels, :channels] = high
        mixed_ref[b * channels : (b + 1) * channels, channels:] = low
    for cell in range(cells):
        columns = own_ref[cell, channels : channels + 8, :].T
        for axis in range(3):
            own_col_ref[cell, axis] = jnp.broadcast_to(columns[:, axis : axis + 1], (slots, slots))

    def fill(step, move):
        place_x = step_ref[0, step] + 1 + (move - 1)
        place_y = step_ref[1, step]
        plane = step_ref[2, step]
        if last:
            plane = jnp.where(is_even("gz"), plane, 1 - plane)
        shift_z = step_ref[3, step].astype(f32)
        left, right = lefts[move], rights[move]
        own = step_ref[4, step]
        near = []
        for n in range(3):
            number = (place_x * along + place_y + n) * planes + plane
            cell = cell_ref[number]
            right[:, n * slots : (n + 1) * slots] = cell
            right[:, (3 + n) * slots : (4 + n) * slots] = cell
            at = at_ref[number]
            near.append((at[0:1] + float(move - 1), at[1:2] + float(n - 1), at[2:3] + shift_z))
        tile = 16
        for m in range(slots // tile):
            at = m * tile
            own_x = own_col_ref[own, 0, at : at + tile, :]
            own_y = own_col_ref[own, 1, at : at + tile, :]
            own_z = own_col_ref[own, 2, at : at + tile, :]
            for n in range(3):
                dx = near[n][0] - own_x
                dy = near[n][1] - own_y
                dz = near[n][2] - own_z
                squared = dx * dx + dy * dy + dz * dz
                distance = squared * lax.rsqrt(jnp.maximum(squared, 1e-30))
                envelope = jnp.maximum(1.0 - squared, 0.0)
                term = envelope * envelope * jnp.exp2(squared * (-float((basis - 1) ** 2) * LOG2E))
                ratio = jnp.exp2(distance * (2.0 * (basis - 1) * LOG2E))
                if not last and move == 1 and n == 1:
                    i = lax.broadcasted_iota(jnp.int32, (tile, slots), 0) + at
                    j = lax.broadcasted_iota(jnp.int32, (tile, slots), 1)
                    same = jnp.logical_and(i == j, step_ref[3, step] == 0)
                    term = jnp.where(same, 0.0, term)
                for b in range(basis):
                    if b > 0:
                        term = term * ratio
                    high, low = split(term)
                    row = b * slots + at
                    left[row : row + tile, n * slots : (n + 1) * slots] = high
                    left[row : row + tile, (3 + n) * slots : (4 + n) * slots] = low

    def product(move):
        return lax.dot_general(
            lefts[move][...], rights[move][...], (((1,), (1,)), ((), ())), preferred_element_type=f32
        )

    fill(0, 0)

    def visit(step, carry):
        own = step_ref[4, step]
        fresh = step_ref[5, step] == 1
        acc_ref[own] = jnp.where(fresh, 0.0, acc_ref[own]) + product(0)
        fill(step, 1)
        acc_ref[own] += product(1)
        fill(step, 2)
        acc_ref[own] += product(2)
        fill(jnp.minimum(step + 1, count - 1), 0)
        return carry

    lax.fori_loop(0, count, visit, 0)
    wide = basis * channels
    for cell in range(cells):
        gathered = acc_ref[cell, :, :channels] + acc_ref[cell, :, channels:]
        if not last:
            out_ref[cell] = gathered
            continue
        high, low = split(gathered + before_ref[cell])
        here = slice(cell * slots, (cell + 1) * slots)
        for b in range(basis):
            wide_ref[here, b * channels : (b + 1) * channels] = high[b * slots : (b + 1) * slots]
            wide_ref[here, wide + b * channels : wide + (b + 1) * channels] = low[b * slots : (b + 1) * slots]
    if last:
        both = jnp.dot(wide_ref[:, :wide], mixed_ref[...], preferred_element_type=f32)
        both = both + jnp.dot(wide_ref[:, wide:], mixed_ref[...], preferred_element_type=f32)
        for cell in range(cells):
            part = both[cell * slots : (cell + 1) * slots]
            out_ref[cell] = (part[:, :channels] + part[:, channels:]).T


def pair_messages(steps, own, blocks, table, mix, w_value, before=None):
    cells, _, slots = own.shape
    basis, channels = mix.shape
    around = len(table) * len(table[0]) * len(table[0][0])
    count = steps.shape[1]
    last = before is not None
    sums = (cells, basis * slots, channels)
    closing = [
        pltpu.VMEM((basis * channels, 2 * channels), bf16),
        pltpu.VMEM((cells * slots, 2 * basis * channels), bf16),
    ]
    return pl.pallas_call(
        functools.partial(message_kernel, basis, len(blocks), table, last),
        in_specs=[pl.BlockSpec(memory_space=pltpu.SMEM)] + [whole()] * (3 + len(blocks) + last),
        out_specs=whole(),
        scratch_shapes=[
            pltpu.VMEM((around, 2 * channels, slots), bf16),
            pltpu.VMEM((around, 8, slots), f32),
            pltpu.VMEM((cells, 3, slots, slots), f32),
            pltpu.VMEM((cells, basis * slots, 2 * channels), f32),
        ]
        + closing * last
        + [pltpu.VMEM((basis * slots, 6 * slots), bf16)] * 3
        + [pltpu.VMEM((2 * channels, 6 * slots), bf16)] * 3,
        out_shape=jax.ShapeDtypeStruct((cells, channels, slots) if last else sums, f32),
        compiler_params=params(),
        cost_estimate=pl.CostEstimate(
            flops=count * 8 * basis * slots * 9 * slots * channels, bytes_accessed=1 << 20,
            transcendentals=0,
        ),
        name="messages",
    )(steps, own, mix, w_value, *blocks, *([before] if last else []))


def visits(cells_x, cells_y, cells_z, inside):
    table = []
    for x in range(cells_x):
        for y in range(cells_y):
            for z in range(cells_z):
                own = (x * cells_y + y) * cells_z + z
                for shift in (-1, 0, 1):
                    plane = z + shift
                    if (0 <= plane < cells_z) != inside:
                        continue
                    if not inside:
                        plane = 0 if shift > 0 else 1
                    table.append([x, y, plane, shift, own, 1, 1])
    for one, after in zip(table, table[1:]):
        if one[4] == after[4]:
            one[6] = after[5] = 0
    return np.array(table, np.int32).T.copy()


def mlp_kernel(count, shape, *refs):
    counts_ref, feature_ref = refs[:2]
    message_ref = refs[2]
    potentials = refs[3 : 3 + count]
    hidden_ref, back_ref, out_ref = refs[3 + count :]
    cells, channels, slots = feature_ref.shape
    columns = []
    for cell in range(cells):
        mixed = feature_ref[cell] + message_scale * message_ref[cell]
        for potential in potentials:
            mixed = mixed + potential[cell]
        columns.append(mixed)
    mixed = jnp.concatenate(columns, axis=1)
    inner = jnp.dot(hidden_ref[...].T, mixed, precision=HIGH, preferred_element_type=f32)
    hidden = inner * jax.nn.sigmoid(inner)
    updated = mixed + jnp.dot(back_ref[...].T, hidden, precision=HIGH, preferred_element_type=f32)
    slot = lax.broadcasted_iota(jnp.int32, (channels, slots), 1)
    for cell in range(cells):
        part = updated[:, cell * slots : (cell + 1) * slots]
        x, y, z = place_of(cell, shape)
        out_ref[cell] = jnp.where(slot < counts_ref[x, z, y], part, 0.0)


def atom_mlp(shape, counts, features, messages, potentials, w_hidden, w_out):
    return pl.pallas_call(
        functools.partial(mlp_kernel, len(potentials), shape),
        in_specs=[pl.BlockSpec(memory_space=pltpu.SMEM)]
        + [whole()] * (4 + len(potentials)),
        out_specs=whole(),
        out_shape=jax.ShapeDtypeStruct(features.shape, f32),
        compiler_params=params(),
        name="atom_mlp",
    )(counts, features, messages, *potentials, w_hidden, w_out)


def next_in_x(block, shape):
    size = lax.axis_size("gx")
    if size == 2:
        other = exchange(block, "gx", 1)
        return (other, shape[0] - 1), (other, 0)
    wide = block.reshape(shape + block.shape[1:])
    below, above = below_above(wide[:1], wide[-1:], "gx")
    return tuple((side.reshape((-1,) + block.shape[1:]), 0) for side in (below, above))


class Sources:
    def __init__(self):
        self.arrays = []

    def add(self, array):
        for n, held in enumerate(self.arrays):
            if held is array:
                return n
        self.arrays.append(array)
        return len(self.arrays) - 1

    def columns(self, block, shape):
        below, above = next_in_x(block, shape)
        inside = [(self.add(block), x) for x in range(shape[0])]
        return [(self.add(below[0]), below[1])] + inside + [(self.add(above[0]), above[1])]


def always():
    return True


def shards(
    features, positions, counts, waves, filter_table, w_value, w_charge, radial_mix, w_hidden, w_out
):
    shape = cells_x, cells_y, cells_z = features.shape[:3]
    channels, slots = features.shape[3:]
    total_waves = waves.shape[1]
    size_x, size_y, size_z = (lax.axis_size(a) for a in ("gx", "gy", "gz"))
    at_x, at_y, at_z = (lax.axis_index(a) for a in ("gx", "gy", "gz"))
    grid = (cells_x * size_x, cells_y * size_y, cells_z * size_z)
    cells = cells_x * cells_y * cells_z
    some_counts = jnp.transpose(counts, (0, 2, 1))
    flat_features = features.reshape(cells, channels, slots)

    own = pack(shape, grid, some_counts, flat_features, positions.reshape(cells * 3, 1, slots))
    rows = own.shape[1]
    packed = own.reshape(shape + (rows, slots))

    gathered = [own] + [exchange(own, "gy", s) for s in range(1, size_y)]
    if cells_z == 1:
        sides = neighbours(own, own, "gz", same=True)
    else:
        flat = (cells_x * cells_y, rows, slots)
        sides = neighbours(packed[:, :, 0].reshape(flat), packed[:, :, -1].reshape(flat), "gz")

    share = total_waves // size_y
    half = 2 * share // size_x
    piece = half // size_z
    chunk = min(piece, share // size_x)
    parts, tables = (), []
    for block in gathered:
        *parts, table = partial_factors(waves, share, chunk, block, parts, size_x)
        tables.append(table)

    summed = parts[0]
    for s in range(1, size_x):
        other = partner(at_x, s, size_x)
        to = parts[1]
        for n in range(2, size_x):
            to = jnp.where(lax.rem(other - at_x + size_x, size_x) == n, parts[n], to)
        summed = summed + exchange(to, "gx", s)
    low, high = (
        jnp.concatenate(
            [side[n : n + 1] for n in range(y, cells_x * cells_y, cells_y) for side in sides], axis=0
        )
        for y in (0, cells_y - 1)
    )
    edges = neighbours(low, high, "gy")
    value_near, summed = lax.optimization_barrier((w_value, summed))
    pieces = [lax.dynamic_slice_in_dim(summed, at_z * piece, piece, 0)]
    for s in range(1, size_z):
        other = partner(at_z, s, size_z)
        pieces.append(exchange(lax.dynamic_slice_in_dim(summed, other * piece, piece, 0), "gz", s))

    sources = Sources()

    def reaches(step, rank):
        return any(partner(i, step, size_y) == (i + rank) % size_y for i in range(size_y))

    columns = {
        step: sources.columns(block, shape)
        for step, block in enumerate(gathered)
        if any(reaches(step, rank) for rank in (-1, 0, 1))
    }

    def at_rank(step, rank):
        def condition():
            at = lax.axis_index("gy")
            return partner(at, step, size_y) == (at + rank) % size_y

        return condition

    def choices(x, y, z):
        rank = -1 if y < 0 else 1 if y == cells_y else 0
        y = y % cells_y
        found = []
        for step in columns:
            if reaches(step, rank):
                source, from_x = columns[step][x + 1]
                found.append((at_rank(step, rank), source, (from_x * cells_y + y) * cells_z + z))
        return found

    table = [
        [[choices(x, y, z) for z in range(cells_z)] for y in range(-1, cells_y + 1)]
        for x in range(-1, cells_x + 1)
    ]
    inner = jnp.asarray(visits(cells_x, cells_y, cells_z, True))
    near = pair_messages(inner, own, sources.arrays, table, radial_mix, value_near)

    scale = 1.0 / math.sqrt(grid[0] * grid[1] * grid[2] * slots) / math.sqrt(total_waves)
    rank = at_x * size_z + at_z
    block = at_y * (share // chunk) + (rank * piece) // (2 * chunk)
    charge, near, *edges = lax.optimization_barrier((w_charge, near, *edges))
    filtered = filtered_piece(scale, block.reshape(1), chunk, pieces, charge, filter_table)

    held_z = jnp.concatenate(
        [filtered] + [exchange(filtered, "gz", s) for s in range(1, size_z)], axis=0
    )
    held = [held_z] + [exchange(held_z, "gx", s) for s in range(1, size_x)]

    sources = Sources()
    flat = (cells_x, cells_y, 1)
    side_columns = [sources.columns(side, flat) for side in sides]
    edge_columns = [sources.columns(edge, (cells_x, 1, 2)) for edge in edges]

    def choices(x, y, z):
        if 0 <= y < cells_y:
            source, from_x = side_columns[z][x + 1]
            return [(always, source, from_x * cells_y + y)]
        found = []
        for n, columns in enumerate(edge_columns):
            source, from_x = columns[x + 1]
            first_is_here = y == cells_y
            condition = (lambda: is_even("gy")) if (n == 0) == first_is_here else (
                lambda: jnp.logical_not(is_even("gy"))
            )
            found.append((condition, source, from_x * 2 + z))
        return found

    table = [
        [[choices(x, y, z) for z in range(2)] for y in range(-1, cells_y + 1)]
        for x in range(-1, cells_x + 1)
    ]
    found = potentials_of(held, held_z.shape[0] // piece, tables, cells, slots)
    value_far, *found = lax.optimization_barrier((w_value, *found))
    returned = [found[0]] + [exchange(found[s], "gy", s) for s in range(1, size_y)]
    outer = jnp.asarray(visits(cells_x, cells_y, cells_z, False))
    messages = pair_messages(outer, own, sources.arrays, table, radial_mix, value_far, near)

    updated = atom_mlp(
        shape, some_counts, flat_features, messages, returned, w_hidden, w_out
    )
    return updated.reshape(features.shape)


def solution(mesh):
    placed = (
        P("gx", "gy", "gz", None, None),
        P("gx", "gy", "gz", None, None),
        P("gx", "gy", "gz"),
        P(),
        P(),
        P(),
        P(),
        P(),
        P(),
        P(),
    )
    return jax.shard_map(
        shards,
        mesh=mesh,
        in_specs=placed,
        out_specs=P("gx", "gy", "gz", None, None),
        check_vma=False,
    )
```

```python
import functools
import math

import numpy as np

import jax
import jax.numpy as jnp
from jax import lax
from jax.experimental import pallas as pl
from jax.experimental.pallas import tpu as pltpu
from jax.sharding import PartitionSpec as P


HIGH = lax.Precision.HIGH
message_scale = 0.125
bf16 = jnp.bfloat16
f32 = jnp.float32
VMEM_LIMIT = 28 * 1024 * 1024
PACK_LIMIT = 62 * 1024 * 1024


LOG2E = math.log2(math.e)


def partner(i, step, count):
    return i ^ step


def exchange(block, axis, step):
    count = lax.axis_size(axis)
    pairs = [(i, partner(i, step, count)) for i in range(count)]
    return lax.ppermute(block, axis, pairs)


def is_even(axis):
    if lax.axis_size(axis) % 2:
        return jnp.bool_(True)
    return lax.rem(lax.axis_index(axis), 2) == 0


def neighbours(low, high, axis, same=False):
    count = lax.axis_size(axis)
    if count == 1:
        return low, high
    if count % 2:
        up = lax.ppermute(low, axis, [(i, (i - 1) % count) for i in range(count)])
        down = lax.ppermute(high, axis, [(i, (i + 1) % count) for i in range(count)])
        return up, down
    even = is_even(axis)
    first = high if same else jnp.where(even, high, low)
    second = low if same else jnp.where(even, low, high)
    one = [(i, i ^ 1) for i in range(count)]
    two = [(i, (i + 1 if i % 2 else i - 1) % count) for i in range(count)]
    return lax.ppermute(first, axis, one), lax.ppermute(second, axis, two)


def below_above(low, high, axis):
    first, second = neighbours(low, high, axis)
    even = is_even(axis)
    return jnp.where(even, second, first), jnp.where(even, first, second)


def split(x):
    high = x.astype(bf16)
    low = (x - high.astype(f32)).astype(bf16)
    return high, low


def whole():
    return pl.BlockSpec(memory_space=pltpu.VMEM)


def params(limit=VMEM_LIMIT):
    return pltpu.CompilerParams(vmem_limit_bytes=limit)


def place_of(cell, shape):
    return cell // (shape[1] * shape[2]), cell // shape[2] % shape[1], cell % shape[2]


def pack_kernel(
    shape, grid, counts_hbm, feature_hbm, position_hbm, waves_hbm, out_ref, column_ref,
    counts_ref, feature_ref, position_ref, waves_ref, sems,
):
    total = column_ref.shape[0]
    begin = pl.multiple_of(lax.axis_index("gy") * total, total)
    cells, channels, slots = feature_ref.shape
    copies = [
        pltpu.make_async_copy(counts_hbm, counts_ref, sems.at[0]),
        pltpu.make_async_copy(position_hbm, position_ref, sems.at[1]),
        pltpu.make_async_copy(waves_hbm.at[:, pl.ds(begin, total)], waves_ref, sems.at[2]),
        pltpu.make_async_copy(feature_hbm, feature_ref, sems.at[3]),
    ]
    for copy in copies:
        copy.start()
    for copy in copies[:3]:
        copy.wait()
    waves = waves_ref[...].astype(f32)
    column_ref[...] = jnp.concatenate([waves, jnp.zeros((5, total), f32)], axis=0).T
    copies[3].wait()
    slot = lax.broadcasted_iota(jnp.int32, (channels, slots), 1)
    for cell in range(cells):
        place = place_of(cell, shape)
        held = slot < counts_ref[place[0], place[2], place[1]]
        out_ref[cell, :channels, :] = jnp.where(held, feature_ref[cell], 0.0)
        at = [position_ref[3 * cell + axis] for axis in range(3)]
        rows = list(at)
        for axis, name in enumerate(("gx", "gy", "gz")):
            here = lax.axis_index(name) * shape[axis] + place[axis]
            rows.append((at[axis] + here.astype(f32)) * (1.0 / grid[axis]))
        out_ref[cell, channels:, :] = jnp.concatenate(rows + [jnp.zeros((2, slots), f32)], axis=0)


def pack(shape, grid, counts, features, positions, waves, total):
    cells, channels, slots = features.shape
    return pl.pallas_call(
        functools.partial(pack_kernel, shape, grid),
        in_specs=[pl.BlockSpec(memory_space=pltpu.HBM)] * 4,
        out_specs=[whole()] * 2,
        out_shape=[
            jax.ShapeDtypeStruct((cells, channels + 8, slots), f32),
            jax.ShapeDtypeStruct((total, 8), f32),
        ],
        scratch_shapes=[
            pltpu.SMEM(counts.shape, jnp.int32),
            pltpu.VMEM(features.shape, f32),
            pltpu.VMEM(positions.shape, f32),
            pltpu.VMEM((3, total), jnp.int32),
            pltpu.SemaphoreType.DMA((4,)),
        ],
        compiler_params=params(PACK_LIMIT),
        name="pack",
    )(counts, features, positions, waves)


def fitted(function, terms):
    t = 0.125 * (1.0 + np.cos(np.pi * (np.arange(terms) + 0.5) / terms))
    solved = np.linalg.solve(np.vander(t, terms, increasing=True), function(np.sqrt(t)))
    return [float(c) for c in solved]


SIN = fitted(lambda u: math.sqrt(2.0) * np.sin(np.pi * u) / u, 5)
COS = fitted(lambda u: math.sqrt(2.0) * np.cos(np.pi * u), 5)


def poly(coefficients, t):
    acc = t * coefficients[-1] + coefficients[-2]
    for c in coefficients[-3::-1]:
        acc = acc * t + c
    return acc


def turns(u):
    u = u - jnp.round(u)
    t = u * u
    sine = poly(SIN, t) * u
    cosine = poly(COS, t)
    return 1.0 - sine * sine, sine * cosine


def factor_kernel(parts, chunk, first, column_ref, block_ref, *refs):
    before = refs[: 0 if first else parts]
    refs = refs[len(before) :]
    after, wave_ref, weight_ref = refs[:parts], refs[parts], refs[parts + 1]
    cells, _, slots = block_ref.shape
    channels = after[0].shape[-1]
    span = cells * slots
    total = wave_ref.shape[0] // 2
    at_x = lax.axis_index("gx")
    for cell in range(cells):
        high, low = split(block_ref[cell, :channels, :])
        for at in (cell * slots, span + cell * slots):
            weight_ref[:channels, at : at + slots] = high
            weight_ref[channels:, at : at + slots] = low

    def some(j, carry):
        here = pl.multiple_of(j * chunk, chunk)
        wave_x = column_ref[pl.ds(here, chunk), 0:1]
        wave_y = column_ref[pl.ds(here, chunk), 1:2]
        wave_z = column_ref[pl.ds(here, chunk), 2:3]
        row = pl.multiple_of(j * 2 * chunk, 2 * chunk)
        for cell in range(cells):
            at = cell * slots
            frac = block_ref[cell, channels + 3 : channels + 6, :]
            u = wave_x * frac[0:1] + wave_y * frac[1:2] + wave_z * frac[2:3]
            cosine, sine = turns(u)
            high, low = split(cosine)
            wave_ref[pl.ds(row, chunk), at : at + slots] = high
            wave_ref[pl.ds(row, chunk), span + at : span + at + slots] = low
            high, low = split(sine)
            wave_ref[pl.ds(row + chunk, chunk), at : at + slots] = high
            wave_ref[pl.ds(row + chunk, chunk), span + at : span + at + slots] = low
        return carry

    lax.fori_loop(0, total // chunk, some, 0, unroll=total // chunk <= 8)
    half = 2 * total // parts
    for n in range(parts):
        row = pl.multiple_of(lax.rem(at_x + n, parts) * half, half)
        both = lax.dot_general(
            wave_ref[pl.ds(row, half), :], weight_ref[...], (((1,), (1,)), ((), ())),
            preferred_element_type=f32,
        )
        both = both[:, :channels] + both[:, channels:]
        after[n][...] = both if first else before[n][...] + both


def partial_factors(columns, chunk, block, before, parts):
    total = columns.shape[0]
    cells, rows, slots = block.shape
    channels = rows - 8
    span = cells * slots
    out = [jax.ShapeDtypeStruct((2 * total // parts, channels), f32)] * parts
    return pl.pallas_call(
        functools.partial(factor_kernel, parts, chunk, not before),
        in_specs=[whole()] * (2 + len(before)),
        out_specs=[whole()] * (parts + 1),
        out_shape=out + [jax.ShapeDtypeStruct((2 * total, 2 * span), bf16)],
        input_output_aliases={2 + n: n for n in range(len(before))},
        scratch_shapes=[pltpu.VMEM((2 * channels, 2 * span), bf16)],
        compiler_params=params(),
        cost_estimate=pl.CostEstimate(
            flops=8 * total * span * channels, bytes_accessed=8 * total * span, transcendentals=0
        ),
        name="factors",
    )(columns, block, *before)


def filter_kernel(scale, block_ref, *refs):
    parts, (weight_ref, table_ref, out_ref) = refs[:-3], refs[-3:]
    summed = parts[0][...]
    for part in parts[1:]:
        summed = summed + part[...]
    projected = jnp.dot(summed, weight_ref[...], precision=HIGH, preferred_element_type=f32)
    table = table_ref[...] * scale
    for n in range(0, summed.shape[0], table.shape[0]):
        out_ref[n : n + table.shape[0], :] = projected[n : n + table.shape[0]] * table


def filtered_piece(scale, block, chunk, parts, w_charge, table):
    rows, channels = parts[0].shape
    fixed = pl.BlockSpec((rows, channels), lambda i, block: (0, 0))
    return pl.pallas_call(
        functools.partial(filter_kernel, scale),
        grid_spec=pltpu.PrefetchScalarGridSpec(
            num_scalar_prefetch=1,
            grid=(1,),
            in_specs=[fixed] * len(parts)
            + [
                pl.BlockSpec(w_charge.shape, lambda i, block: (0, 0)),
                pl.BlockSpec((chunk, channels), lambda i, block: (block[0], 0)),
            ],
            out_specs=fixed,
        ),
        out_shape=jax.ShapeDtypeStruct((rows, channels), f32),
        compiler_params=params(),
        name="filter",
    )(block, *parts, w_charge, table)


def potential_kernel(groups, pieces, blocks, *refs):
    held = refs[:groups]
    waves = refs[groups : groups + blocks]
    outs = refs[groups + blocks : -2]
    ordered_ref, turned_ref = refs[-2:]
    channels = ordered_ref.shape[-1]
    piece = held[0].shape[0] // pieces
    for group in range(groups):
        for n in range(pieces):
            rank_x = partner(lax.axis_index("gx"), group, groups)
            rank_z = partner(lax.axis_index("gz"), n, pieces)
            at = pl.multiple_of((rank_x * pieces + rank_z) * piece, piece)
            ordered_ref[pl.ds(at, piece), :] = held[group][n * piece : (n + 1) * piece, :]
    high, low = split(ordered_ref[...].T)
    turned_ref[:channels, :] = high
    turned_ref[channels:, :] = low
    for wave_ref, out in zip(waves, outs):
        cells, _, slots = out.shape
        span = cells * slots
        both = jnp.dot(turned_ref[...], wave_ref[:, :span], preferred_element_type=f32)
        third = jnp.dot(turned_ref[:channels, :], wave_ref[:, span:], preferred_element_type=f32)
        potential = both[:channels] + both[channels:] + third
        for cell in range(cells):
            out[cell] = potential[:, cell * slots : (cell + 1) * slots]


def potentials_of(held, pieces, waves, cells, slots):
    rows = waves[0].shape[0]
    channels = held[0].shape[-1]
    return pl.pallas_call(
        functools.partial(potential_kernel, len(held), pieces, len(waves)),
        in_specs=[whole()] * (len(held) + len(waves)),
        out_specs=[whole()] * len(waves),
        scratch_shapes=[
            pltpu.VMEM((rows, channels), f32),
            pltpu.VMEM((2 * channels, rows), bf16),
        ],
        out_shape=[jax.ShapeDtypeStruct((cells, channels, slots), f32)] * len(waves),
        compiler_params=params(),
        cost_estimate=pl.CostEstimate(
            flops=6 * rows * len(waves) * cells * slots * channels,
            bytes_accessed=4 * rows * len(waves) * cells * slots, transcendentals=0,
        ),
        name="potentials",
    )(*held, *waves)


def message_kernel(
    basis, sources, table, last, first, step_ref, own_ref, mix_ref, value_ref, *refs
):
    blocks, refs = refs[:sources], refs[sources:]
    if last:
        before, refs = refs[:last], refs[last:]
        out_ref, cell_ref, at_ref, own_col_ref, acc_ref, mixed_ref, wide_ref = refs[:7]
    else:
        out_ref, cell_ref, at_ref, own_col_ref, acc_ref = refs[:5]
    left_0, left_1, left_2, right_0, right_1, right_2 = refs[-6:]
    count = step_ref.shape[1]
    cells = acc_ref.shape[0]
    slots = own_ref.shape[-1]
    along, planes = len(table[0]), len(table[0][0])
    channels = value_ref.shape[0]
    lefts, rights = (left_0, left_1, left_2), (right_0, right_1, right_2)

    for x, columns in enumerate(table):
        for y, column in enumerate(columns):
            for z, choices in enumerate(column):
                n = (x * along + y) * planes + z
                (_, source, index), others = choices[0], choices[1:]
                block = blocks[source][index]
                for condition, source, index in others:
                    block = jnp.where(condition(), blocks[source][index], block)
                high, low = split(block[:channels])
                cell_ref[n, :channels, :] = high
                cell_ref[n, channels:, :] = low
                at_ref[n] = block[channels:]
    for b in range(basis) if last else ():
        high, low = split(value_ref[...] * (mix_ref[b : b + 1, :] * math.exp(-b * b)))
        mixed_ref[b * channels : (b + 1) * channels, :channels] = high
        mixed_ref[b * channels : (b + 1) * channels, channels:] = low
    for cell in range(cells):
        columns = own_ref[first + cell, channels : channels + 8, :].T
        for axis in range(3):
            own_col_ref[cell, axis] = jnp.broadcast_to(columns[:, axis : axis + 1], (slots, slots))

    def fill(step, move):
        place_x = step_ref[0, step] + 1 + (move - 1)
        place_y = step_ref[1, step]
        plane = step_ref[2, step]
        if last:
            plane = jnp.where(is_even("gz"), plane, 1 - plane)
        shift_z = step_ref[3, step].astype(f32)
        left, right = lefts[move], rights[move]
        own = step_ref[4, step]
        near = []
        for n in range(3):
            number = (place_x * along + place_y + n) * planes + plane
            cell = cell_ref[number]
            right[:, n * slots : (n + 1) * slots] = cell
            right[:, (3 + n) * slots : (4 + n) * slots] = cell
            at = at_ref[number]
            near.append((at[0:1] + float(move - 1), at[1:2] + float(n - 1), at[2:3] + shift_z))
        tile = 16
        for m in range(slots // tile):
            at = m * tile
            own_x = own_col_ref[own, 0, at : at + tile, :]
            own_y = own_col_ref[own, 1, at : at + tile, :]
            own_z = own_col_ref[own, 2, at : at + tile, :]
            for n in range(3):
                dx = near[n][0] - own_x
                dy = near[n][1] - own_y
                dz = near[n][2] - own_z
                squared = dx * dx + dy * dy + dz * dz
                distance = squared * lax.rsqrt(jnp.maximum(squared, 1e-30))
                envelope = jnp.maximum(1.0 - squared, 0.0)
                term = envelope * envelope * jnp.exp2(squared * (-float((basis - 1) ** 2) * LOG2E))
                ratio = jnp.exp2(distance * (2.0 * (basis - 1) * LOG2E))
                if not last and move == 1 and n == 1:
                    i = lax.broadcasted_iota(jnp.int32, (tile, slots), 0) + at
                    j = lax.broadcasted_iota(jnp.int32, (tile, slots), 1)
                    same = jnp.logical_and(i == j, step_ref[3, step] == 0)
                    term = jnp.where(same, 0.0, term)
                for b in range(basis):
                    if b > 0:
                        term = term * ratio
                    high, low = split(term)
                    row = b * slots + at
                    left[row : row + tile, n * slots : (n + 1) * slots] = high
                    left[row : row + tile, (3 + n) * slots : (4 + n) * slots] = low

    def product(move):
        return lax.dot_general(
            lefts[move][...], rights[move][...], (((1,), (1,)), ((), ())), preferred_element_type=f32
        )

    fill(0, 0)

    def visit(step, carry):
        own = step_ref[4, step]
        fresh = step_ref[5, step] == 1
        acc_ref[own] = jnp.where(fresh, 0.0, acc_ref[own]) + product(0)
        fill(step, 1)
        acc_ref[own] += product(1)
        fill(step, 2)
        acc_ref[own] += product(2)
        fill(jnp.minimum(step + 1, count - 1), 0)
        return carry

    lax.fori_loop(0, count, visit, 0)
    wide = basis * channels
    for cell in range(cells):
        gathered = acc_ref[cell, :, :channels] + acc_ref[cell, :, channels:]
        if not last:
            out_ref[cell] = gathered
            continue
        per = cells // last
        high, low = split(gathered + before[cell // per][cell % per])
        here = slice(cell * slots, (cell + 1) * slots)
        for b in range(basis):
            wide_ref[here, b * channels : (b + 1) * channels] = high[b * slots : (b + 1) * slots]
            wide_ref[here, wide + b * channels : wide + (b + 1) * channels] = low[b * slots : (b + 1) * slots]
    if last:
        both = jnp.dot(wide_ref[:, :wide], mixed_ref[...], preferred_element_type=f32)
        both = both + jnp.dot(wide_ref[:, wide:], mixed_ref[...], preferred_element_type=f32)
        for cell in range(cells):
            part = both[cell * slots : (cell + 1) * slots]
            out_ref[cell] = (part[:, :channels] + part[:, channels:]).T


def pair_messages(steps, own, blocks, table, mix, w_value, cells, first, before=()):
    slots = own.shape[-1]
    basis, channels = mix.shape
    around = len(table) * len(table[0]) * len(table[0][0])
    count = steps.shape[1]
    last = len(before)
    sums = (cells, basis * slots, channels)
    closing = [
        pltpu.VMEM((basis * channels, 2 * channels), bf16),
        pltpu.VMEM((cells * slots, 2 * basis * channels), bf16),
    ]
    return pl.pallas_call(
        functools.partial(message_kernel, basis, len(blocks), table, last, first),
        in_specs=[pl.BlockSpec(memory_space=pltpu.SMEM)] + [whole()] * (3 + len(blocks) + last),
        out_specs=whole(),
        scratch_shapes=[
            pltpu.VMEM((around, 2 * channels, slots), bf16),
            pltpu.VMEM((around, 8, slots), f32),
            pltpu.VMEM((cells, 3, slots, slots), f32),
            pltpu.VMEM((cells, basis * slots, 2 * channels), f32),
        ]
        + closing * bool(last)
        + [pltpu.VMEM((basis * slots, 6 * slots), bf16)] * 3
        + [pltpu.VMEM((2 * channels, 6 * slots), bf16)] * 3,
        out_shape=jax.ShapeDtypeStruct((cells, channels, slots) if last else sums, f32),
        compiler_params=params(),
        cost_estimate=pl.CostEstimate(
            flops=count * 8 * basis * slots * 9 * slots * channels, bytes_accessed=1 << 20,
            transcendentals=0,
        ),
        name="messages",
    )(steps, own, mix, w_value, *blocks, *before)


def visits(cells_x, cells_y, cells_z, inside, first=0, end=None):
    table = []
    for x in range(cells_x):
        for y in range(cells_y):
            for z in range(cells_z):
                own = (x * cells_y + y) * cells_z + z
                if not first <= own < (cells_x * cells_y * cells_z if end is None else end):
                    continue
                for shift in (-1, 0, 1):
                    plane = z + shift
                    if (0 <= plane < cells_z) != inside:
                        continue
                    if not inside:
                        plane = 0 if shift > 0 else 1
                    table.append([x - first // (cells_y * cells_z), y, plane, shift, own - first, 1, 1])
    for one, after in zip(table, table[1:]):
        if one[4] == after[4]:
            one[6] = after[5] = 0
    return np.array(table, np.int32).T.copy()


def mlp_kernel(count, shape, *refs):
    counts_ref, feature_ref = refs[:2]
    message_ref = refs[2]
    potentials = refs[3 : 3 + count]
    hidden_ref, back_ref, out_ref = refs[3 + count :]
    cells, channels, slots = feature_ref.shape
    columns = []
    for cell in range(cells):
        mixed = feature_ref[cell] + message_scale * message_ref[cell]
        for potential in potentials:
            mixed = mixed + potential[cell]
        columns.append(mixed)
    mixed = jnp.concatenate(columns, axis=1)
    inner = lax.dot_general(
        hidden_ref[...], mixed, (((0,), (0,)), ((), ())), precision=HIGH, preferred_element_type=f32
    )
    hidden = inner * jax.nn.sigmoid(inner)
    updated = mixed + lax.dot_general(
        back_ref[...], hidden, (((0,), (0,)), ((), ())), precision=HIGH, preferred_element_type=f32
    )
    slot = lax.broadcasted_iota(jnp.int32, (channels, slots), 1)
    for cell in range(cells):
        part = updated[:, cell * slots : (cell + 1) * slots]
        x, y, z = place_of(cell, shape)
        out_ref[cell] = jnp.where(slot < counts_ref[x, z, y], part, 0.0)


def atom_mlp(shape, counts, features, messages, potentials, w_hidden, w_out):
    return pl.pallas_call(
        functools.partial(mlp_kernel, len(potentials), shape),
        in_specs=[pl.BlockSpec(memory_space=pltpu.SMEM)]
        + [whole()] * (4 + len(potentials)),
        out_specs=whole(),
        out_shape=jax.ShapeDtypeStruct(features.shape, f32),
        compiler_params=params(),
        name="atom_mlp",
    )(counts, features, messages, *potentials, w_hidden, w_out)


def next_in_x(block, shape):
    size = lax.axis_size("gx")
    if size == 2:
        other = exchange(block, "gx", 1)
        return (other, shape[0] - 1), (other, 0)
    wide = block.reshape(shape + block.shape[1:])
    below, above = below_above(wide[:1], wide[-1:], "gx")
    return tuple((side.reshape((-1,) + block.shape[1:]), 0) for side in (below, above))


class Sources:
    def __init__(self):
        self.arrays = []

    def add(self, array):
        for n, held in enumerate(self.arrays):
            if held is array:
                return n
        self.arrays.append(array)
        return len(self.arrays) - 1

    def columns(self, block, shape):
        below, above = next_in_x(block, shape)
        inside = [(self.add(block), x) for x in range(shape[0])]
        return [(self.add(below[0]), below[1])] + inside + [(self.add(above[0]), above[1])]


def always():
    return True


def shards(
    features, positions, counts, waves, filter_table, w_value, w_charge, radial_mix, w_hidden, w_out
):
    shape = cells_x, cells_y, cells_z = features.shape[:3]
    channels, slots = features.shape[3:]
    total_waves = waves.shape[1]
    size_x, size_y, size_z = (lax.axis_size(a) for a in ("gx", "gy", "gz"))
    at_x, at_y, at_z = (lax.axis_index(a) for a in ("gx", "gy", "gz"))
    grid = (cells_x * size_x, cells_y * size_y, cells_z * size_z)
    cells = cells_x * cells_y * cells_z
    some_counts = jnp.transpose(counts, (0, 2, 1))
    flat_features = features.reshape(cells, channels, slots)

    share = total_waves // size_y
    own, columns = pack(
        shape, grid, some_counts, flat_features, positions.reshape(cells * 3, 1, slots), waves, share
    )
    rows = own.shape[1]
    packed = own.reshape(shape + (rows, slots))

    gathered = [own] + [exchange(own, "gy", s) for s in range(1, size_y)]
    if cells_z == 1:
        sides = neighbours(own, own, "gz", same=True)
    else:
        flat = (cells_x * cells_y, rows, slots)
        sides = neighbours(packed[:, :, 0].reshape(flat), packed[:, :, -1].reshape(flat), "gz")

    half = 2 * share // size_x
    piece = half // size_z
    chunk = min(piece, share // size_x)
    parts, tables = (), []
    for block in gathered:
        *parts, table = partial_factors(columns, chunk, block, parts, size_x)
        tables.append(table)

    summed = parts[0]
    for s in range(1, size_x):
        other = partner(at_x, s, size_x)
        to = parts[1]
        for n in range(2, size_x):
            to = jnp.where(lax.rem(other - at_x + size_x, size_x) == n, parts[n], to)
        summed = summed + exchange(to, "gx", s)
    low, high = (
        jnp.concatenate(
            [side[n : n + 1] for n in range(y, cells_x * cells_y, cells_y) for side in sides], axis=0
        )
        for y in (0, cells_y - 1)
    )
    edges = neighbours(low, high, "gy")
    value_near, summed = lax.optimization_barrier((w_value, summed))
    pieces = [lax.dynamic_slice_in_dim(summed, at_z * piece, piece, 0)]
    for s in range(1, size_z):
        other = partner(at_z, s, size_z)
        pieces.append(exchange(lax.dynamic_slice_in_dim(summed, other * piece, piece, 0), "gz", s))

    sources = Sources()

    def reaches(step, rank):
        return any(partner(i, step, size_y) == (i + rank) % size_y for i in range(size_y))

    columns = {
        step: sources.columns(block, shape)
        for step, block in enumerate(gathered)
        if any(reaches(step, rank) for rank in (-1, 0, 1))
    }

    def at_rank(step, rank):
        def condition():
            at = lax.axis_index("gy")
            return partner(at, step, size_y) == (at + rank) % size_y

        return condition

    def choices(x, y, z):
        rank = -1 if y < 0 else 1 if y == cells_y else 0
        y = y % cells_y
        found = []
        for step in columns:
            if reaches(step, rank):
                source, from_x = columns[step][x + 1]
                found.append((at_rank(step, rank), source, (from_x * cells_y + y) * cells_z + z))
        return found

    table = [
        [[choices(x, y, z) for z in range(cells_z)] for y in range(-1, cells_y + 1)]
        for x in range(-1, cells_x + 1)
    ]
    layer = cells_y * cells_z
    at_once = (cells_x + 1) // 2
    near = []

    def near_messages(begin, value):
        end = min(begin + at_once, cells_x)
        inner = visits(cells_x, cells_y, cells_z, True, begin * layer, end * layer)
        return pair_messages(
            jnp.asarray(inner), own, sources.arrays, table[begin : end + 2], radial_mix, value,
            (end - begin) * layer, begin * layer,
        )

    near.append(near_messages(0, value_near))

    scale = 1.0 / math.sqrt(grid[0] * grid[1] * grid[2] * slots) / math.sqrt(total_waves)
    rank = at_x * size_z + at_z
    block = at_y * (share // chunk) + (rank * piece) // (2 * chunk)
    charge, near[0], *edges = lax.optimization_barrier((w_charge, near[0], *edges))
    filtered = filtered_piece(scale, block.reshape(1), chunk, pieces, charge, filter_table)

    value_near, filtered = lax.optimization_barrier((w_value, filtered))
    if cells_x > 1:
        near.append(near_messages(at_once, value_near))
    held_z = jnp.concatenate(
        [filtered] + [exchange(filtered, "gz", s) for s in range(1, size_z)], axis=0
    )
    held_z, *near = lax.optimization_barrier((held_z, *near))
    held = [held_z] + [exchange(held_z, "gx", s) for s in range(1, size_x)]

    sources = Sources()
    flat = (cells_x, cells_y, 1)
    side_columns = [sources.columns(side, flat) for side in sides]
    edge_columns = [sources.columns(edge, (cells_x, 1, 2)) for edge in edges]

    def choices(x, y, z):
        if 0 <= y < cells_y:
            source, from_x = side_columns[z][x + 1]
            return [(always, source, from_x * cells_y + y)]
        found = []
        for n, columns in enumerate(edge_columns):
            source, from_x = columns[x + 1]
            first_is_here = y == cells_y
            condition = (lambda: is_even("gy")) if (n == 0) == first_is_here else (
                lambda: jnp.logical_not(is_even("gy"))
            )
            found.append((condition, source, from_x * 2 + z))
        return found

    table = [
        [[choices(x, y, z) for z in range(2)] for y in range(-1, cells_y + 1)]
        for x in range(-1, cells_x + 1)
    ]
    found = potentials_of(held, held_z.shape[0] // piece, tables, cells, slots)
    value_far, *found = lax.optimization_barrier((w_value, *found))
    returned = [found[0]] + [exchange(found[s], "gy", s) for s in range(1, size_y)]
    outer = jnp.asarray(visits(cells_x, cells_y, cells_z, False))
    messages = pair_messages(
        outer, own, sources.arrays, table, radial_mix, value_far, cells, 0, near
    )

    updated = atom_mlp(
        shape, some_counts, flat_features, messages, returned, w_hidden, w_out
    )
    return updated.reshape(features.shape)


def solution(mesh):
    placed = (
        P("gx", "gy", "gz", None, None),
        P("gx", "gy", "gz", None, None),
        P("gx", "gy", "gz"),
        P(),
        P(),
        P(),
        P(),
        P(),
        P(),
        P(),
    )
    return jax.shard_map(
        shards,
        mesh=mesh,
        in_specs=placed,
        out_specs=P("gx", "gy", "gz", None, None),
        check_vma=False,
    )
```

```python
import functools
import math

import numpy as np

import jax
import jax.numpy as jnp
from jax import lax
from jax.experimental import pallas as pl
from jax.experimental.pallas import tpu as pltpu
from jax.sharding import PartitionSpec as P


HIGH = lax.Precision.HIGH
message_scale = 0.125
bf16 = jnp.bfloat16
f32 = jnp.float32
VMEM_LIMIT = 28 * 1024 * 1024
PACK_LIMIT = 62 * 1024 * 1024


LOG2E = math.log2(math.e)


def partner(i, step, count):
    return i ^ step


def exchange(block, axis, step):
    count = lax.axis_size(axis)
    pairs = [(i, partner(i, step, count)) for i in range(count)]
    return lax.ppermute(block, axis, pairs)


def is_even(axis):
    if lax.axis_size(axis) % 2:
        return jnp.bool_(True)
    return lax.rem(lax.axis_index(axis), 2) == 0


def neighbours(low, high, axis, same=False):
    count = lax.axis_size(axis)
    if count == 1:
        return low, high
    if count % 2:
        up = lax.ppermute(low, axis, [(i, (i - 1) % count) for i in range(count)])
        down = lax.ppermute(high, axis, [(i, (i + 1) % count) for i in range(count)])
        return up, down
    even = is_even(axis)
    first = high if same else jnp.where(even, high, low)
    second = low if same else jnp.where(even, low, high)
    one = [(i, i ^ 1) for i in range(count)]
    two = [(i, (i + 1 if i % 2 else i - 1) % count) for i in range(count)]
    return lax.ppermute(first, axis, one), lax.ppermute(second, axis, two)


def below_above(low, high, axis):
    first, second = neighbours(low, high, axis)
    even = is_even(axis)
    return jnp.where(even, second, first), jnp.where(even, first, second)


def split(x):
    high = x.astype(bf16)
    low = (x - high.astype(f32)).astype(bf16)
    return high, low


def whole():
    return pl.BlockSpec(memory_space=pltpu.VMEM)


def params(limit=VMEM_LIMIT):
    return pltpu.CompilerParams(vmem_limit_bytes=limit)


def place_of(cell, shape):
    return cell // (shape[1] * shape[2]), cell // shape[2] % shape[1], cell % shape[2]


def pack_kernel(
    shape, grid, counts_hbm, feature_hbm, position_hbm, waves_hbm, out_ref, column_ref,
    counts_ref, feature_ref, position_ref, waves_ref, sems,
):
    total = column_ref.shape[0]
    begin = pl.multiple_of(lax.axis_index("gy") * total, total)
    cells, channels, slots = feature_ref.shape
    copies = [
        pltpu.make_async_copy(counts_hbm, counts_ref, sems.at[0]),
        pltpu.make_async_copy(position_hbm, position_ref, sems.at[1]),
        pltpu.make_async_copy(waves_hbm.at[:, pl.ds(begin, total)], waves_ref, sems.at[2]),
        pltpu.make_async_copy(feature_hbm, feature_ref, sems.at[3]),
    ]
    for copy in copies:
        copy.start()
    for copy in copies[:3]:
        copy.wait()
    waves = waves_ref[...].astype(f32)
    column_ref[...] = jnp.concatenate([waves, jnp.zeros((5, total), f32)], axis=0).T
    copies[3].wait()
    slot = lax.broadcasted_iota(jnp.int32, (channels, slots), 1)
    for cell in range(cells):
        place = place_of(cell, shape)
        held = slot < counts_ref[place[0], place[2], place[1]]
        out_ref[cell, :channels, :] = jnp.where(held, feature_ref[cell], 0.0)
        at = [position_ref[3 * cell + axis] for axis in range(3)]
        rows = list(at)
        for axis, name in enumerate(("gx", "gy", "gz")):
            here = lax.axis_index(name) * shape[axis] + place[axis]
            rows.append((at[axis] + here.astype(f32)) * (1.0 / grid[axis]))
        out_ref[cell, channels:, :] = jnp.concatenate(rows + [jnp.zeros((2, slots), f32)], axis=0)


def pack(shape, grid, counts, features, positions, waves, total):
    cells, channels, slots = features.shape
    return pl.pallas_call(
        functools.partial(pack_kernel, shape, grid),
        in_specs=[pl.BlockSpec(memory_space=pltpu.HBM)] * 4,
        out_specs=[whole()] * 2,
        out_shape=[
            jax.ShapeDtypeStruct((cells, channels + 8, slots), f32),
            jax.ShapeDtypeStruct((total, 8), f32),
        ],
        scratch_shapes=[
            pltpu.SMEM(counts.shape, jnp.int32),
            pltpu.VMEM(features.shape, f32),
            pltpu.VMEM(positions.shape, f32),
            pltpu.VMEM((3, total), jnp.int32),
            pltpu.SemaphoreType.DMA((4,)),
        ],
        compiler_params=params(PACK_LIMIT),
        name="pack",
    )(counts, features, positions, waves)


def fitted(function, terms):
    t = 0.125 * (1.0 + np.cos(np.pi * (np.arange(terms) + 0.5) / terms))
    solved = np.linalg.solve(np.vander(t, terms, increasing=True), function(np.sqrt(t)))
    return [float(c) for c in solved]


SIN = fitted(lambda u: math.sqrt(2.0) * np.sin(np.pi * u) / u, 5)
COS = fitted(lambda u: math.sqrt(2.0) * np.cos(np.pi * u), 5)


def poly(coefficients, t):
    acc = t * coefficients[-1] + coefficients[-2]
    for c in coefficients[-3::-1]:
        acc = acc * t + c
    return acc


def turns(u):
    u = u - jnp.round(u)
    t = u * u
    sine = poly(SIN, t) * u
    cosine = poly(COS, t)
    return 1.0 - sine * sine, sine * cosine


def factor_kernel(parts, chunk, first, column_ref, block_ref, *refs):
    before = refs[: 0 if first else parts]
    refs = refs[len(before) :]
    after, wave_ref, refs = refs[:parts], refs[parts], refs[parts + 1 :]
    weight_ref = refs[-1]
    if first:
        columns_out, block_out, sems = refs[0], refs[1], refs[2]
        copies = [
            pltpu.make_async_copy(column_ref, columns_out, sems.at[0]),
            pltpu.make_async_copy(block_ref, block_out, sems.at[1]),
        ]
        for copy in copies:
            copy.start()
        for copy in copies:
            copy.wait()
        column_ref, block_ref = columns_out, block_out
    cells, _, slots = block_ref.shape
    channels = after[0].shape[-1]
    span = cells * slots
    total = wave_ref.shape[0] // 2
    at_x = lax.axis_index("gx")
    for cell in range(cells):
        high, low = split(block_ref[cell, :channels, :])
        for at in (cell * slots, span + cell * slots):
            weight_ref[:channels, at : at + slots] = high
            weight_ref[channels:, at : at + slots] = low

    def some(j, carry):
        here = pl.multiple_of(j * chunk, chunk)
        wave_x = column_ref[pl.ds(here, chunk), 0:1]
        wave_y = column_ref[pl.ds(here, chunk), 1:2]
        wave_z = column_ref[pl.ds(here, chunk), 2:3]
        row = pl.multiple_of(j * 2 * chunk, 2 * chunk)
        for cell in range(cells):
            at = cell * slots
            frac = block_ref[cell, channels + 3 : channels + 6, :]
            u = wave_x * frac[0:1] + wave_y * frac[1:2] + wave_z * frac[2:3]
            cosine, sine = turns(u)
            high, low = split(cosine)
            wave_ref[pl.ds(row, chunk), at : at + slots] = high
            wave_ref[pl.ds(row, chunk), span + at : span + at + slots] = low
            high, low = split(sine)
            wave_ref[pl.ds(row + chunk, chunk), at : at + slots] = high
            wave_ref[pl.ds(row + chunk, chunk), span + at : span + at + slots] = low
        return carry

    lax.fori_loop(0, total // chunk, some, 0, unroll=total // chunk <= 8)
    half = 2 * total // parts
    for n in range(parts):
        row = pl.multiple_of(lax.rem(at_x + n, parts) * half, half)
        both = lax.dot_general(
            wave_ref[pl.ds(row, half), :], weight_ref[...], (((1,), (1,)), ((), ())),
            preferred_element_type=f32,
        )
        both = both[:, :channels] + both[:, channels:]
        after[n][...] = both if first else before[n][...] + both


def partial_factors(columns, chunk, block, before, parts):
    total = columns.shape[0]
    cells, rows, slots = block.shape
    channels = rows - 8
    span = cells * slots
    out = [jax.ShapeDtypeStruct((2 * total // parts, channels), f32)] * parts
    out.append(jax.ShapeDtypeStruct((2 * total, 2 * span), bf16))
    in_specs = [whole()] * (2 + len(before))
    scratch = [pltpu.VMEM((2 * channels, 2 * span), bf16)]
    if not before:
        in_specs = [pl.BlockSpec(memory_space=pltpu.HBM)] * 2
        out += [jax.ShapeDtypeStruct(columns.shape, f32), jax.ShapeDtypeStruct(block.shape, f32)]
        scratch = [pltpu.SemaphoreType.DMA((2,))] + scratch
    return pl.pallas_call(
        functools.partial(factor_kernel, parts, chunk, not before),
        in_specs=in_specs,
        out_specs=[whole()] * len(out),
        out_shape=out,
        input_output_aliases={2 + n: n for n in range(len(before))},
        scratch_shapes=scratch,
        compiler_params=params(),
        cost_estimate=pl.CostEstimate(
            flops=8 * total * span * channels, bytes_accessed=8 * total * span, transcendentals=0
        ),
        name="factors",
    )(columns, block, *before)


def filter_kernel(scale, block_ref, *refs):
    parts, (weight_ref, table_ref, out_ref) = refs[:-3], refs[-3:]
    summed = parts[0][...]
    for part in parts[1:]:
        summed = summed + part[...]
    projected = jnp.dot(summed, weight_ref[...], precision=HIGH, preferred_element_type=f32)
    table = table_ref[...] * scale
    for n in range(0, summed.shape[0], table.shape[0]):
        out_ref[n : n + table.shape[0], :] = projected[n : n + table.shape[0]] * table


def filtered_piece(scale, block, chunk, parts, w_charge, table):
    rows, channels = parts[0].shape
    fixed = pl.BlockSpec((rows, channels), lambda i, block: (0, 0))
    return pl.pallas_call(
        functools.partial(filter_kernel, scale),
        grid_spec=pltpu.PrefetchScalarGridSpec(
            num_scalar_prefetch=1,
            grid=(1,),
            in_specs=[fixed] * len(parts)
            + [
                pl.BlockSpec(w_charge.shape, lambda i, block: (0, 0)),
                pl.BlockSpec((chunk, channels), lambda i, block: (block[0], 0)),
            ],
            out_specs=fixed,
        ),
        out_shape=jax.ShapeDtypeStruct((rows, channels), f32),
        compiler_params=params(),
        name="filter",
    )(block, *parts, w_charge, table)


def potential_kernel(groups, pieces, blocks, *refs):
    held = refs[:groups]
    waves = refs[groups : groups + blocks]
    outs = refs[groups + blocks : -2]
    ordered_ref, turned_ref = refs[-2:]
    channels = ordered_ref.shape[-1]
    piece = held[0].shape[0] // pieces
    for group in range(groups):
        for n in range(pieces):
            rank_x = partner(lax.axis_index("gx"), group, groups)
            rank_z = partner(lax.axis_index("gz"), n, pieces)
            at = pl.multiple_of((rank_x * pieces + rank_z) * piece, piece)
            ordered_ref[pl.ds(at, piece), :] = held[group][n * piece : (n + 1) * piece, :]
    high, low = split(ordered_ref[...].T)
    turned_ref[:channels, :] = high
    turned_ref[channels:, :] = low
    for wave_ref, out in zip(waves, outs):
        cells, _, slots = out.shape
        span = cells * slots
        both = jnp.dot(turned_ref[...], wave_ref[:, :span], preferred_element_type=f32)
        third = jnp.dot(turned_ref[:channels, :], wave_ref[:, span:], preferred_element_type=f32)
        potential = both[:channels] + both[channels:] + third
        for cell in range(cells):
            out[cell] = potential[:, cell * slots : (cell + 1) * slots]


def potentials_of(held, pieces, waves, cells, slots):
    rows = waves[0].shape[0]
    channels = held[0].shape[-1]
    return pl.pallas_call(
        functools.partial(potential_kernel, len(held), pieces, len(waves)),
        in_specs=[whole()] * (len(held) + len(waves)),
        out_specs=[whole()] * len(waves),
        scratch_shapes=[
            pltpu.VMEM((rows, channels), f32),
            pltpu.VMEM((2 * channels, rows), bf16),
        ],
        out_shape=[jax.ShapeDtypeStruct((cells, channels, slots), f32)] * len(waves),
        compiler_params=params(),
        cost_estimate=pl.CostEstimate(
            flops=6 * rows * len(waves) * cells * slots * channels,
            bytes_accessed=4 * rows * len(waves) * cells * slots, transcendentals=0,
        ),
        name="potentials",
    )(*held, *waves)


def message_kernel(
    basis, sources, table, last, first, own_source, step_ref, mix_ref, value_ref, *refs
):
    blocks, refs = refs[:sources], refs[sources:]
    own_ref = blocks[own_source]
    if last:
        before, refs = refs[:last], refs[last:]
        out_ref, cell_ref, at_ref, own_col_ref, acc_ref, mixed_ref, wide_ref = refs[:7]
    else:
        out_ref, cell_ref, at_ref, own_col_ref, acc_ref = refs[:5]
    left_0, left_1, left_2, right_0, right_1, right_2 = refs[-6:]
    count = step_ref.shape[1]
    cells = acc_ref.shape[0]
    slots = own_ref.shape[-1]
    along, planes = len(table[0]), len(table[0][0])
    channels = value_ref.shape[0]
    lefts, rights = (left_0, left_1, left_2), (right_0, right_1, right_2)

    for x, columns in enumerate(table):
        for y, column in enumerate(columns):
            for z, choices in enumerate(column):
                n = (x * along + y) * planes + z
                (_, source, index), others = choices[0], choices[1:]
                block = blocks[source][index]
                for condition, source, index in others:
                    block = jnp.where(condition(), blocks[source][index], block)
                high, low = split(block[:channels])
                cell_ref[n, :channels, :] = high
                cell_ref[n, channels:, :] = low
                at_ref[n] = block[channels:]
    for b in range(basis) if last else ():
        high, low = split(value_ref[...] * (mix_ref[b : b + 1, :] * math.exp(-b * b)))
        mixed_ref[b * channels : (b + 1) * channels, :channels] = high
        mixed_ref[b * channels : (b + 1) * channels, channels:] = low
    for cell in range(cells):
        columns = own_ref[first + cell, channels : channels + 8, :].T
        for axis in range(3):
            own_col_ref[cell, axis] = jnp.broadcast_to(columns[:, axis : axis + 1], (slots, slots))

    def fill(step, move):
        place_x = step_ref[0, step] + 1 + (move - 1)
        place_y = step_ref[1, step]
        plane = step_ref[2, step]
        if last:
            plane = jnp.where(is_even("gz"), plane, 1 - plane)
        shift_z = step_ref[3, step].astype(f32)
        left, right = lefts[move], rights[move]
        own = step_ref[4, step]
        near = []
        for n in range(3):
            number = (place_x * along + place_y + n) * planes + plane
            cell = cell_ref[number]
            right[:, n * slots : (n + 1) * slots] = cell
            right[:, (3 + n) * slots : (4 + n) * slots] = cell
            at = at_ref[number]
            near.append((at[0:1] + float(move - 1), at[1:2] + float(n - 1), at[2:3] + shift_z))
        tile = 16
        for m in range(slots // tile):
            at = m * tile
            own_x = own_col_ref[own, 0, at : at + tile, :]
            own_y = own_col_ref[own, 1, at : at + tile, :]
            own_z = own_col_ref[own, 2, at : at + tile, :]
            for n in range(3):
                dx = near[n][0] - own_x
                dy = near[n][1] - own_y
                dz = near[n][2] - own_z
                squared = dx * dx + dy * dy + dz * dz
                distance = squared * lax.rsqrt(jnp.maximum(squared, 1e-30))
                envelope = jnp.maximum(1.0 - squared, 0.0)
                term = envelope * envelope * jnp.exp2(squared * (-float((basis - 1) ** 2) * LOG2E))
                ratio = jnp.exp2(distance * (2.0 * (basis - 1) * LOG2E))
                if not last and move == 1 and n == 1:
                    i = lax.broadcasted_iota(jnp.int32, (tile, slots), 0) + at
                    j = lax.broadcasted_iota(jnp.int32, (tile, slots), 1)
                    same = jnp.logical_and(i == j, step_ref[3, step] == 0)
                    term = jnp.where(same, 0.0, term)
                for b in range(basis):
                    if b > 0:
                        term = term * ratio
                    high, low = split(term)
                    row = b * slots + at
                    left[row : row + tile, n * slots : (n + 1) * slots] = high
                    left[row : row + tile, (3 + n) * slots : (4 + n) * slots] = low

    def product(move):
        return lax.dot_general(
            lefts[move][...], rights[move][...], (((1,), (1,)), ((), ())), preferred_element_type=f32
        )

    fill(0, 0)

    def visit(step, carry):
        own = step_ref[4, step]
        fresh = step_ref[5, step] == 1
        acc_ref[own] = jnp.where(fresh, 0.0, acc_ref[own]) + product(0)
        fill(step, 1)
        acc_ref[own] += product(1)
        fill(step, 2)
        acc_ref[own] += product(2)
        fill(jnp.minimum(step + 1, count - 1), 0)
        return carry

    lax.fori_loop(0, count, visit, 0)
    wide = basis * channels
    for cell in range(cells):
        gathered = acc_ref[cell, :, :channels] + acc_ref[cell, :, channels:]
        if not last:
            out_ref[cell] = gathered
            continue
        per = cells // last
        high, low = split(gathered + before[cell // per][cell % per])
        here = slice(cell * slots, (cell + 1) * slots)
        for b in range(basis):
            wide_ref[here, b * channels : (b + 1) * channels] = high[b * slots : (b + 1) * slots]
            wide_ref[here, wide + b * channels : wide + (b + 1) * channels] = low[b * slots : (b + 1) * slots]
    if last:
        both = jnp.dot(wide_ref[:, :wide], mixed_ref[...], preferred_element_type=f32)
        both = both + jnp.dot(wide_ref[:, wide:], mixed_ref[...], preferred_element_type=f32)
        for cell in range(cells):
            part = both[cell * slots : (cell + 1) * slots]
            out_ref[cell] = (part[:, :channels] + part[:, channels:]).T


def pair_messages(steps, own, blocks, table, mix, w_value, cells, first, before=()):
    slots = blocks[own].shape[-1]
    basis, channels = mix.shape
    around = len(table) * len(table[0]) * len(table[0][0])
    count = steps.shape[1]
    last = len(before)
    sums = (cells, basis * slots, channels)
    closing = [
        pltpu.VMEM((basis * channels, 2 * channels), bf16),
        pltpu.VMEM((cells * slots, 2 * basis * channels), bf16),
    ]
    return pl.pallas_call(
        functools.partial(message_kernel, basis, len(blocks), table, last, first, own),
        in_specs=[pl.BlockSpec(memory_space=pltpu.SMEM)] + [whole()] * (2 + len(blocks) + last),
        out_specs=whole(),
        scratch_shapes=[
            pltpu.VMEM((around, 2 * channels, slots), bf16),
            pltpu.VMEM((around, 8, slots), f32),
            pltpu.VMEM((cells, 3, slots, slots), f32),
            pltpu.VMEM((cells, basis * slots, 2 * channels), f32),
        ]
        + closing * bool(last)
        + [pltpu.VMEM((basis * slots, 6 * slots), bf16)] * 3
        + [pltpu.VMEM((2 * channels, 6 * slots), bf16)] * 3,
        out_shape=jax.ShapeDtypeStruct((cells, channels, slots) if last else sums, f32),
        compiler_params=params(),
        cost_estimate=pl.CostEstimate(
            flops=count * 8 * basis * slots * 9 * slots * channels, bytes_accessed=1 << 20,
            transcendentals=0,
        ),
        name="messages",
    )(steps, mix, w_value, *blocks, *before)


def visits(cells_x, cells_y, cells_z, inside, first=0, end=None):
    table = []
    for x in range(cells_x):
        for y in range(cells_y):
            for z in range(cells_z):
                own = (x * cells_y + y) * cells_z + z
                if not first <= own < (cells_x * cells_y * cells_z if end is None else end):
                    continue
                for shift in (-1, 0, 1):
                    plane = z + shift
                    if (0 <= plane < cells_z) != inside:
                        continue
                    if not inside:
                        plane = 0 if shift > 0 else 1
                    table.append([x - first // (cells_y * cells_z), y, plane, shift, own - first, 1, 1])
    for one, after in zip(table, table[1:]):
        if one[4] == after[4]:
            one[6] = after[5] = 0
    return np.array(table, np.int32).T.copy()


def mlp_kernel(count, shape, *refs):
    counts_ref, feature_ref = refs[:2]
    message_ref = refs[2]
    potentials = refs[3 : 3 + count]
    hidden_ref, back_ref, out_ref = refs[3 + count :]
    cells, channels, slots = feature_ref.shape
    columns = []
    for cell in range(cells):
        mixed = feature_ref[cell] + message_scale * message_ref[cell]
        for potential in potentials:
            mixed = mixed + potential[cell]
        columns.append(mixed)
    mixed = jnp.concatenate(columns, axis=1)
    inner = lax.dot_general(
        hidden_ref[...], mixed, (((0,), (0,)), ((), ())), precision=HIGH, preferred_element_type=f32
    )
    hidden = inner * jax.nn.sigmoid(inner)
    updated = mixed + lax.dot_general(
        back_ref[...], hidden, (((0,), (0,)), ((), ())), precision=HIGH, preferred_element_type=f32
    )
    slot = lax.broadcasted_iota(jnp.int32, (channels, slots), 1)
    for cell in range(cells):
        part = updated[:, cell * slots : (cell + 1) * slots]
        x, y, z = place_of(cell, shape)
        out_ref[cell] = jnp.where(slot < counts_ref[x, z, y], part, 0.0)


def atom_mlp(shape, counts, features, messages, potentials, w_hidden, w_out):
    return pl.pallas_call(
        functools.partial(mlp_kernel, len(potentials), shape),
        in_specs=[pl.BlockSpec(memory_space=pltpu.SMEM)]
        + [whole()] * (4 + len(potentials)),
        out_specs=whole(),
        out_shape=jax.ShapeDtypeStruct(features.shape, f32),
        compiler_params=params(),
        name="atom_mlp",
    )(counts, features, messages, *potentials, w_hidden, w_out)


def next_in_x(block, shape):
    size = lax.axis_size("gx")
    if size == 2:
        other = exchange(block, "gx", 1)
        return (other, shape[0] - 1), (other, 0)
    wide = block.reshape(shape + block.shape[1:])
    below, above = below_above(wide[:1], wide[-1:], "gx")
    return tuple((side.reshape((-1,) + block.shape[1:]), 0) for side in (below, above))


class Sources:
    def __init__(self):
        self.arrays = []

    def add(self, array):
        for n, held in enumerate(self.arrays):
            if held is array:
                return n
        self.arrays.append(array)
        return len(self.arrays) - 1

    def columns(self, block, shape):
        below, above = next_in_x(block, shape)
        inside = [(self.add(block), x) for x in range(shape[0])]
        return [(self.add(below[0]), below[1])] + inside + [(self.add(above[0]), above[1])]


def always():
    return True


def shards(
    features, positions, counts, waves, filter_table, w_value, w_charge, radial_mix, w_hidden, w_out
):
    shape = cells_x, cells_y, cells_z = features.shape[:3]
    channels, slots = features.shape[3:]
    total_waves = waves.shape[1]
    size_x, size_y, size_z = (lax.axis_size(a) for a in ("gx", "gy", "gz"))
    at_x, at_y, at_z = (lax.axis_index(a) for a in ("gx", "gy", "gz"))
    grid = (cells_x * size_x, cells_y * size_y, cells_z * size_z)
    cells = cells_x * cells_y * cells_z
    some_counts = jnp.transpose(counts, (0, 2, 1))
    flat_features = features.reshape(cells, channels, slots)

    share = total_waves // size_y
    own, columns = pack(
        shape, grid, some_counts, flat_features, positions.reshape(cells * 3, 1, slots), waves, share
    )
    rows = own.shape[1]
    packed = own.reshape(shape + (rows, slots))

    gathered = [own] + [exchange(own, "gy", s) for s in range(1, size_y)]
    if cells_z == 1:
        sides = neighbours(own, own, "gz", same=True)
    else:
        flat = (cells_x * cells_y, rows, slots)
        sides = neighbours(packed[:, :, 0].reshape(flat), packed[:, :, -1].reshape(flat), "gz")

    half = 2 * share // size_x
    piece = half // size_z
    chunk = min(piece, share // size_x)
    *parts, table, columns, own = partial_factors(columns, chunk, own, (), size_x)
    gathered[0] = own
    tables = [table]
    for block in gathered[1:]:
        *parts, table = partial_factors(columns, chunk, block, parts, size_x)
        tables.append(table)

    summed = parts[0]
    for s in range(1, size_x):
        other = partner(at_x, s, size_x)
        to = parts[1]
        for n in range(2, size_x):
            to = jnp.where(lax.rem(other - at_x + size_x, size_x) == n, parts[n], to)
        summed = summed + exchange(to, "gx", s)
    value_near, summed = lax.optimization_barrier((w_value, summed))
    pieces = [lax.dynamic_slice_in_dim(summed, at_z * piece, piece, 0)]
    for s in range(1, size_z):
        other = partner(at_z, s, size_z)
        pieces.append(exchange(lax.dynamic_slice_in_dim(summed, other * piece, piece, 0), "gz", s))

    sources = Sources()

    def reaches(step, rank):
        return any(partner(i, step, size_y) == (i + rank) % size_y for i in range(size_y))

    columns = {
        step: sources.columns(block, shape)
        for step, block in enumerate(gathered)
        if any(reaches(step, rank) for rank in (-1, 0, 1))
    }

    def at_rank(step, rank):
        def condition():
            at = lax.axis_index("gy")
            return partner(at, step, size_y) == (at + rank) % size_y

        return condition

    def choices(x, y, z):
        rank = -1 if y < 0 else 1 if y == cells_y else 0
        y = y % cells_y
        found = []
        for step in columns:
            if reaches(step, rank):
                source, from_x = columns[step][x + 1]
                found.append((at_rank(step, rank), source, (from_x * cells_y + y) * cells_z + z))
        return found

    table = [
        [[choices(x, y, z) for z in range(cells_z)] for y in range(-1, cells_y + 1)]
        for x in range(-1, cells_x + 1)
    ]
    layer = cells_y * cells_z
    at_once = (cells_x + 1) // 2
    near = []

    def near_messages(begin, value):
        end = min(begin + at_once, cells_x)
        inner = visits(cells_x, cells_y, cells_z, True, begin * layer, end * layer)
        return pair_messages(
            jnp.asarray(inner), sources.add(own), sources.arrays, table[begin : end + 2], radial_mix, value,
            (end - begin) * layer, begin * layer,
        )

    near.append(near_messages(0, value_near))

    scale = 1.0 / math.sqrt(grid[0] * grid[1] * grid[2] * slots) / math.sqrt(total_waves)
    rank = at_x * size_z + at_z
    block = at_y * (share // chunk) + (rank * piece) // (2 * chunk)
    charge, near[0], *sides = lax.optimization_barrier((w_charge, near[0], *sides))
    filtered = filtered_piece(scale, block.reshape(1), chunk, pieces, charge, filter_table)

    low, high = (
        jnp.concatenate(
            [side[n : n + 1] for n in range(y, cells_x * cells_y, cells_y) for side in sides], axis=0
        )
        for y in (0, cells_y - 1)
    )
    value_near, filtered, low, high = lax.optimization_barrier((w_value, filtered, low, high))
    edges = neighbours(low, high, "gy")
    if cells_x > 1:
        near.append(near_messages(at_once, value_near))
    held_z = jnp.concatenate(
        [filtered] + [exchange(filtered, "gz", s) for s in range(1, size_z)], axis=0
    )
    held_z, *near = lax.optimization_barrier((held_z, *near))
    held = [held_z] + [exchange(held_z, "gx", s) for s in range(1, size_x)]

    found = potentials_of(held, held_z.shape[0] // piece, tables, cells, slots)
    value_far, first, second, *found = lax.optimization_barrier((w_value, *edges, *found))
    edges = first, second

    sources = Sources()
    flat = (cells_x, cells_y, 1)
    side_columns = [sources.columns(side, flat) for side in sides]
    edge_columns = [sources.columns(edge, (cells_x, 1, 2)) for edge in edges]

    def choices(x, y, z):
        if 0 <= y < cells_y:
            source, from_x = side_columns[z][x + 1]
            return [(always, source, from_x * cells_y + y)]
        found = []
        for n, columns in enumerate(edge_columns):
            source, from_x = columns[x + 1]
            first_is_here = y == cells_y
            condition = (lambda: is_even("gy")) if (n == 0) == first_is_here else (
                lambda: jnp.logical_not(is_even("gy"))
            )
            found.append((condition, source, from_x * 2 + z))
        return found

    table = [
        [[choices(x, y, z) for z in range(2)] for y in range(-1, cells_y + 1)]
        for x in range(-1, cells_x + 1)
    ]
    returned = [found[0]] + [exchange(found[s], "gy", s) for s in range(1, size_y)]
    outer = jnp.asarray(visits(cells_x, cells_y, cells_z, False))
    messages = pair_messages(
        outer, sources.add(own), sources.arrays, table, radial_mix, value_far, cells, 0, near
    )

    updated = atom_mlp(
        shape, some_counts, flat_features, messages, returned, w_hidden, w_out
    )
    return updated.reshape(features.shape)


def solution(mesh):
    placed = (
        P("gx", "gy", "gz", None, None),
        P("gx", "gy", "gz", None, None),
        P("gx", "gy", "gz"),
        P(),
        P(),
        P(),
        P(),
        P(),
        P(),
        P(),
    )
    return jax.shard_map(
        shards,
        mesh=mesh,
        in_specs=placed,
        out_specs=P("gx", "gy", "gz", None, None),
        check_vma=False,
    )
```

```python
import functools
import math

import numpy as np

import jax
import jax.numpy as jnp
from jax import lax
from jax.experimental import pallas as pl
from jax.experimental.pallas import tpu as pltpu
from jax.sharding import PartitionSpec as P


HIGH = lax.Precision.HIGH
message_scale = 0.125
bf16 = jnp.bfloat16
f32 = jnp.float32
VMEM_LIMIT = 28 * 1024 * 1024
PACK_LIMIT = 62 * 1024 * 1024


LOG2E = math.log2(math.e)


def partner(i, step, count):
    return i ^ step


def exchange(block, axis, step):
    count = lax.axis_size(axis)
    pairs = [(i, partner(i, step, count)) for i in range(count)]
    return lax.ppermute(block, axis, pairs)


def is_even(axis):
    if lax.axis_size(axis) % 2:
        return jnp.bool_(True)
    return lax.rem(lax.axis_index(axis), 2) == 0


def neighbours(low, high, axis, same=False):
    count = lax.axis_size(axis)
    if count == 1:
        return low, high
    if count % 2:
        up = lax.ppermute(low, axis, [(i, (i - 1) % count) for i in range(count)])
        down = lax.ppermute(high, axis, [(i, (i + 1) % count) for i in range(count)])
        return up, down
    even = is_even(axis)
    first = high if same else jnp.where(even, high, low)
    second = low if same else jnp.where(even, low, high)
    one = [(i, i ^ 1) for i in range(count)]
    two = [(i, (i + 1 if i % 2 else i - 1) % count) for i in range(count)]
    return lax.ppermute(first, axis, one), lax.ppermute(second, axis, two)


def below_above(low, high, axis):
    first, second = neighbours(low, high, axis)
    even = is_even(axis)
    return jnp.where(even, second, first), jnp.where(even, first, second)


def split(x):
    high = x.astype(bf16)
    low = (x - high.astype(f32)).astype(bf16)
    return high, low


def whole():
    return pl.BlockSpec(memory_space=pltpu.VMEM)


def params(limit=VMEM_LIMIT):
    return pltpu.CompilerParams(vmem_limit_bytes=limit)


def place_of(cell, shape):
    return cell // (shape[1] * shape[2]), cell // shape[2] % shape[1], cell % shape[2]


def pack_kernel(
    shape, grid, counts_hbm, feature_hbm, position_hbm, out_ref,
    counts_ref, feature_ref, position_ref, sems,
):
    cells, channels, slots = feature_ref.shape
    copies = [
        pltpu.make_async_copy(counts_hbm, counts_ref, sems.at[0]),
        pltpu.make_async_copy(position_hbm, position_ref, sems.at[1]),
        pltpu.make_async_copy(feature_hbm, feature_ref, sems.at[2]),
    ]
    for copy in copies:
        copy.start()
    for copy in copies:
        copy.wait()
    slot = lax.broadcasted_iota(jnp.int32, (channels, slots), 1)
    for cell in range(cells):
        place = place_of(cell, shape)
        held = slot < counts_ref[place[0], place[2], place[1]]
        out_ref[cell, :channels, :] = jnp.where(held, feature_ref[cell], 0.0)
        at = [position_ref[3 * cell + axis] for axis in range(3)]
        rows = list(at)
        for axis, name in enumerate(("gx", "gy", "gz")):
            here = lax.axis_index(name) * shape[axis] + place[axis]
            rows.append((at[axis] + here.astype(f32)) * (1.0 / grid[axis]))
        out_ref[cell, channels:, :] = jnp.concatenate(rows + [jnp.zeros((2, slots), f32)], axis=0)


def pack(shape, grid, counts, features, positions):
    cells, channels, slots = features.shape
    return pl.pallas_call(
        functools.partial(pack_kernel, shape, grid),
        in_specs=[pl.BlockSpec(memory_space=pltpu.HBM)] * 3,
        out_specs=whole(),
        out_shape=jax.ShapeDtypeStruct((cells, channels + 8, slots), f32),
        scratch_shapes=[
            pltpu.SMEM(counts.shape, jnp.int32),
            pltpu.VMEM(features.shape, f32),
            pltpu.VMEM(positions.shape, f32),
            pltpu.SemaphoreType.DMA((3,)),
        ],
        compiler_params=params(),
        name="pack",
    )(counts, features, positions)


def fitted(function, terms):
    t = 0.125 * (1.0 + np.cos(np.pi * (np.arange(terms) + 0.5) / terms))
    solved = np.linalg.solve(np.vander(t, terms, increasing=True), function(np.sqrt(t)))
    return [float(c) for c in solved]


SIN = fitted(lambda u: math.sqrt(2.0) * np.sin(np.pi * u) / u, 5)
COS = fitted(lambda u: math.sqrt(2.0) * np.cos(np.pi * u), 5)


def poly(coefficients, t):
    acc = t * coefficients[-1] + coefficients[-2]
    for c in coefficients[-3::-1]:
        acc = acc * t + c
    return acc


def turns(u):
    u = u - jnp.round(u)
    t = u * u
    sine = poly(SIN, t) * u
    cosine = poly(COS, t)
    return 1.0 - sine * sine, sine * cosine


def factor_kernel(parts, chunk, first, column_ref, block_ref, *refs):
    before = refs[: 0 if first else parts]
    refs = refs[len(before) :]
    after, wave_ref, refs = refs[:parts], refs[parts], refs[parts + 1 :]
    weight_ref = refs[-1]
    cells, _, slots = block_ref.shape
    channels = after[0].shape[-1]
    span = cells * slots
    total = wave_ref.shape[0] // 2
    at_x = lax.axis_index("gx")
    if first:
        begin = pl.multiple_of(lax.axis_index("gy") * total, total)
        rows = column_ref[:, pl.ds(begin, total)].astype(f32)
        column_ref = refs[0]
        column_ref[...] = jnp.concatenate([rows, jnp.zeros((5, total), f32)], axis=0).T
    for cell in range(cells):
        high, low = split(block_ref[cell, :channels, :])
        for at in (cell * slots, span + cell * slots):
            weight_ref[:channels, at : at + slots] = high
            weight_ref[channels:, at : at + slots] = low

    def some(j, carry):
        here = pl.multiple_of(j * chunk, chunk)
        wave_x = column_ref[pl.ds(here, chunk), 0:1]
        wave_y = column_ref[pl.ds(here, chunk), 1:2]
        wave_z = column_ref[pl.ds(here, chunk), 2:3]
        row = pl.multiple_of(j * 2 * chunk, 2 * chunk)
        for cell in range(cells):
            at = cell * slots
            frac = block_ref[cell, channels + 3 : channels + 6, :]
            u = wave_x * frac[0:1] + wave_y * frac[1:2] + wave_z * frac[2:3]
            cosine, sine = turns(u)
            high, low = split(cosine)
            wave_ref[pl.ds(row, chunk), at : at + slots] = high
            wave_ref[pl.ds(row, chunk), span + at : span + at + slots] = low
            high, low = split(sine)
            wave_ref[pl.ds(row + chunk, chunk), at : at + slots] = high
            wave_ref[pl.ds(row + chunk, chunk), span + at : span + at + slots] = low
        return carry

    lax.fori_loop(0, total // chunk, some, 0, unroll=total // chunk <= 8)
    half = 2 * total // parts
    for n in range(parts):
        row = pl.multiple_of(lax.rem(at_x + n, parts) * half, half)
        both = lax.dot_general(
            wave_ref[pl.ds(row, half), :], weight_ref[...], (((1,), (1,)), ((), ())),
            preferred_element_type=f32,
        )
        both = both[:, :channels] + both[:, channels:]
        after[n][...] = both if first else before[n][...] + both


def partial_factors(columns, total, chunk, block, before, parts):
    cells, rows, slots = block.shape
    channels = rows - 8
    span = cells * slots
    out = [jax.ShapeDtypeStruct((2 * total // parts, channels), f32)] * parts
    out.append(jax.ShapeDtypeStruct((2 * total, 2 * span), bf16))
    if not before:
        out.append(jax.ShapeDtypeStruct((total, 8), f32))
    return pl.pallas_call(
        functools.partial(factor_kernel, parts, chunk, not before),
        in_specs=[whole()] * (2 + len(before)),
        out_specs=[whole()] * len(out),
        out_shape=out,
        input_output_aliases={2 + n: n for n in range(len(before))},
        scratch_shapes=[pltpu.VMEM((2 * channels, 2 * span), bf16)],
        compiler_params=params(),
        cost_estimate=pl.CostEstimate(
            flops=8 * total * span * channels, bytes_accessed=8 * total * span, transcendentals=0
        ),
        name="factors",
    )(columns, block, *before)


def filter_kernel(scale, block_ref, *refs):
    parts, (weight_ref, table_ref, out_ref) = refs[:-3], refs[-3:]
    summed = parts[0][...]
    for part in parts[1:]:
        summed = summed + part[...]
    projected = jnp.dot(summed, weight_ref[...], precision=HIGH, preferred_element_type=f32)
    table = table_ref[...] * scale
    for n in range(0, summed.shape[0], table.shape[0]):
        out_ref[n : n + table.shape[0], :] = projected[n : n + table.shape[0]] * table


def filtered_piece(scale, block, chunk, parts, w_charge, table):
    rows, channels = parts[0].shape
    fixed = pl.BlockSpec((rows, channels), lambda i, block: (0, 0))
    return pl.pallas_call(
        functools.partial(filter_kernel, scale),
        grid_spec=pltpu.PrefetchScalarGridSpec(
            num_scalar_prefetch=1,
            grid=(1,),
            in_specs=[fixed] * len(parts)
            + [
                pl.BlockSpec(w_charge.shape, lambda i, block: (0, 0)),
                pl.BlockSpec((chunk, channels), lambda i, block: (block[0], 0)),
            ],
            out_specs=fixed,
        ),
        out_shape=jax.ShapeDtypeStruct((rows, channels), f32),
        compiler_params=params(),
        name="filter",
    )(block, *parts, w_charge, table)


def potential_kernel(groups, pieces, blocks, *refs):
    held = refs[:groups]
    waves = refs[groups : groups + blocks]
    outs = refs[groups + blocks : -2]
    ordered_ref, turned_ref = refs[-2:]
    channels = ordered_ref.shape[-1]
    piece = held[0].shape[0] // pieces
    for group in range(groups):
        for n in range(pieces):
            rank_x = partner(lax.axis_index("gx"), group, groups)
            rank_z = partner(lax.axis_index("gz"), n, pieces)
            at = pl.multiple_of((rank_x * pieces + rank_z) * piece, piece)
            ordered_ref[pl.ds(at, piece), :] = held[group][n * piece : (n + 1) * piece, :]
    high, low = split(ordered_ref[...].T)
    turned_ref[:channels, :] = high
    turned_ref[channels:, :] = low
    for wave_ref, out in zip(waves, outs):
        cells, _, slots = out.shape
        span = cells * slots
        both = jnp.dot(turned_ref[...], wave_ref[:, :span], preferred_element_type=f32)
        third = jnp.dot(turned_ref[:channels, :], wave_ref[:, span:], preferred_element_type=f32)
        potential = both[:channels] + both[channels:] + third
        for cell in range(cells):
            out[cell] = potential[:, cell * slots : (cell + 1) * slots]


def potentials_of(held, pieces, waves, cells, slots):
    rows = waves[0].shape[0]
    channels = held[0].shape[-1]
    return pl.pallas_call(
        functools.partial(potential_kernel, len(held), pieces, len(waves)),
        in_specs=[whole()] * (len(held) + len(waves)),
        out_specs=[whole()] * len(waves),
        scratch_shapes=[
            pltpu.VMEM((rows, channels), f32),
            pltpu.VMEM((2 * channels, rows), bf16),
        ],
        out_shape=[jax.ShapeDtypeStruct((cells, channels, slots), f32)] * len(waves),
        compiler_params=params(),
        cost_estimate=pl.CostEstimate(
            flops=6 * rows * len(waves) * cells * slots * channels,
            bytes_accessed=4 * rows * len(waves) * cells * slots, transcendentals=0,
        ),
        name="potentials",
    )(*held, *waves)


def message_kernel(
    basis, sources, table, last, first, own_source, step_ref, mix_ref, value_ref, *refs
):
    blocks, refs = refs[:sources], refs[sources:]
    own_ref = blocks[own_source]
    if last:
        before, refs = refs[:last], refs[last:]
        out_ref, cell_ref, at_ref, own_col_ref, acc_ref, mixed_ref, wide_ref = refs[:7]
    else:
        out_ref, cell_ref, at_ref, own_col_ref, acc_ref = refs[:5]
    left_0, left_1, left_2, right_0, right_1, right_2 = refs[-6:]
    count = step_ref.shape[1]
    cells = acc_ref.shape[0]
    slots = own_ref.shape[-1]
    along, planes = len(table[0]), len(table[0][0])
    channels = value_ref.shape[0]
    lefts, rights = (left_0, left_1, left_2), (right_0, right_1, right_2)

    for x, columns in enumerate(table):
        for y, column in enumerate(columns):
            for z, choices in enumerate(column):
                n = (x * along + y) * planes + z
                (_, source, index), others = choices[0], choices[1:]
                block = blocks[source][index]
                for condition, source, index in others:
                    block = jnp.where(condition(), blocks[source][index], block)
                high, low = split(block[:channels])
                cell_ref[n, :channels, :] = high
                cell_ref[n, channels:, :] = low
                at_ref[n] = block[channels:]
    for b in range(basis) if last else ():
        high, low = split(value_ref[...] * (mix_ref[b : b + 1, :] * math.exp(-b * b)))
        mixed_ref[b * channels : (b + 1) * channels, :channels] = high
        mixed_ref[b * channels : (b + 1) * channels, channels:] = low
    for cell in range(cells):
        columns = own_ref[first + cell, channels : channels + 8, :].T
        for axis in range(3):
            own_col_ref[cell, axis] = jnp.broadcast_to(columns[:, axis : axis + 1], (slots, slots))

    def fill(step, move):
        place_x = step_ref[0, step] + 1 + (move - 1)
        place_y = step_ref[1, step]
        plane = step_ref[2, step]
        if last:
            plane = jnp.where(is_even("gz"), plane, 1 - plane)
        shift_z = step_ref[3, step].astype(f32)
        left, right = lefts[move], rights[move]
        own = step_ref[4, step]
        near = []
        for n in range(3):
            number = (place_x * along + place_y + n) * planes + plane
            cell = cell_ref[number]
            right[:, n * slots : (n + 1) * slots] = cell
            right[:, (3 + n) * slots : (4 + n) * slots] = cell
            at = at_ref[number]
            near.append((at[0:1] + float(move - 1), at[1:2] + float(n - 1), at[2:3] + shift_z))
        tile = 16
        for m in range(slots // tile):
            at = m * tile
            own_x = own_col_ref[own, 0, at : at + tile, :]
            own_y = own_col_ref[own, 1, at : at + tile, :]
            own_z = own_col_ref[own, 2, at : at + tile, :]
            for n in range(3):
                dx = near[n][0] - own_x
                dy = near[n][1] - own_y
                dz = near[n][2] - own_z
                squared = dx * dx + dy * dy + dz * dz
                distance = squared * lax.rsqrt(jnp.maximum(squared, 1e-30))
                envelope = jnp.maximum(1.0 - squared, 0.0)
                term = envelope * envelope * jnp.exp2(squared * (-float((basis - 1) ** 2) * LOG2E))
                ratio = jnp.exp2(distance * (2.0 * (basis - 1) * LOG2E))
                if not last and move == 1 and n == 1:
                    i = lax.broadcasted_iota(jnp.int32, (tile, slots), 0) + at
                    j = lax.broadcasted_iota(jnp.int32, (tile, slots), 1)
                    same = jnp.logical_and(i == j, step_ref[3, step] == 0)
                    term = jnp.where(same, 0.0, term)
                for b in range(basis):
                    if b > 0:
                        term = term * ratio
                    high, low = split(term)
                    row = b * slots + at
                    left[row : row + tile, n * slots : (n + 1) * slots] = high
                    left[row : row + tile, (3 + n) * slots : (4 + n) * slots] = low

    def product(move):
        return lax.dot_general(
            lefts[move][...], rights[move][...], (((1,), (1,)), ((), ())), preferred_element_type=f32
        )

    fill(0, 0)

    def visit(step, carry):
        own = step_ref[4, step]
        fresh = step_ref[5, step] == 1
        acc_ref[own] = jnp.where(fresh, 0.0, acc_ref[own]) + product(0)
        fill(step, 1)
        acc_ref[own] += product(1)
        fill(step, 2)
        acc_ref[own] += product(2)
        fill(jnp.minimum(step + 1, count - 1), 0)
        return carry

    lax.fori_loop(0, count, visit, 0)
    wide = basis * channels
    for cell in range(cells):
        gathered = acc_ref[cell, :, :channels] + acc_ref[cell, :, channels:]
        if not last:
            out_ref[cell] = gathered
            continue
        per = cells // last
        high, low = split(gathered + before[cell // per][cell % per])
        here = slice(cell * slots, (cell + 1) * slots)
        for b in range(basis):
            wide_ref[here, b * channels : (b + 1) * channels] = high[b * slots : (b + 1) * slots]
            wide_ref[here, wide + b * channels : wide + (b + 1) * channels] = low[b * slots : (b + 1) * slots]
    if last:
        both = jnp.dot(wide_ref[:, :wide], mixed_ref[...], preferred_element_type=f32)
        both = both + jnp.dot(wide_ref[:, wide:], mixed_ref[...], preferred_element_type=f32)
        for cell in range(cells):
            part = both[cell * slots : (cell + 1) * slots]
            out_ref[cell] = (part[:, :channels] + part[:, channels:]).T


def pair_messages(steps, own, blocks, table, mix, w_value, cells, first, before=()):
    slots = blocks[own].shape[-1]
    basis, channels = mix.shape
    around = len(table) * len(table[0]) * len(table[0][0])
    count = steps.shape[1]
    last = len(before)
    sums = (cells, basis * slots, channels)
    closing = [
        pltpu.VMEM((basis * channels, 2 * channels), bf16),
        pltpu.VMEM((cells * slots, 2 * basis * channels), bf16),
    ]
    return pl.pallas_call(
        functools.partial(message_kernel, basis, len(blocks), table, last, first, own),
        in_specs=[pl.BlockSpec(memory_space=pltpu.SMEM)] + [whole()] * (2 + len(blocks) + last),
        out_specs=whole(),
        scratch_shapes=[
            pltpu.VMEM((around, 2 * channels, slots), bf16),
            pltpu.VMEM((around, 8, slots), f32),
            pltpu.VMEM((cells, 3, slots, slots), f32),
            pltpu.VMEM((cells, basis * slots, 2 * channels), f32),
        ]
        + closing * bool(last)
        + [pltpu.VMEM((basis * slots, 6 * slots), bf16)] * 3
        + [pltpu.VMEM((2 * channels, 6 * slots), bf16)] * 3,
        out_shape=jax.ShapeDtypeStruct((cells, channels, slots) if last else sums, f32),
        compiler_params=params(),
        cost_estimate=pl.CostEstimate(
            flops=count * 8 * basis * slots * 9 * slots * channels, bytes_accessed=1 << 20,
            transcendentals=0,
        ),
        name="messages",
    )(steps, mix, w_value, *blocks, *before)


def visits(cells_x, cells_y, cells_z, inside, first=0, end=None):
    table = []
    for x in range(cells_x):
        for y in range(cells_y):
            for z in range(cells_z):
                own = (x * cells_y + y) * cells_z + z
                if not first <= own < (cells_x * cells_y * cells_z if end is None else end):
                    continue
                for shift in (-1, 0, 1):
                    plane = z + shift
                    if (0 <= plane < cells_z) != inside:
                        continue
                    if not inside:
                        plane = 0 if shift > 0 else 1
                    table.append([x - first // (cells_y * cells_z), y, plane, shift, own - first, 1, 1])
    for one, after in zip(table, table[1:]):
        if one[4] == after[4]:
            one[6] = after[5] = 0
    return np.array(table, np.int32).T.copy()


def mlp_kernel(count, shape, *refs):
    counts_ref, feature_ref = refs[:2]
    message_ref = refs[2]
    potentials = refs[3 : 3 + count]
    hidden_ref, back_ref, out_ref = refs[3 + count :]
    cells, channels, slots = feature_ref.shape
    columns = []
    for cell in range(cells):
        mixed = feature_ref[cell] + message_scale * message_ref[cell]
        for potential in potentials:
            mixed = mixed + potential[cell]
        columns.append(mixed)
    mixed = jnp.concatenate(columns, axis=1)
    inner = lax.dot_general(
        hidden_ref[...], mixed, (((0,), (0,)), ((), ())), precision=HIGH, preferred_element_type=f32
    )
    hidden = inner * jax.nn.sigmoid(inner)
    updated = mixed + lax.dot_general(
        back_ref[...], hidden, (((0,), (0,)), ((), ())), precision=HIGH, preferred_element_type=f32
    )
    slot = lax.broadcasted_iota(jnp.int32, (channels, slots), 1)
    for cell in range(cells):
        part = updated[:, cell * slots : (cell + 1) * slots]
        x, y, z = place_of(cell, shape)
        out_ref[cell] = jnp.where(slot < counts_ref[x, z, y], part, 0.0)


def atom_mlp(shape, counts, features, messages, potentials, w_hidden, w_out):
    return pl.pallas_call(
        functools.partial(mlp_kernel, len(potentials), shape),
        in_specs=[pl.BlockSpec(memory_space=pltpu.SMEM)]
        + [whole()] * (4 + len(potentials)),
        out_specs=whole(),
        out_shape=jax.ShapeDtypeStruct(features.shape, f32),
        compiler_params=params(),
        name="atom_mlp",
    )(counts, features, messages, *potentials, w_hidden, w_out)


def next_in_x(block, shape):
    size = lax.axis_size("gx")
    if size == 2:
        other = exchange(block, "gx", 1)
        return (other, shape[0] - 1), (other, 0)
    wide = block.reshape(shape + block.shape[1:])
    below, above = below_above(wide[:1], wide[-1:], "gx")
    return tuple((side.reshape((-1,) + block.shape[1:]), 0) for side in (below, above))


class Sources:
    def __init__(self):
        self.arrays = []

    def add(self, array):
        for n, held in enumerate(self.arrays):
            if held is array:
                return n
        self.arrays.append(array)
        return len(self.arrays) - 1

    def columns(self, block, shape):
        below, above = next_in_x(block, shape)
        inside = [(self.add(block), x) for x in range(shape[0])]
        return [(self.add(below[0]), below[1])] + inside + [(self.add(above[0]), above[1])]


def always():
    return True


def shards(
    features, positions, counts, waves, filter_table, w_value, w_charge, radial_mix, w_hidden, w_out
):
    shape = cells_x, cells_y, cells_z = features.shape[:3]
    channels, slots = features.shape[3:]
    total_waves = waves.shape[1]
    size_x, size_y, size_z = (lax.axis_size(a) for a in ("gx", "gy", "gz"))
    at_x, at_y, at_z = (lax.axis_index(a) for a in ("gx", "gy", "gz"))
    grid = (cells_x * size_x, cells_y * size_y, cells_z * size_z)
    cells = cells_x * cells_y * cells_z
    some_counts = jnp.transpose(counts, (0, 2, 1))
    flat_features = features.reshape(cells, channels, slots)

    share = total_waves // size_y
    own = pack(shape, grid, some_counts, flat_features, positions.reshape(cells * 3, 1, slots))
    rows = own.shape[1]
    packed = own.reshape(shape + (rows, slots))

    gathered = [own]
    for s in range(1, size_y):
        high = 1 << (s.bit_length() - 1)
        gathered.append(exchange(gathered[s - high], "gy", high))
    if cells_z == 1:
        sides = neighbours(own, own, "gz", same=True)
    else:
        flat = (cells_x * cells_y, rows, slots)
        sides = neighbours(packed[:, :, 0].reshape(flat), packed[:, :, -1].reshape(flat), "gz")

    half = 2 * share // size_x
    piece = half // size_z
    chunk = min(piece, share // size_x)
    first = min(1, size_y - 1)
    waves, gathered[first] = lax.optimization_barrier((waves, gathered[first]))
    *parts, table, columns = partial_factors(waves, share, chunk, own, (), size_x)
    tables = [table]
    for block in gathered[1:]:
        *parts, table = partial_factors(columns, share, chunk, block, parts, size_x)
        tables.append(table)

    summed = parts[0]
    for s in range(1, size_x):
        other = partner(at_x, s, size_x)
        to = parts[1]
        for n in range(2, size_x):
            to = jnp.where(lax.rem(other - at_x + size_x, size_x) == n, parts[n], to)
        summed = summed + exchange(to, "gx", s)
    low, high = (
        jnp.concatenate(
            [side[n : n + 1] for n in range(y, cells_x * cells_y, cells_y) for side in sides], axis=0
        )
        for y in (0, cells_y - 1)
    )
    edges = neighbours(low, high, "gy")
    value_near, summed = lax.optimization_barrier((w_value, summed))
    pieces = [lax.dynamic_slice_in_dim(summed, at_z * piece, piece, 0)]
    for s in range(1, size_z):
        other = partner(at_z, s, size_z)
        pieces.append(exchange(lax.dynamic_slice_in_dim(summed, other * piece, piece, 0), "gz", s))

    sources = Sources()

    def reaches(step, rank):
        return any(partner(i, step, size_y) == (i + rank) % size_y for i in range(size_y))

    columns = {
        step: sources.columns(block, shape)
        for step, block in enumerate(gathered)
        if any(reaches(step, rank) for rank in (-1, 0, 1))
    }

    def at_rank(step, rank):
        def condition():
            at = lax.axis_index("gy")
            return partner(at, step, size_y) == (at + rank) % size_y

        return condition

    def choices(x, y, z):
        rank = -1 if y < 0 else 1 if y == cells_y else 0
        y = y % cells_y
        found = []
        for step in columns:
            if reaches(step, rank):
                source, from_x = columns[step][x + 1]
                found.append((at_rank(step, rank), source, (from_x * cells_y + y) * cells_z + z))
        return found

    table = [
        [[choices(x, y, z) for z in range(cells_z)] for y in range(-1, cells_y + 1)]
        for x in range(-1, cells_x + 1)
    ]
    layer = cells_y * cells_z
    at_once = (cells_x + 1) // 2
    near = []

    def near_messages(begin, value):
        end = min(begin + at_once, cells_x)
        inner = visits(cells_x, cells_y, cells_z, True, begin * layer, end * layer)
        return pair_messages(
            jnp.asarray(inner), sources.add(own), sources.arrays, table[begin : end + 2], radial_mix, value,
            (end - begin) * layer, begin * layer,
        )

    near.append(near_messages(0, value_near))

    scale = 1.0 / math.sqrt(grid[0] * grid[1] * grid[2] * slots) / math.sqrt(total_waves)
    rank = at_x * size_z + at_z
    block = at_y * (share // chunk) + (rank * piece) // (2 * chunk)
    charge, near[0] = lax.optimization_barrier((w_charge, near[0]))
    filtered = filtered_piece(scale, block.reshape(1), chunk, pieces, charge, filter_table)

    value_near, filtered = lax.optimization_barrier((w_value, filtered))
    if cells_x > 1:
        near.append(near_messages(at_once, value_near))
    held_z = jnp.concatenate(
        [filtered] + [exchange(filtered, "gz", s) for s in range(1, size_z)], axis=0
    )
    held_z, *rest = lax.optimization_barrier((held_z, *near, *edges))
    near, edges = rest[:-2], rest[-2:]
    held = [held_z] + [exchange(held_z, "gx", s) for s in range(1, size_x)]

    sources = Sources()
    flat = (cells_x, cells_y, 1)
    side_columns = [sources.columns(side, flat) for side in sides]
    edge_columns = [sources.columns(edge, (cells_x, 1, 2)) for edge in edges]

    def choices(x, y, z):
        if 0 <= y < cells_y:
            source, from_x = side_columns[z][x + 1]
            return [(always, source, from_x * cells_y + y)]
        found = []
        for n, columns in enumerate(edge_columns):
            source, from_x = columns[x + 1]
            first_is_here = y == cells_y
            condition = (lambda: is_even("gy")) if (n == 0) == first_is_here else (
                lambda: jnp.logical_not(is_even("gy"))
            )
            found.append((condition, source, from_x * 2 + z))
        return found

    table = [
        [[choices(x, y, z) for z in range(2)] for y in range(-1, cells_y + 1)]
        for x in range(-1, cells_x + 1)
    ]
    found = potentials_of(held, held_z.shape[0] // piece, tables, cells, slots)
    value_far, *found = lax.optimization_barrier((w_value, *found))
    returned = [found[0]] + [exchange(found[s], "gy", s) for s in range(1, size_y)]
    outer = jnp.asarray(visits(cells_x, cells_y, cells_z, False))
    messages = pair_messages(
        outer, sources.add(own), sources.arrays, table, radial_mix, value_far, cells, 0, near
    )

    updated = atom_mlp(
        shape, some_counts, flat_features, messages, returned, w_hidden, w_out
    )
    return updated.reshape(features.shape)


def solution(mesh):
    placed = (
        P("gx", "gy", "gz", None, None),
        P("gx", "gy", "gz", None, None),
        P("gx", "gy", "gz"),
        P(),
        P(),
        P(),
        P(),
        P(),
        P(),
        P(),
    )
    return jax.shard_map(
        shards,
        mesh=mesh,
        in_specs=placed,
        out_specs=P("gx", "gy", "gz", None, None),
        check_vma=False,
    )
```

```python
import functools
import math

import numpy as np

import jax
import jax.numpy as jnp
from jax import lax
from jax.experimental import pallas as pl
from jax.experimental.pallas import tpu as pltpu
from jax.sharding import PartitionSpec as P


HIGH = lax.Precision.HIGH
message_scale = 0.125
bf16 = jnp.bfloat16
f32 = jnp.float32
VMEM_LIMIT = 28 * 1024 * 1024
PACK_LIMIT = 62 * 1024 * 1024


LOG2E = math.log2(math.e)


def partner(i, step, count):
    return i ^ step


def exchange(block, axis, step):
    count = lax.axis_size(axis)
    pairs = [(i, partner(i, step, count)) for i in range(count)]
    return lax.ppermute(block, axis, pairs)


def is_even(axis):
    if lax.axis_size(axis) % 2:
        return jnp.bool_(True)
    return lax.rem(lax.axis_index(axis), 2) == 0


def neighbours(low, high, axis, same=False):
    count = lax.axis_size(axis)
    if count == 1:
        return low, high
    if count % 2:
        up = lax.ppermute(low, axis, [(i, (i - 1) % count) for i in range(count)])
        down = lax.ppermute(high, axis, [(i, (i + 1) % count) for i in range(count)])
        return up, down
    even = is_even(axis)
    first = high if same else jnp.where(even, high, low)
    second = low if same else jnp.where(even, low, high)
    one = [(i, i ^ 1) for i in range(count)]
    two = [(i, (i + 1 if i % 2 else i - 1) % count) for i in range(count)]
    return lax.ppermute(first, axis, one), lax.ppermute(second, axis, two)


def below_above(low, high, axis):
    first, second = neighbours(low, high, axis)
    even = is_even(axis)
    return jnp.where(even, second, first), jnp.where(even, first, second)


def split(x):
    high = x.astype(bf16)
    low = (x - high.astype(f32)).astype(bf16)
    return high, low


def whole():
    return pl.BlockSpec(memory_space=pltpu.VMEM)


def params(limit=VMEM_LIMIT):
    return pltpu.CompilerParams(vmem_limit_bytes=limit)


def place_of(cell, shape):
    return cell // (shape[1] * shape[2]), cell // shape[2] % shape[1], cell % shape[2]


def pack_kernel(
    shape, grid, counts_hbm, feature_hbm, position_hbm, out_ref,
    counts_ref, feature_ref, position_ref, sems,
):
    cells, channels, slots = feature_ref.shape
    copies = [
        pltpu.make_async_copy(counts_hbm, counts_ref, sems.at[0]),
        pltpu.make_async_copy(position_hbm, position_ref, sems.at[1]),
        pltpu.make_async_copy(feature_hbm, feature_ref, sems.at[2]),
    ]
    for copy in copies:
        copy.start()
    for copy in copies:
        copy.wait()
    slot = lax.broadcasted_iota(jnp.int32, (channels, slots), 1)
    for cell in range(cells):
        place = place_of(cell, shape)
        held = slot < counts_ref[place[0], place[2], place[1]]
        out_ref[cell, :channels, :] = jnp.where(held, feature_ref[cell], 0.0)
        at = [position_ref[3 * cell + axis] for axis in range(3)]
        rows = list(at)
        for axis, name in enumerate(("gx", "gy", "gz")):
            here = lax.axis_index(name) * shape[axis] + place[axis]
            rows.append((at[axis] + here.astype(f32)) * (1.0 / grid[axis]))
        out_ref[cell, channels:, :] = jnp.concatenate(rows + [jnp.zeros((2, slots), f32)], axis=0)


def pack(shape, grid, counts, features, positions):
    cells, channels, slots = features.shape
    return pl.pallas_call(
        functools.partial(pack_kernel, shape, grid),
        in_specs=[pl.BlockSpec(memory_space=pltpu.HBM)] * 3,
        out_specs=whole(),
        out_shape=jax.ShapeDtypeStruct((cells, channels + 8, slots), f32),
        scratch_shapes=[
            pltpu.SMEM(counts.shape, jnp.int32),
            pltpu.VMEM(features.shape, f32),
            pltpu.VMEM(positions.shape, f32),
            pltpu.SemaphoreType.DMA((3,)),
        ],
        compiler_params=params(),
        name="pack",
    )(counts, features, positions)


def fitted(function, terms):
    t = 0.125 * (1.0 + np.cos(np.pi * (np.arange(terms) + 0.5) / terms))
    solved = np.linalg.solve(np.vander(t, terms, increasing=True), function(np.sqrt(t)))
    return [float(c) for c in solved]


SIN = fitted(lambda u: math.sqrt(2.0) * np.sin(np.pi * u) / u, 5)
COS = fitted(lambda u: math.sqrt(2.0) * np.cos(np.pi * u), 5)


def poly(coefficients, t):
    acc = t * coefficients[-1] + coefficients[-2]
    for c in coefficients[-3::-1]:
        acc = acc * t + c
    return acc


def turns(u):
    u = u - jnp.round(u)
    t = u * u
    sine = poly(SIN, t) * u
    cosine = poly(COS, t)
    return 1.0 - sine * sine, sine * cosine


def factor_kernel(parts, chunk, first, column_ref, block_ref, *refs):
    before = refs[: 0 if first else parts]
    refs = refs[len(before) :]
    after, wave_ref, refs = refs[:parts], refs[parts], refs[parts + 1 :]
    weight_ref = refs[-1]
    cells, _, slots = block_ref.shape
    channels = after[0].shape[-1]
    span = cells * slots
    total = wave_ref.shape[0] // 2
    at_x = lax.axis_index("gx")
    if first:
        begin = pl.multiple_of(lax.axis_index("gy") * total, total)
        rows = column_ref[:, pl.ds(begin, total)].astype(f32)
        column_ref = refs[0]
        column_ref[...] = jnp.concatenate([rows, jnp.zeros((5, total), f32)], axis=0).T
    for cell in range(cells):
        high, low = split(block_ref[cell, :channels, :])
        for at in (cell * slots, span + cell * slots):
            weight_ref[:channels, at : at + slots] = high
            weight_ref[channels:, at : at + slots] = low

    def some(j, carry):
        here = pl.multiple_of(j * chunk, chunk)
        wave_x = column_ref[pl.ds(here, chunk), 0:1]
        wave_y = column_ref[pl.ds(here, chunk), 1:2]
        wave_z = column_ref[pl.ds(here, chunk), 2:3]
        row = pl.multiple_of(j * 2 * chunk, 2 * chunk)
        for cell in range(cells):
            at = cell * slots
            frac = block_ref[cell, channels + 3 : channels + 6, :]
            u = wave_x * frac[0:1] + wave_y * frac[1:2] + wave_z * frac[2:3]
            cosine, sine = turns(u)
            high, low = split(cosine)
            wave_ref[pl.ds(row, chunk), at : at + slots] = high
            wave_ref[pl.ds(row, chunk), span + at : span + at + slots] = low
            high, low = split(sine)
            wave_ref[pl.ds(row + chunk, chunk), at : at + slots] = high
            wave_ref[pl.ds(row + chunk, chunk), span + at : span + at + slots] = low
        return carry

    lax.fori_loop(0, total // chunk, some, 0, unroll=total // chunk <= 8)
    half = 2 * total // parts
    for n in range(parts):
        row = pl.multiple_of(lax.rem(at_x + n, parts) * half, half)
        both = lax.dot_general(
            wave_ref[pl.ds(row, half), :], weight_ref[...], (((1,), (1,)), ((), ())),
            preferred_element_type=f32,
        )
        both = both[:, :channels] + both[:, channels:]
        after[n][...] = both if first else before[n][...] + both


def partial_factors(columns, total, chunk, block, before, parts):
    cells, rows, slots = block.shape
    channels = rows - 8
    span = cells * slots
    out = [jax.ShapeDtypeStruct((2 * total // parts, channels), f32)] * parts
    out.append(jax.ShapeDtypeStruct((2 * total, 2 * span), bf16))
    if not before:
        out.append(jax.ShapeDtypeStruct((total, 8), f32))
    return pl.pallas_call(
        functools.partial(factor_kernel, parts, chunk, not before),
        in_specs=[whole()] * (2 + len(before)),
        out_specs=[whole()] * len(out),
        out_shape=out,
        input_output_aliases={2 + n: n for n in range(len(before))},
        scratch_shapes=[pltpu.VMEM((2 * channels, 2 * span), bf16)],
        compiler_params=params(),
        cost_estimate=pl.CostEstimate(
            flops=8 * total * span * channels, bytes_accessed=8 * total * span, transcendentals=0
        ),
        name="factors",
    )(columns, block, *before)


def filter_kernel(scale, block_ref, *refs):
    parts, (weight_ref, table_ref, out_ref) = refs[:-3], refs[-3:]
    summed = parts[0][...]
    for part in parts[1:]:
        summed = summed + part[...]
    projected = jnp.dot(summed, weight_ref[...], precision=HIGH, preferred_element_type=f32)
    table = table_ref[...] * scale
    for n in range(0, summed.shape[0], table.shape[0]):
        out_ref[n : n + table.shape[0], :] = projected[n : n + table.shape[0]] * table


def filtered_piece(scale, block, chunk, parts, w_charge, table):
    rows, channels = parts[0].shape
    fixed = pl.BlockSpec((rows, channels), lambda i, block: (0, 0))
    return pl.pallas_call(
        functools.partial(filter_kernel, scale),
        grid_spec=pltpu.PrefetchScalarGridSpec(
            num_scalar_prefetch=1,
            grid=(1,),
            in_specs=[fixed] * len(parts)
            + [
                pl.BlockSpec(w_charge.shape, lambda i, block: (0, 0)),
                pl.BlockSpec((chunk, channels), lambda i, block: (block[0], 0)),
            ],
            out_specs=fixed,
        ),
        out_shape=jax.ShapeDtypeStruct((rows, channels), f32),
        compiler_params=params(),
        name="filter",
    )(block, *parts, w_charge, table)


def potential_kernel(groups, pieces, blocks, *refs):
    held = refs[:groups]
    waves = refs[groups : groups + blocks]
    outs = refs[groups + blocks : -2]
    ordered_ref, turned_ref = refs[-2:]
    channels = ordered_ref.shape[-1]
    piece = held[0].shape[0] // pieces
    for group in range(groups):
        for n in range(pieces):
            rank_x = partner(lax.axis_index("gx"), group, groups)
            rank_z = partner(lax.axis_index("gz"), n, pieces)
            at = pl.multiple_of((rank_x * pieces + rank_z) * piece, piece)
            ordered_ref[pl.ds(at, piece), :] = held[group][n * piece : (n + 1) * piece, :]
    high, low = split(ordered_ref[...].T)
    turned_ref[:channels, :] = high
    turned_ref[channels:, :] = low
    for wave_ref, out in zip(waves, outs):
        cells, _, slots = out.shape
        span = cells * slots
        both = jnp.dot(turned_ref[...], wave_ref[:, :span], preferred_element_type=f32)
        third = jnp.dot(turned_ref[:channels, :], wave_ref[:, span:], preferred_element_type=f32)
        potential = both[:channels] + both[channels:] + third
        for cell in range(cells):
            out[cell] = potential[:, cell * slots : (cell + 1) * slots]


def potentials_of(held, pieces, waves, cells, slots):
    rows = waves[0].shape[0]
    channels = held[0].shape[-1]
    return pl.pallas_call(
        functools.partial(potential_kernel, len(held), pieces, len(waves)),
        in_specs=[whole()] * (len(held) + len(waves)),
        out_specs=[whole()] * len(waves),
        scratch_shapes=[
            pltpu.VMEM((rows, channels), f32),
            pltpu.VMEM((2 * channels, rows), bf16),
        ],
        out_shape=[jax.ShapeDtypeStruct((cells, channels, slots), f32)] * len(waves),
        compiler_params=params(),
        cost_estimate=pl.CostEstimate(
            flops=6 * rows * len(waves) * cells * slots * channels,
            bytes_accessed=4 * rows * len(waves) * cells * slots, transcendentals=0,
        ),
        name="potentials",
    )(*held, *waves)


def message_kernel(
    basis, sources, table, together, once, last, first, own_source, step_ref, mix_ref, value_ref, *refs
):
    blocks, refs = refs[:sources], refs[sources:]
    own_ref = blocks[own_source]
    if last:
        before, refs = refs[:last], refs[last:]
        out_ref, cell_ref, at_ref, own_col_ref, acc_ref, mixed_ref, wide_ref = refs[:7]
    else:
        out_ref, cell_ref, at_ref, own_col_ref, acc_ref = refs[:5]
    left_ref = refs[-1]
    count = step_ref.shape[1]
    cells = acc_ref.shape[0]
    slots = own_ref.shape[-1]
    along, planes = len(table[0]), len(table[0][0])
    channels = value_ref.shape[0]

    for x, columns in enumerate(table):
        for y, column in enumerate(columns):
            for z, choices in enumerate(column):
                n = (x * along + y) * planes + z
                (_, source, index), others = choices[0], choices[1:]
                block = blocks[source][index]
                for condition, source, index in others:
                    block = jnp.where(condition(), blocks[source][index], block)
                high, low = split(block[:channels])
                cell_ref[n, :channels, :] = high
                cell_ref[n, channels:, :] = low
                at_ref[n] = block[channels:]
    for b in range(basis) if last else ():
        high, low = split(value_ref[...] * (mix_ref[b : b + 1, :] * math.exp(-b * b)))
        mixed_ref[b * channels : (b + 1) * channels, :channels] = high
        mixed_ref[b * channels : (b + 1) * channels, channels:] = low
    for cell in range(cells):
        columns = own_ref[first + cell, channels : channels + 8, :].T
        for axis in range(3):
            own_col_ref[cell, axis] = jnp.broadcast_to(columns[:, axis : axis + 1], (slots, slots))

    def fill(step, visit, move):
        place_x = step_ref[0, step] + 1 + (move - 1)
        place_y = step_ref[1, step]
        plane = plane_of(step)
        shift_z = step_ref[3, step].astype(f32)
        own = step_ref[4, step]
        near = []
        for n in range(3):
            number = (place_x * along + place_y + n) * planes + plane
            at = at_ref[number]
            near.append((at[0:1] + float(move - 1), at[1:2] + float(n - 1), at[2:3] + shift_z))
        tile = 16
        for m in range(slots // tile):
            at = m * tile
            own_x = own_col_ref[own, 0, at : at + tile, :]
            own_y = own_col_ref[own, 1, at : at + tile, :]
            own_z = own_col_ref[own, 2, at : at + tile, :]
            for n in range(3):
                dx = near[n][0] - own_x
                dy = near[n][1] - own_y
                dz = near[n][2] - own_z
                squared = dx * dx + dy * dy + dz * dz
                distance = squared * lax.rsqrt(jnp.maximum(squared, 1e-30))
                envelope = jnp.maximum(1.0 - squared, 0.0)
                term = envelope * envelope * jnp.exp2(squared * (-float((basis - 1) ** 2) * LOG2E))
                ratio = jnp.exp2(distance * (2.0 * (basis - 1) * LOG2E))
                if not last and move == 1 and n == 1:
                    i = lax.broadcasted_iota(jnp.int32, (tile, slots), 0) + at
                    j = lax.broadcasted_iota(jnp.int32, (tile, slots), 1)
                    same = jnp.logical_and(i == j, step_ref[3, step] == 0)
                    term = jnp.where(same, 0.0, term)
                for b in range(basis):
                    if b > 0:
                        term = term * ratio
                    high, low = split(term)
                    row = b * slots + at
                    here = 9 * visit + 3 * move + n
                    left_ref[row : row + tile, here * slots : (here + 1) * slots] = high
                    here += 9 * together
                    left_ref[row : row + tile, here * slots : (here + 1) * slots] = low

    def plane_of(step):
        plane = step_ref[2, step]
        return jnp.where(is_even("gz"), plane, 1 - plane) if last else plane

    def near_of(step):
        held = []
        for n in range(together):
            x, y = step_ref[0, step + n], step_ref[1, step + n]
            plane = plane_of(step + n)
            held += [
                cell_ref[((x + over_x) * along + y + over_y) * planes + plane]
                for over_x in range(3)
                for over_y in range(3)
            ]
        return jnp.concatenate(held + held, axis=1)

    def product(step):
        return lax.dot_general(
            left_ref[...], near_of(step), (((1,), (1,)), ((), ())), preferred_element_type=f32
        )

    def visit(group, carry):
        step = group * together
        own = step_ref[4, step]
        for n in range(together):
            for move in range(3):
                fill(step + n, n, move)
        if once:
            acc_ref[own] = product(step)
        else:
            fresh = step_ref[5, step] == 1
            acc_ref[own] = jnp.where(fresh, 0.0, acc_ref[own]) + product(step)
        return carry

    lax.fori_loop(0, count // together, visit, 0)
    wide = basis * channels
    for cell in range(cells):
        gathered = acc_ref[cell, :, :channels] + acc_ref[cell, :, channels:]
        if not last:
            out_ref[cell] = gathered
            continue
        per = cells // last
        high, low = split(gathered + before[cell // per][cell % per])
        here = slice(cell * slots, (cell + 1) * slots)
        for b in range(basis):
            wide_ref[here, b * channels : (b + 1) * channels] = high[b * slots : (b + 1) * slots]
            wide_ref[here, wide + b * channels : wide + (b + 1) * channels] = low[b * slots : (b + 1) * slots]
    if last:
        both = jnp.dot(wide_ref[:, :wide], mixed_ref[...], preferred_element_type=f32)
        both = both + jnp.dot(wide_ref[:, wide:], mixed_ref[...], preferred_element_type=f32)
        for cell in range(cells):
            part = both[cell * slots : (cell + 1) * slots]
            out_ref[cell] = (part[:, :channels] + part[:, channels:]).T


def pair_messages(steps, own, blocks, table, mix, w_value, cells, first, before=()):
    slots = blocks[own].shape[-1]
    basis, channels = mix.shape
    around = len(table) * len(table[0]) * len(table[0][0])
    count = steps.shape[1]
    per_cell = np.bincount(steps[4], minlength=cells)
    once = bool(np.all(per_cell == per_cell[0]))
    together = int(per_cell[0]) if once else 1
    last = len(before)
    sums = (cells, basis * slots, channels)
    closing = [
        pltpu.VMEM((basis * channels, 2 * channels), bf16),
        pltpu.VMEM((cells * slots, 2 * basis * channels), bf16),
    ]
    return pl.pallas_call(
        functools.partial(
            message_kernel, basis, len(blocks), table, together, once, last, first, own
        ),
        in_specs=[pl.BlockSpec(memory_space=pltpu.SMEM)] + [whole()] * (2 + len(blocks) + last),
        out_specs=whole(),
        scratch_shapes=[
            pltpu.VMEM((around, 2 * channels, slots), bf16),
            pltpu.VMEM((around, 8, slots), f32),
            pltpu.VMEM((cells, 3, slots, slots), f32),
            pltpu.VMEM((cells, basis * slots, 2 * channels), f32),
        ]
        + closing * bool(last)
        + [pltpu.VMEM((basis * slots, 18 * together * slots), bf16)],
        out_shape=jax.ShapeDtypeStruct((cells, channels, slots) if last else sums, f32),
        compiler_params=params(),
        cost_estimate=pl.CostEstimate(
            flops=count * 8 * basis * slots * 9 * slots * channels, bytes_accessed=1 << 20,
            transcendentals=0,
        ),
        name="messages",
    )(jnp.asarray(steps), mix, w_value, *blocks, *before)


def visits(cells_x, cells_y, cells_z, inside, first=0, end=None):
    table = []
    for x in range(cells_x):
        for y in range(cells_y):
            for z in range(cells_z):
                own = (x * cells_y + y) * cells_z + z
                if not first <= own < (cells_x * cells_y * cells_z if end is None else end):
                    continue
                for shift in (-1, 0, 1):
                    plane = z + shift
                    if (0 <= plane < cells_z) != inside:
                        continue
                    if not inside:
                        plane = 0 if shift > 0 else 1
                    table.append([x - first // (cells_y * cells_z), y, plane, shift, own - first, 1, 1])
    for one, after in zip(table, table[1:]):
        if one[4] == after[4]:
            one[6] = after[5] = 0
    return np.array(table, np.int32).T.copy()


def mlp_kernel(count, shape, *refs):
    counts_ref, feature_ref = refs[:2]
    message_ref = refs[2]
    potentials = refs[3 : 3 + count]
    hidden_ref, back_ref, out_ref = refs[3 + count :]
    cells, channels, slots = feature_ref.shape
    columns = []
    for cell in range(cells):
        mixed = feature_ref[cell] + message_scale * message_ref[cell]
        for potential in potentials:
            mixed = mixed + potential[cell]
        columns.append(mixed)
    mixed = jnp.concatenate(columns, axis=1)
    inner = lax.dot_general(
        hidden_ref[...], mixed, (((0,), (0,)), ((), ())), precision=HIGH, preferred_element_type=f32
    )
    hidden = inner * jax.nn.sigmoid(inner)
    updated = mixed + lax.dot_general(
        back_ref[...], hidden, (((0,), (0,)), ((), ())), precision=HIGH, preferred_element_type=f32
    )
    slot = lax.broadcasted_iota(jnp.int32, (channels, slots), 1)
    for cell in range(cells):
        part = updated[:, cell * slots : (cell + 1) * slots]
        x, y, z = place_of(cell, shape)
        out_ref[cell] = jnp.where(slot < counts_ref[x, z, y], part, 0.0)


def atom_mlp(shape, counts, features, messages, potentials, w_hidden, w_out):
    return pl.pallas_call(
        functools.partial(mlp_kernel, len(potentials), shape),
        in_specs=[pl.BlockSpec(memory_space=pltpu.SMEM)]
        + [whole()] * (4 + len(potentials)),
        out_specs=whole(),
        out_shape=jax.ShapeDtypeStruct(features.shape, f32),
        compiler_params=params(),
        name="atom_mlp",
    )(counts, features, messages, *potentials, w_hidden, w_out)


def next_in_x(block, shape):
    size = lax.axis_size("gx")
    if size == 2:
        other = exchange(block, "gx", 1)
        return (other, shape[0] - 1), (other, 0)
    wide = block.reshape(shape + block.shape[1:])
    below, above = below_above(wide[:1], wide[-1:], "gx")
    return tuple((side.reshape((-1,) + block.shape[1:]), 0) for side in (below, above))


class Sources:
    def __init__(self):
        self.arrays = []

    def add(self, array):
        for n, held in enumerate(self.arrays):
            if held is array:
                return n
        self.arrays.append(array)
        return len(self.arrays) - 1

    def columns(self, block, shape):
        below, above = next_in_x(block, shape)
        inside = [(self.add(block), x) for x in range(shape[0])]
        return [(self.add(below[0]), below[1])] + inside + [(self.add(above[0]), above[1])]


def always():
    return True


def shards(
    features, positions, counts, waves, filter_table, w_value, w_charge, radial_mix, w_hidden, w_out
):
    shape = cells_x, cells_y, cells_z = features.shape[:3]
    channels, slots = features.shape[3:]
    total_waves = waves.shape[1]
    size_x, size_y, size_z = (lax.axis_size(a) for a in ("gx", "gy", "gz"))
    at_x, at_y, at_z = (lax.axis_index(a) for a in ("gx", "gy", "gz"))
    grid = (cells_x * size_x, cells_y * size_y, cells_z * size_z)
    cells = cells_x * cells_y * cells_z
    some_counts = jnp.transpose(counts, (0, 2, 1))
    flat_features = features.reshape(cells, channels, slots)

    share = total_waves // size_y
    own = pack(shape, grid, some_counts, flat_features, positions.reshape(cells * 3, 1, slots))
    rows = own.shape[1]
    packed = own.reshape(shape + (rows, slots))

    gathered = [own]
    for s in range(1, size_y):
        high = 1 << (s.bit_length() - 1)
        gathered.append(exchange(gathered[s - high], "gy", high))
    if cells_z == 1:
        sides = neighbours(own, own, "gz", same=True)
    else:
        flat = (cells_x * cells_y, rows, slots)
        sides = neighbours(packed[:, :, 0].reshape(flat), packed[:, :, -1].reshape(flat), "gz")

    half = 2 * share // size_x
    piece = half // size_z
    chunk = min(piece, share // size_x)
    first = min(1, size_y - 1)
    waves, gathered[first] = lax.optimization_barrier((waves, gathered[first]))
    *parts, table, columns = partial_factors(waves, share, chunk, own, (), size_x)
    tables = [table]
    for block in gathered[1:]:
        *parts, table = partial_factors(columns, share, chunk, block, parts, size_x)
        tables.append(table)

    summed = parts[0]
    for s in range(1, size_x):
        other = partner(at_x, s, size_x)
        to = parts[1]
        for n in range(2, size_x):
            to = jnp.where(lax.rem(other - at_x + size_x, size_x) == n, parts[n], to)
        summed = summed + exchange(to, "gx", s)
    low, high = (
        jnp.concatenate(
            [side[n : n + 1] for n in range(y, cells_x * cells_y, cells_y) for side in sides], axis=0
        )
        for y in (0, cells_y - 1)
    )
    edges = neighbours(low, high, "gy")
    value_near, summed = lax.optimization_barrier((w_value, summed))
    pieces = [lax.dynamic_slice_in_dim(summed, at_z * piece, piece, 0)]
    for s in range(1, size_z):
        other = partner(at_z, s, size_z)
        pieces.append(exchange(lax.dynamic_slice_in_dim(summed, other * piece, piece, 0), "gz", s))

    sources = Sources()

    def reaches(step, rank):
        return any(partner(i, step, size_y) == (i + rank) % size_y for i in range(size_y))

    columns = {
        step: sources.columns(block, shape)
        for step, block in enumerate(gathered)
        if any(reaches(step, rank) for rank in (-1, 0, 1))
    }

    def at_rank(step, rank):
        def condition():
            at = lax.axis_index("gy")
            return partner(at, step, size_y) == (at + rank) % size_y

        return condition

    def choices(x, y, z):
        rank = -1 if y < 0 else 1 if y == cells_y else 0
        y = y % cells_y
        found = []
        for step in columns:
            if reaches(step, rank):
                source, from_x = columns[step][x + 1]
                found.append((at_rank(step, rank), source, (from_x * cells_y + y) * cells_z + z))
        return found

    table = [
        [[choices(x, y, z) for z in range(cells_z)] for y in range(-1, cells_y + 1)]
        for x in range(-1, cells_x + 1)
    ]
    layer = cells_y * cells_z
    at_once = (cells_x + 1) // 2
    near = []

    def near_messages(begin, value):
        end = min(begin + at_once, cells_x)
        inner = visits(cells_x, cells_y, cells_z, True, begin * layer, end * layer)
        return pair_messages(
            inner, sources.add(own), sources.arrays, table[begin : end + 2], radial_mix, value,
            (end - begin) * layer, begin * layer,
        )

    near.append(near_messages(0, value_near))

    scale = 1.0 / math.sqrt(grid[0] * grid[1] * grid[2] * slots) / math.sqrt(total_waves)
    rank = at_x * size_z + at_z
    block = at_y * (share // chunk) + (rank * piece) // (2 * chunk)
    charge, near[0] = lax.optimization_barrier((w_charge, near[0]))
    filtered = filtered_piece(scale, block.reshape(1), chunk, pieces, charge, filter_table)

    value_near, filtered = lax.optimization_barrier((w_value, filtered))
    if cells_x > 1:
        near.append(near_messages(at_once, value_near))
    held_z = jnp.concatenate(
        [filtered] + [exchange(filtered, "gz", s) for s in range(1, size_z)], axis=0
    )
    held_z, *rest = lax.optimization_barrier((held_z, *near, *edges))
    near, edges = rest[:-2], rest[-2:]
    held = [held_z] + [exchange(held_z, "gx", s) for s in range(1, size_x)]

    sources = Sources()
    flat = (cells_x, cells_y, 1)
    side_columns = [sources.columns(side, flat) for side in sides]
    edge_columns = [sources.columns(edge, (cells_x, 1, 2)) for edge in edges]

    def choices(x, y, z):
        if 0 <= y < cells_y:
            source, from_x = side_columns[z][x + 1]
            return [(always, source, from_x * cells_y + y)]
        found = []
        for n, columns in enumerate(edge_columns):
            source, from_x = columns[x + 1]
            first_is_here = y == cells_y
            condition = (lambda: is_even("gy")) if (n == 0) == first_is_here else (
                lambda: jnp.logical_not(is_even("gy"))
            )
            found.append((condition, source, from_x * 2 + z))
        return found

    table = [
        [[choices(x, y, z) for z in range(2)] for y in range(-1, cells_y + 1)]
        for x in range(-1, cells_x + 1)
    ]
    found = potentials_of(held, held_z.shape[0] // piece, tables, cells, slots)
    value_far, *found = lax.optimization_barrier((w_value, *found))
    returned = [found[0]] + [exchange(found[s], "gy", s) for s in range(1, size_y)]
    outer = visits(cells_x, cells_y, cells_z, False)
    messages = pair_messages(
        outer, sources.add(own), sources.arrays, table, radial_mix, value_far, cells, 0, near
    )

    updated = atom_mlp(
        shape, some_counts, flat_features, messages, returned, w_hidden, w_out
    )
    return updated.reshape(features.shape)


def solution(mesh):
    placed = (
        P("gx", "gy", "gz", None, None),
        P("gx", "gy", "gz", None, None),
        P("gx", "gy", "gz"),
        P(),
        P(),
        P(),
        P(),
        P(),
        P(),
        P(),
    )
    return jax.shard_map(
        shards,
        mesh=mesh,
        in_specs=placed,
        out_specs=P("gx", "gy", "gz", None, None),
        check_vma=False,
    )
```

```python
import functools
import math

import numpy as np

import jax
import jax.numpy as jnp
from jax import lax
from jax.experimental import pallas as pl
from jax.experimental.pallas import tpu as pltpu
from jax.sharding import PartitionSpec as P


HIGH = lax.Precision.HIGH
message_scale = 0.125
bf16 = jnp.bfloat16
f32 = jnp.float32
VMEM_LIMIT = 28 * 1024 * 1024
PACK_LIMIT = 62 * 1024 * 1024


LOG2E = math.log2(math.e)


def partner(i, step, count):
    return i ^ step


def exchange(block, axis, step):
    count = lax.axis_size(axis)
    pairs = [(i, partner(i, step, count)) for i in range(count)]
    return lax.ppermute(block, axis, pairs)


def is_even(axis):
    if lax.axis_size(axis) % 2:
        return jnp.bool_(True)
    return lax.rem(lax.axis_index(axis), 2) == 0


def neighbours(low, high, axis, same=False):
    count = lax.axis_size(axis)
    if count == 1:
        return low, high
    if count % 2:
        up = lax.ppermute(low, axis, [(i, (i - 1) % count) for i in range(count)])
        down = lax.ppermute(high, axis, [(i, (i + 1) % count) for i in range(count)])
        return up, down
    even = is_even(axis)
    first = high if same else jnp.where(even, high, low)
    second = low if same else jnp.where(even, low, high)
    one = [(i, i ^ 1) for i in range(count)]
    two = [(i, (i + 1 if i % 2 else i - 1) % count) for i in range(count)]
    return lax.ppermute(first, axis, one), lax.ppermute(second, axis, two)


def below_above(low, high, axis):
    first, second = neighbours(low, high, axis)
    even = is_even(axis)
    return jnp.where(even, second, first), jnp.where(even, first, second)


def split(x):
    high = x.astype(bf16)
    low = (x - high.astype(f32)).astype(bf16)
    return high, low


def whole():
    return pl.BlockSpec(memory_space=pltpu.VMEM)


def params(limit=VMEM_LIMIT):
    return pltpu.CompilerParams(vmem_limit_bytes=limit)


def place_of(cell, shape):
    return cell // (shape[1] * shape[2]), cell // shape[2] % shape[1], cell % shape[2]


def pack_kernel(
    shape, grid, counts_hbm, feature_hbm, position_hbm, out_ref,
    counts_ref, feature_ref, position_ref, sems,
):
    cells, channels, slots = feature_ref.shape
    copies = [
        pltpu.make_async_copy(counts_hbm, counts_ref, sems.at[0]),
        pltpu.make_async_copy(position_hbm, position_ref, sems.at[1]),
        pltpu.make_async_copy(feature_hbm, feature_ref, sems.at[2]),
    ]
    for copy in copies:
        copy.start()
    for copy in copies:
        copy.wait()
    slot = lax.broadcasted_iota(jnp.int32, (channels, slots), 1)
    for cell in range(cells):
        place = place_of(cell, shape)
        held = slot < counts_ref[place[0], place[2], place[1]]
        out_ref[cell, :channels, :] = jnp.where(held, feature_ref[cell], 0.0)
        at = [position_ref[3 * cell + axis] for axis in range(3)]
        rows = list(at)
        for axis, name in enumerate(("gx", "gy", "gz")):
            here = lax.axis_index(name) * shape[axis] + place[axis]
            rows.append((at[axis] + here.astype(f32)) * (1.0 / grid[axis]))
        out_ref[cell, channels:, :] = jnp.concatenate(rows + [jnp.zeros((2, slots), f32)], axis=0)


def pack(shape, grid, counts, features, positions):
    cells, channels, slots = features.shape
    return pl.pallas_call(
        functools.partial(pack_kernel, shape, grid),
        in_specs=[pl.BlockSpec(memory_space=pltpu.HBM)] * 3,
        out_specs=whole(),
        out_shape=jax.ShapeDtypeStruct((cells, channels + 8, slots), f32),
        scratch_shapes=[
            pltpu.SMEM(counts.shape, jnp.int32),
            pltpu.VMEM(features.shape, f32),
            pltpu.VMEM(positions.shape, f32),
            pltpu.SemaphoreType.DMA((3,)),
        ],
        compiler_params=params(),
        name="pack",
    )(counts, features, positions)


def fitted(function, terms):
    t = 0.125 * (1.0 + np.cos(np.pi * (np.arange(terms) + 0.5) / terms))
    solved = np.linalg.solve(np.vander(t, terms, increasing=True), function(np.sqrt(t)))
    return [float(c) for c in solved]


SIN = fitted(lambda u: math.sqrt(2.0) * np.sin(np.pi * u) / u, 5)
COS = fitted(lambda u: math.sqrt(2.0) * np.cos(np.pi * u), 5)


def poly(coefficients, t):
    acc = t * coefficients[-1] + coefficients[-2]
    for c in coefficients[-3::-1]:
        acc = acc * t + c
    return acc


def turns(u):
    u = u - jnp.round(u)
    t = u * u
    sine = poly(SIN, t) * u
    cosine = poly(COS, t)
    return 1.0 - sine * sine, sine * cosine


def factor_kernel(parts, chunk, first, column_ref, block_ref, *refs):
    before = refs[: 0 if first else parts]
    refs = refs[len(before) :]
    after, wave_ref, refs = refs[:parts], refs[parts], refs[parts + 1 :]
    weight_ref = refs[-1]
    cells, _, slots = block_ref.shape
    channels = after[0].shape[-1]
    span = cells * slots
    total = wave_ref.shape[0] // 2
    at_x = lax.axis_index("gx")
    if first:
        begin = pl.multiple_of(lax.axis_index("gy") * total, total)
        rows = column_ref[:, pl.ds(begin, total)].astype(f32)
        column_ref = refs[0]
        column_ref[...] = jnp.concatenate([rows, jnp.zeros((5, total), f32)], axis=0).T
    for cell in range(cells):
        high, low = split(block_ref[cell, :channels, :])
        for at in (cell * slots, span + cell * slots):
            weight_ref[:channels, at : at + slots] = high
            weight_ref[channels:, at : at + slots] = low

    def some(j, carry):
        here = pl.multiple_of(j * chunk, chunk)
        wave_x = column_ref[pl.ds(here, chunk), 0:1]
        wave_y = column_ref[pl.ds(here, chunk), 1:2]
        wave_z = column_ref[pl.ds(here, chunk), 2:3]
        row = pl.multiple_of(j * 2 * chunk, 2 * chunk)
        for cell in range(cells):
            at = cell * slots
            frac = block_ref[cell, channels + 3 : channels + 6, :]
            u = wave_x * frac[0:1] + wave_y * frac[1:2] + wave_z * frac[2:3]
            cosine, sine = turns(u)
            high, low = split(cosine)
            wave_ref[pl.ds(row, chunk), at : at + slots] = high
            wave_ref[pl.ds(row, chunk), span + at : span + at + slots] = low
            high, low = split(sine)
            wave_ref[pl.ds(row + chunk, chunk), at : at + slots] = high
            wave_ref[pl.ds(row + chunk, chunk), span + at : span + at + slots] = low
        return carry

    lax.fori_loop(0, total // chunk, some, 0, unroll=total // chunk <= 8)
    half = 2 * total // parts
    for n in range(parts):
        row = pl.multiple_of(lax.rem(at_x + n, parts) * half, half)
        both = lax.dot_general(
            wave_ref[pl.ds(row, half), :], weight_ref[...], (((1,), (1,)), ((), ())),
            preferred_element_type=f32,
        )
        both = both[:, :channels] + both[:, channels:]
        after[n][...] = both if first else before[n][...] + both


def partial_factors(columns, total, chunk, block, before, parts):
    cells, rows, slots = block.shape
    channels = rows - 8
    span = cells * slots
    out = [jax.ShapeDtypeStruct((2 * total // parts, channels), f32)] * parts
    out.append(jax.ShapeDtypeStruct((2 * total, 2 * span), bf16))
    if not before:
        out.append(jax.ShapeDtypeStruct((total, 8), f32))
    return pl.pallas_call(
        functools.partial(factor_kernel, parts, chunk, not before),
        in_specs=[whole()] * (2 + len(before)),
        out_specs=[whole()] * len(out),
        out_shape=out,
        input_output_aliases={2 + n: n for n in range(len(before))},
        scratch_shapes=[pltpu.VMEM((2 * channels, 2 * span), bf16)],
        compiler_params=params(),
        cost_estimate=pl.CostEstimate(
            flops=8 * total * span * channels, bytes_accessed=8 * total * span, transcendentals=0
        ),
        name="factors",
    )(columns, block, *before)


def filter_kernel(scale, block_ref, *refs):
    parts, (weight_ref, table_ref, out_ref) = refs[:-3], refs[-3:]
    summed = parts[0][...]
    for part in parts[1:]:
        summed = summed + part[...]
    projected = jnp.dot(summed, weight_ref[...], precision=HIGH, preferred_element_type=f32)
    table = table_ref[...] * scale
    for n in range(0, summed.shape[0], table.shape[0]):
        out_ref[n : n + table.shape[0], :] = projected[n : n + table.shape[0]] * table


def filtered_piece(scale, block, chunk, parts, w_charge, table):
    rows, channels = parts[0].shape
    fixed = pl.BlockSpec((rows, channels), lambda i, block: (0, 0))
    return pl.pallas_call(
        functools.partial(filter_kernel, scale),
        grid_spec=pltpu.PrefetchScalarGridSpec(
            num_scalar_prefetch=1,
            grid=(1,),
            in_specs=[fixed] * len(parts)
            + [
                pl.BlockSpec(w_charge.shape, lambda i, block: (0, 0)),
                pl.BlockSpec((chunk, channels), lambda i, block: (block[0], 0)),
            ],
            out_specs=fixed,
        ),
        out_shape=jax.ShapeDtypeStruct((rows, channels), f32),
        compiler_params=params(),
        name="filter",
    )(block, *parts, w_charge, table)


def potential_kernel(groups, pieces, blocks, *refs):
    held = refs[:groups]
    waves = refs[groups : groups + blocks]
    outs = refs[groups + blocks : -2]
    ordered_ref, turned_ref = refs[-2:]
    channels = ordered_ref.shape[-1]
    piece = held[0].shape[0] // pieces
    for group in range(groups):
        for n in range(pieces):
            rank_x = partner(lax.axis_index("gx"), group, groups)
            rank_z = partner(lax.axis_index("gz"), n, pieces)
            at = pl.multiple_of((rank_x * pieces + rank_z) * piece, piece)
            ordered_ref[pl.ds(at, piece), :] = held[group][n * piece : (n + 1) * piece, :]
    high, low = split(ordered_ref[...].T)
    turned_ref[:channels, :] = high
    turned_ref[channels:, :] = low
    for wave_ref, out in zip(waves, outs):
        cells, _, slots = out.shape
        span = cells * slots
        both = jnp.dot(turned_ref[...], wave_ref[:, :span], preferred_element_type=f32)
        third = jnp.dot(turned_ref[:channels, :], wave_ref[:, span:], preferred_element_type=f32)
        potential = both[:channels] + both[channels:] + third
        for cell in range(cells):
            out[cell] = potential[:, cell * slots : (cell + 1) * slots]


def potentials_of(held, pieces, waves, cells, slots):
    rows = waves[0].shape[0]
    channels = held[0].shape[-1]
    return pl.pallas_call(
        functools.partial(potential_kernel, len(held), pieces, len(waves)),
        in_specs=[whole()] * (len(held) + len(waves)),
        out_specs=[whole()] * len(waves),
        scratch_shapes=[
            pltpu.VMEM((rows, channels), f32),
            pltpu.VMEM((2 * channels, rows), bf16),
        ],
        out_shape=[jax.ShapeDtypeStruct((cells, channels, slots), f32)] * len(waves),
        compiler_params=params(),
        cost_estimate=pl.CostEstimate(
            flops=6 * rows * len(waves) * cells * slots * channels,
            bytes_accessed=4 * rows * len(waves) * cells * slots, transcendentals=0,
        ),
        name="potentials",
    )(*held, *waves)


def message_kernel(
    basis, sources, table, together, once, last, first, own_source, step_ref, mix_ref, value_ref, *refs
):
    blocks, refs = refs[:sources], refs[sources:]
    own_ref = blocks[own_source]
    if last:
        before, refs = refs[:last], refs[last:]
        out_ref, cell_ref, at_ref, own_col_ref, acc_ref, mixed_ref, wide_ref = refs[:7]
    else:
        out_ref, cell_ref, at_ref, own_col_ref, acc_ref = refs[:5]
    left_ref = refs[-1]
    count = step_ref.shape[1]
    cells = acc_ref.shape[0]
    slots = own_ref.shape[-1]
    along, planes = len(table[0]), len(table[0][0])
    channels = value_ref.shape[0]

    for x, columns in enumerate(table):
        for y, column in enumerate(columns):
            for z, choices in enumerate(column):
                n = (x * along + y) * planes + z
                (_, source, index), others = choices[0], choices[1:]
                block = blocks[source][index]
                for condition, source, index in others:
                    block = jnp.where(condition(), blocks[source][index], block)
                high, low = split(block[:channels])
                cell_ref[n, :channels, :] = high
                cell_ref[n, channels:, :] = low
                at_ref[n] = block[channels:]
    for b in range(basis) if last else ():
        high, low = split(value_ref[...] * (mix_ref[b : b + 1, :] * math.exp(-b * b)))
        mixed_ref[b * channels : (b + 1) * channels, :channels] = high
        mixed_ref[b * channels : (b + 1) * channels, channels:] = low
    for cell in range(cells):
        columns = own_ref[first + cell, channels : channels + 8, :].T
        for axis in range(3):
            own_col_ref[cell, axis] = jnp.broadcast_to(columns[:, axis : axis + 1], (slots, slots))

    def fill(step, visit, move):
        place_x = step_ref[0, step] + 1 + (move - 1)
        place_y = step_ref[1, step]
        plane = plane_of(step)
        shift_z = step_ref[3, step].astype(f32)
        own = step_ref[4, step]
        near = []
        for n in range(3):
            number = (place_x * along + place_y + n) * planes + plane
            at = at_ref[number]
            near.append((at[0:1] + float(move - 1), at[1:2] + float(n - 1), at[2:3] + shift_z))
        tile = 32
        for m in range(slots // tile):
            at = m * tile
            own_x = own_col_ref[own, 0, at : at + tile, :]
            own_y = own_col_ref[own, 1, at : at + tile, :]
            own_z = own_col_ref[own, 2, at : at + tile, :]
            for n in range(3):
                dx = near[n][0] - own_x
                dy = near[n][1] - own_y
                dz = near[n][2] - own_z
                squared = dx * dx + dy * dy + dz * dz
                distance = squared * lax.rsqrt(jnp.maximum(squared, 1e-30))
                envelope = jnp.maximum(1.0 - squared, 0.0)
                term = envelope * envelope * jnp.exp2(squared * (-float((basis - 1) ** 2) * LOG2E))
                ratio = jnp.exp2(distance * (2.0 * (basis - 1) * LOG2E))
                if not last and move == 1 and n == 1:
                    i = lax.broadcasted_iota(jnp.int32, (tile, slots), 0) + at
                    j = lax.broadcasted_iota(jnp.int32, (tile, slots), 1)
                    same = jnp.logical_and(i == j, step_ref[3, step] == 0)
                    term = jnp.where(same, 0.0, term)
                for b in range(basis):
                    if b > 0:
                        term = term * ratio
                    high, low = split(term)
                    row = b * slots + at
                    here = 9 * visit + 3 * move + n
                    left_ref[row : row + tile, here * slots : (here + 1) * slots] = high
                    here += 9 * together
                    left_ref[row : row + tile, here * slots : (here + 1) * slots] = low

    def plane_of(step):
        plane = step_ref[2, step]
        return jnp.where(is_even("gz"), plane, 1 - plane) if last else plane

    def near_of(step):
        held = []
        for n in range(together):
            x, y = step_ref[0, step + n], step_ref[1, step + n]
            plane = plane_of(step + n)
            held += [
                cell_ref[((x + over_x) * along + y + over_y) * planes + plane]
                for over_x in range(3)
                for over_y in range(3)
            ]
        return jnp.concatenate(held + held, axis=1)

    def product(step):
        return lax.dot_general(
            left_ref[...], near_of(step), (((1,), (1,)), ((), ())), preferred_element_type=f32
        )

    def visit(group, carry):
        step = group * together
        own = step_ref[4, step]
        for n in range(together):
            for move in range(3):
                fill(step + n, n, move)
        if once:
            acc_ref[own] = product(step)
        else:
            fresh = step_ref[5, step] == 1
            acc_ref[own] = jnp.where(fresh, 0.0, acc_ref[own]) + product(step)
        return carry

    lax.fori_loop(0, count // together, visit, 0)
    wide = basis * channels
    for cell in range(cells):
        gathered = acc_ref[cell, :, :channels] + acc_ref[cell, :, channels:]
        if not last:
            out_ref[cell] = gathered
            continue
        per = cells // last
        high, low = split(gathered + before[cell // per][cell % per])
        here = slice(cell * slots, (cell + 1) * slots)
        for b in range(basis):
            wide_ref[here, b * channels : (b + 1) * channels] = high[b * slots : (b + 1) * slots]
            wide_ref[here, wide + b * channels : wide + (b + 1) * channels] = low[b * slots : (b + 1) * slots]
    if last:
        both = jnp.dot(wide_ref[:, :wide], mixed_ref[...], preferred_element_type=f32)
        both = both + jnp.dot(wide_ref[:, wide:], mixed_ref[...], preferred_element_type=f32)
        for cell in range(cells):
            part = both[cell * slots : (cell + 1) * slots]
            out_ref[cell] = (part[:, :channels] + part[:, channels:]).T


def pair_messages(steps, own, blocks, table, mix, w_value, cells, first, before=()):
    slots = blocks[own].shape[-1]
    basis, channels = mix.shape
    around = len(table) * len(table[0]) * len(table[0][0])
    count = steps.shape[1]
    per_cell = np.bincount(steps[4], minlength=cells)
    once = bool(np.all(per_cell == per_cell[0]))
    together = int(per_cell[0]) if once else 1
    last = len(before)
    sums = (cells, basis * slots, channels)
    closing = [
        pltpu.VMEM((basis * channels, 2 * channels), bf16),
        pltpu.VMEM((cells * slots, 2 * basis * channels), bf16),
    ]
    return pl.pallas_call(
        functools.partial(
            message_kernel, basis, len(blocks), table, together, once, last, first, own
        ),
        in_specs=[pl.BlockSpec(memory_space=pltpu.SMEM)] + [whole()] * (2 + len(blocks) + last),
        out_specs=whole(),
        scratch_shapes=[
            pltpu.VMEM((around, 2 * channels, slots), bf16),
            pltpu.VMEM((around, 8, slots), f32),
            pltpu.VMEM((cells, 3, slots, slots), f32),
            pltpu.VMEM((cells, basis * slots, 2 * channels), f32),
        ]
        + closing * bool(last)
        + [pltpu.VMEM((basis * slots, 18 * together * slots), bf16)],
        out_shape=jax.ShapeDtypeStruct((cells, channels, slots) if last else sums, f32),
        compiler_params=params(),
        cost_estimate=pl.CostEstimate(
            flops=count * 8 * basis * slots * 9 * slots * channels, bytes_accessed=1 << 20,
            transcendentals=0,
        ),
        name="messages",
    )(jnp.asarray(steps), mix, w_value, *blocks, *before)


def visits(cells_x, cells_y, cells_z, inside, first=0, end=None):
    table = []
    for x in range(cells_x):
        for y in range(cells_y):
            for z in range(cells_z):
                own = (x * cells_y + y) * cells_z + z
                if not first <= own < (cells_x * cells_y * cells_z if end is None else end):
                    continue
                for shift in (-1, 0, 1):
                    plane = z + shift
                    if (0 <= plane < cells_z) != inside:
                        continue
                    if not inside:
                        plane = 0 if shift > 0 else 1
                    table.append([x - first // (cells_y * cells_z), y, plane, shift, own - first, 1, 1])
    for one, after in zip(table, table[1:]):
        if one[4] == after[4]:
            one[6] = after[5] = 0
    return np.array(table, np.int32).T.copy()


def mlp_kernel(count, shape, *refs):
    counts_ref, feature_ref = refs[:2]
    message_ref = refs[2]
    potentials = refs[3 : 3 + count]
    hidden_ref, back_ref, out_ref = refs[3 + count :]
    cells, channels, slots = feature_ref.shape
    columns = []
    for cell in range(cells):
        mixed = feature_ref[cell] + message_scale * message_ref[cell]
        for potential in potentials:
            mixed = mixed + potential[cell]
        columns.append(mixed)
    mixed = jnp.concatenate(columns, axis=1)
    inner = lax.dot_general(
        hidden_ref[...], mixed, (((0,), (0,)), ((), ())), precision=HIGH, preferred_element_type=f32
    )
    hidden = inner * jax.nn.sigmoid(inner)
    updated = mixed + lax.dot_general(
        back_ref[...], hidden, (((0,), (0,)), ((), ())), precision=HIGH, preferred_element_type=f32
    )
    slot = lax.broadcasted_iota(jnp.int32, (channels, slots), 1)
    for cell in range(cells):
        part = updated[:, cell * slots : (cell + 1) * slots]
        x, y, z = place_of(cell, shape)
        out_ref[cell] = jnp.where(slot < counts_ref[x, z, y], part, 0.0)


def atom_mlp(shape, counts, features, messages, potentials, w_hidden, w_out):
    return pl.pallas_call(
        functools.partial(mlp_kernel, len(potentials), shape),
        in_specs=[pl.BlockSpec(memory_space=pltpu.SMEM)]
        + [whole()] * (4 + len(potentials)),
        out_specs=whole(),
        out_shape=jax.ShapeDtypeStruct(features.shape, f32),
        compiler_params=params(),
        name="atom_mlp",
    )(counts, features, messages, *potentials, w_hidden, w_out)


def next_in_x(block, shape):
    size = lax.axis_size("gx")
    if size == 2:
        other = exchange(block, "gx", 1)
        return (other, shape[0] - 1), (other, 0)
    wide = block.reshape(shape + block.shape[1:])
    below, above = below_above(wide[:1], wide[-1:], "gx")
    return tuple((side.reshape((-1,) + block.shape[1:]), 0) for side in (below, above))


class Sources:
    def __init__(self):
        self.arrays = []

    def add(self, array):
        for n, held in enumerate(self.arrays):
            if held is array:
                return n
        self.arrays.append(array)
        return len(self.arrays) - 1

    def columns(self, block, shape):
        below, above = next_in_x(block, shape)
        inside = [(self.add(block), x) for x in range(shape[0])]
        return [(self.add(below[0]), below[1])] + inside + [(self.add(above[0]), above[1])]


def always():
    return True


def shards(
    features, positions, counts, waves, filter_table, w_value, w_charge, radial_mix, w_hidden, w_out
):
    shape = cells_x, cells_y, cells_z = features.shape[:3]
    channels, slots = features.shape[3:]
    total_waves = waves.shape[1]
    size_x, size_y, size_z = (lax.axis_size(a) for a in ("gx", "gy", "gz"))
    at_x, at_y, at_z = (lax.axis_index(a) for a in ("gx", "gy", "gz"))
    grid = (cells_x * size_x, cells_y * size_y, cells_z * size_z)
    cells = cells_x * cells_y * cells_z
    some_counts = jnp.transpose(counts, (0, 2, 1))
    flat_features = features.reshape(cells, channels, slots)

    share = total_waves // size_y
    own = pack(shape, grid, some_counts, flat_features, positions.reshape(cells * 3, 1, slots))
    rows = own.shape[1]
    packed = own.reshape(shape + (rows, slots))

    gathered = [own]
    for s in range(1, size_y):
        high = 1 << (s.bit_length() - 1)
        gathered.append(exchange(gathered[s - high], "gy", high))
    if cells_z == 1:
        sides = neighbours(own, own, "gz", same=True)
    else:
        flat = (cells_x * cells_y, rows, slots)
        sides = neighbours(packed[:, :, 0].reshape(flat), packed[:, :, -1].reshape(flat), "gz")

    half = 2 * share // size_x
    piece = half // size_z
    chunk = min(piece, share // size_x)
    first = min(1, size_y - 1)
    late, gathered[first] = lax.optimization_barrier((own, gathered[first]))
    *parts, table, columns = partial_factors(waves, share, chunk, late, (), size_x)
    tables = [table]
    for block in gathered[1:]:
        *parts, table = partial_factors(columns, share, chunk, block, parts, size_x)
        tables.append(table)

    summed = parts[0]
    for s in range(1, size_x):
        other = partner(at_x, s, size_x)
        to = parts[1]
        for n in range(2, size_x):
            to = jnp.where(lax.rem(other - at_x + size_x, size_x) == n, parts[n], to)
        summed = summed + exchange(to, "gx", s)
    low, high = (
        jnp.concatenate(
            [side[n : n + 1] for n in range(y, cells_x * cells_y, cells_y) for side in sides], axis=0
        )
        for y in (0, cells_y - 1)
    )
    edges = neighbours(low, high, "gy")
    value_near, summed = lax.optimization_barrier((w_value, summed))
    pieces = [lax.dynamic_slice_in_dim(summed, at_z * piece, piece, 0)]
    for s in range(1, size_z):
        other = partner(at_z, s, size_z)
        pieces.append(exchange(lax.dynamic_slice_in_dim(summed, other * piece, piece, 0), "gz", s))

    sources = Sources()

    def reaches(step, rank):
        return any(partner(i, step, size_y) == (i + rank) % size_y for i in range(size_y))

    columns = {
        step: sources.columns(block, shape)
        for step, block in enumerate(gathered)
        if any(reaches(step, rank) for rank in (-1, 0, 1))
    }

    def at_rank(step, rank):
        def condition():
            at = lax.axis_index("gy")
            return partner(at, step, size_y) == (at + rank) % size_y

        return condition

    def choices(x, y, z):
        rank = -1 if y < 0 else 1 if y == cells_y else 0
        y = y % cells_y
        found = []
        for step in columns:
            if reaches(step, rank):
                source, from_x = columns[step][x + 1]
                found.append((at_rank(step, rank), source, (from_x * cells_y + y) * cells_z + z))
        return found

    table = [
        [[choices(x, y, z) for z in range(cells_z)] for y in range(-1, cells_y + 1)]
        for x in range(-1, cells_x + 1)
    ]
    layer = cells_y * cells_z
    at_once = (cells_x + 1) // 2
    near = []

    def near_messages(begin, value):
        end = min(begin + at_once, cells_x)
        inner = visits(cells_x, cells_y, cells_z, True, begin * layer, end * layer)
        return pair_messages(
            inner, sources.add(own), sources.arrays, table[begin : end + 2], radial_mix, value,
            (end - begin) * layer, begin * layer,
        )

    near.append(near_messages(0, value_near))

    scale = 1.0 / math.sqrt(grid[0] * grid[1] * grid[2] * slots) / math.sqrt(total_waves)
    rank = at_x * size_z + at_z
    block = at_y * (share // chunk) + (rank * piece) // (2 * chunk)
    charge, near[0] = lax.optimization_barrier((w_charge, near[0]))
    filtered = filtered_piece(scale, block.reshape(1), chunk, pieces, charge, filter_table)

    value_near, filtered = lax.optimization_barrier((w_value, filtered))
    if cells_x > 1:
        near.append(near_messages(at_once, value_near))
    held_z = jnp.concatenate(
        [filtered] + [exchange(filtered, "gz", s) for s in range(1, size_z)], axis=0
    )
    held_z, *rest = lax.optimization_barrier((held_z, *near, *edges))
    near, edges = rest[:-2], rest[-2:]
    held = [held_z] + [exchange(held_z, "gx", s) for s in range(1, size_x)]

    sources = Sources()
    flat = (cells_x, cells_y, 1)
    side_columns = [sources.columns(side, flat) for side in sides]
    edge_columns = [sources.columns(edge, (cells_x, 1, 2)) for edge in edges]

    def choices(x, y, z):
        if 0 <= y < cells_y:
            source, from_x = side_columns[z][x + 1]
            return [(always, source, from_x * cells_y + y)]
        found = []
        for n, columns in enumerate(edge_columns):
            source, from_x = columns[x + 1]
            first_is_here = y == cells_y
            condition = (lambda: is_even("gy")) if (n == 0) == first_is_here else (
                lambda: jnp.logical_not(is_even("gy"))
            )
            found.append((condition, source, from_x * 2 + z))
        return found

    table = [
        [[choices(x, y, z) for z in range(2)] for y in range(-1, cells_y + 1)]
        for x in range(-1, cells_x + 1)
    ]
    found = potentials_of(held, held_z.shape[0] // piece, tables, cells, slots)
    value_far, *found = lax.optimization_barrier((w_value, *found))
    returned = [found[0]] + [exchange(found[s], "gy", s) for s in range(1, size_y)]
    outer = visits(cells_x, cells_y, cells_z, False)
    messages = pair_messages(
        outer, sources.add(own), sources.arrays, table, radial_mix, value_far, cells, 0, near
    )

    updated = atom_mlp(
        shape, some_counts, flat_features, messages, returned, w_hidden, w_out
    )
    return updated.reshape(features.shape)


def solution(mesh):
    placed = (
        P("gx", "gy", "gz", None, None),
        P("gx", "gy", "gz", None, None),
        P("gx", "gy", "gz"),
        P(),
        P(),
        P(),
        P(),
        P(),
        P(),
        P(),
    )
    return jax.shard_map(
        shards,
        mesh=mesh,
        in_specs=placed,
        out_specs=P("gx", "gy", "gz", None, None),
        check_vma=False,
    )
```

```python
import functools
import math

import numpy as np

import jax
import jax.numpy as jnp
from jax import lax
from jax.experimental import pallas as pl
from jax.experimental.pallas import tpu as pltpu
from jax.sharding import PartitionSpec as P


HIGH = lax.Precision.HIGH
message_scale = 0.125
bf16 = jnp.bfloat16
f32 = jnp.float32
VMEM_LIMIT = 28 * 1024 * 1024
PACK_LIMIT = 62 * 1024 * 1024


LOG2E = math.log2(math.e)


def partner(i, step, count):
    return i ^ step


def exchange(block, axis, step):
    count = lax.axis_size(axis)
    pairs = [(i, partner(i, step, count)) for i in range(count)]
    return lax.ppermute(block, axis, pairs)


def is_even(axis):
    if lax.axis_size(axis) % 2:
        return jnp.bool_(True)
    return lax.rem(lax.axis_index(axis), 2) == 0


def neighbours(low, high, axis, same=False):
    count = lax.axis_size(axis)
    if count == 1:
        return low, high
    if count % 2:
        up = lax.ppermute(low, axis, [(i, (i - 1) % count) for i in range(count)])
        down = lax.ppermute(high, axis, [(i, (i + 1) % count) for i in range(count)])
        return up, down
    even = is_even(axis)
    first = high if same else jnp.where(even, high, low)
    second = low if same else jnp.where(even, low, high)
    one = [(i, i ^ 1) for i in range(count)]
    two = [(i, (i + 1 if i % 2 else i - 1) % count) for i in range(count)]
    return lax.ppermute(first, axis, one), lax.ppermute(second, axis, two)


def below_above(low, high, axis):
    first, second = neighbours(low, high, axis)
    even = is_even(axis)
    return jnp.where(even, second, first), jnp.where(even, first, second)


def split(x):
    high = x.astype(bf16)
    low = (x - high.astype(f32)).astype(bf16)
    return high, low


def whole():
    return pl.BlockSpec(memory_space=pltpu.VMEM)


def params(limit=VMEM_LIMIT):
    return pltpu.CompilerParams(vmem_limit_bytes=limit)


def place_of(cell, shape):
    return cell // (shape[1] * shape[2]), cell // shape[2] % shape[1], cell % shape[2]


def pack_kernel(
    shape, grid, counts_hbm, feature_hbm, position_hbm, out_ref,
    counts_ref, feature_ref, position_ref, sems,
):
    cells, channels, slots = feature_ref.shape
    copies = [
        pltpu.make_async_copy(counts_hbm, counts_ref, sems.at[0]),
        pltpu.make_async_copy(position_hbm, position_ref, sems.at[1]),
        pltpu.make_async_copy(feature_hbm, feature_ref, sems.at[2]),
    ]
    for copy in copies:
        copy.start()
    for copy in copies:
        copy.wait()
    slot = lax.broadcasted_iota(jnp.int32, (channels, slots), 1)
    for cell in range(cells):
        place = place_of(cell, shape)
        held = slot < counts_ref[place[0], place[2], place[1]]
        out_ref[cell, :channels, :] = jnp.where(held, feature_ref[cell], 0.0)
        at = [position_ref[3 * cell + axis] for axis in range(3)]
        rows = list(at)
        for axis, name in enumerate(("gx", "gy", "gz")):
            here = lax.axis_index(name) * shape[axis] + place[axis]
            rows.append((at[axis] + here.astype(f32)) * (1.0 / grid[axis]))
        out_ref[cell, channels:, :] = jnp.concatenate(rows + [jnp.zeros((2, slots), f32)], axis=0)


def pack(shape, grid, counts, features, positions):
    cells, channels, slots = features.shape
    return pl.pallas_call(
        functools.partial(pack_kernel, shape, grid),
        in_specs=[pl.BlockSpec(memory_space=pltpu.HBM)] * 3,
        out_specs=whole(),
        out_shape=jax.ShapeDtypeStruct((cells, channels + 8, slots), f32),
        scratch_shapes=[
            pltpu.SMEM(counts.shape, jnp.int32),
            pltpu.VMEM(features.shape, f32),
            pltpu.VMEM(positions.shape, f32),
            pltpu.SemaphoreType.DMA((3,)),
        ],
        compiler_params=params(),
        name="pack",
    )(counts, features, positions)


def fitted(function, terms):
    t = 0.125 * (1.0 + np.cos(np.pi * (np.arange(terms) + 0.5) / terms))
    solved = np.linalg.solve(np.vander(t, terms, increasing=True), function(np.sqrt(t)))
    return [float(c) for c in solved]


SIN = fitted(lambda u: math.sqrt(2.0) * np.sin(np.pi * u) / u, 5)
COS = fitted(lambda u: math.sqrt(2.0) * np.cos(np.pi * u), 5)


def poly(coefficients, t):
    acc = t * coefficients[-1] + coefficients[-2]
    for c in coefficients[-3::-1]:
        acc = acc * t + c
    return acc


def turns(u):
    u = u - jnp.round(u)
    t = u * u
    sine = poly(SIN, t) * u
    cosine = poly(COS, t)
    return 1.0 - sine * sine, sine * cosine


def factor_kernel(parts, chunk, first, count, column_ref, *refs):
    blocks, refs = refs[:count], refs[count:]
    before = refs[: 0 if first else parts]
    refs = refs[len(before) :]
    after, wave_ref, refs = refs[:parts], refs[parts], refs[parts + 1 :]
    weight_ref = refs[-1]
    cells, _, slots = blocks[0].shape
    channels = after[0].shape[-1]
    span = cells * slots
    total = wave_ref.shape[0] // 2
    at_x = lax.axis_index("gx")
    if first:
        begin = pl.multiple_of(lax.axis_index("gy") * total, total)
        rows = column_ref[:, pl.ds(begin, total)].astype(f32)
        column_ref = refs[0]
        column_ref[...] = jnp.concatenate([rows, jnp.zeros((5, total), f32)], axis=0).T
    places = [
        (block_ref, cell, 2 * span * n + cell * slots)
        for n, block_ref in enumerate(blocks)
        for cell in range(cells)
    ]
    for block_ref, cell, here in places:
        high, low = split(block_ref[cell, :channels, :])
        for at in (here, span + here):
            weight_ref[:channels, at : at + slots] = high
            weight_ref[channels:, at : at + slots] = low

    def some(j, carry):
        here = pl.multiple_of(j * chunk, chunk)
        wave_x = column_ref[pl.ds(here, chunk), 0:1]
        wave_y = column_ref[pl.ds(here, chunk), 1:2]
        wave_z = column_ref[pl.ds(here, chunk), 2:3]
        row = pl.multiple_of(j * 2 * chunk, 2 * chunk)
        for block_ref, cell, at in places:
            frac = block_ref[cell, channels + 3 : channels + 6, :]
            u = wave_x * frac[0:1] + wave_y * frac[1:2] + wave_z * frac[2:3]
            cosine, sine = turns(u)
            high, low = split(cosine)
            wave_ref[pl.ds(row, chunk), at : at + slots] = high
            wave_ref[pl.ds(row, chunk), span + at : span + at + slots] = low
            high, low = split(sine)
            wave_ref[pl.ds(row + chunk, chunk), at : at + slots] = high
            wave_ref[pl.ds(row + chunk, chunk), span + at : span + at + slots] = low
        return carry

    lax.fori_loop(0, total // chunk, some, 0, unroll=total // chunk <= 8)
    half = 2 * total // parts
    for n in range(parts):
        row = pl.multiple_of(lax.rem(at_x + n, parts) * half, half)
        both = lax.dot_general(
            wave_ref[pl.ds(row, half), :], weight_ref[...], (((1,), (1,)), ((), ())),
            preferred_element_type=f32,
        )
        both = both[:, :channels] + both[:, channels:]
        after[n][...] = both if first else before[n][...] + both


def partial_factors(columns, total, chunk, blocks, before, parts):
    cells, rows, slots = blocks[0].shape
    channels = rows - 8
    span = len(blocks) * cells * slots
    out = [jax.ShapeDtypeStruct((2 * total // parts, channels), f32)] * parts
    out.append(jax.ShapeDtypeStruct((2 * total, 2 * span), bf16))
    if not before:
        out.append(jax.ShapeDtypeStruct((total, 8), f32))
    return pl.pallas_call(
        functools.partial(factor_kernel, parts, chunk, not before, len(blocks)),
        in_specs=[whole()] * (1 + len(blocks) + len(before)),
        out_specs=[whole()] * len(out),
        out_shape=out,
        input_output_aliases={1 + len(blocks) + n: n for n in range(len(before))},
        scratch_shapes=[pltpu.VMEM((2 * channels, 2 * span), bf16)],
        compiler_params=params(),
        cost_estimate=pl.CostEstimate(
            flops=8 * total * span * channels, bytes_accessed=8 * total * span, transcendentals=0
        ),
        name="factors",
    )(columns, *blocks, *before)


def filter_kernel(scale, block_ref, *refs):
    parts, (weight_ref, table_ref, out_ref) = refs[:-3], refs[-3:]
    summed = parts[0][...]
    for part in parts[1:]:
        summed = summed + part[...]
    projected = jnp.dot(summed, weight_ref[...], precision=HIGH, preferred_element_type=f32)
    table = table_ref[...] * scale
    for n in range(0, summed.shape[0], table.shape[0]):
        out_ref[n : n + table.shape[0], :] = projected[n : n + table.shape[0]] * table


def filtered_piece(scale, block, chunk, parts, w_charge, table):
    rows, channels = parts[0].shape
    fixed = pl.BlockSpec((rows, channels), lambda i, block: (0, 0))
    return pl.pallas_call(
        functools.partial(filter_kernel, scale),
        grid_spec=pltpu.PrefetchScalarGridSpec(
            num_scalar_prefetch=1,
            grid=(1,),
            in_specs=[fixed] * len(parts)
            + [
                pl.BlockSpec(w_charge.shape, lambda i, block: (0, 0)),
                pl.BlockSpec((chunk, channels), lambda i, block: (block[0], 0)),
            ],
            out_specs=fixed,
        ),
        out_shape=jax.ShapeDtypeStruct((rows, channels), f32),
        compiler_params=params(),
        name="filter",
    )(block, *parts, w_charge, table)


def potential_kernel(groups, pieces, blocks, *refs):
    held = refs[:groups]
    waves = refs[groups : groups + blocks]
    outs = refs[groups + blocks : -2]
    ordered_ref, turned_ref = refs[-2:]
    channels = ordered_ref.shape[-1]
    piece = held[0].shape[0] // pieces
    for group in range(groups):
        for n in range(pieces):
            rank_x = partner(lax.axis_index("gx"), group, groups)
            rank_z = partner(lax.axis_index("gz"), n, pieces)
            at = pl.multiple_of((rank_x * pieces + rank_z) * piece, piece)
            ordered_ref[pl.ds(at, piece), :] = held[group][n * piece : (n + 1) * piece, :]
    high, low = split(ordered_ref[...].T)
    turned_ref[:channels, :] = high
    turned_ref[channels:, :] = low
    cells, _, slots = outs[0].shape
    span = cells * slots
    places = [(wave_ref, at) for wave_ref in waves for at in range(0, wave_ref.shape[1], 2 * span)]
    for (wave_ref, at), out in zip(places, outs):
        both = jnp.dot(turned_ref[...], wave_ref[:, at : at + span], preferred_element_type=f32)
        third = jnp.dot(
            turned_ref[:channels, :], wave_ref[:, at + span : at + 2 * span], preferred_element_type=f32
        )
        potential = both[:channels] + both[channels:] + third
        for cell in range(cells):
            out[cell] = potential[:, cell * slots : (cell + 1) * slots]


def potentials_of(held, pieces, waves, cells, slots):
    rows = waves[0].shape[0]
    channels = held[0].shape[-1]
    count = sum(table.shape[1] for table in waves) // (2 * cells * slots)
    return pl.pallas_call(
        functools.partial(potential_kernel, len(held), pieces, len(waves)),
        in_specs=[whole()] * (len(held) + len(waves)),
        out_specs=[whole()] * count,
        scratch_shapes=[
            pltpu.VMEM((rows, channels), f32),
            pltpu.VMEM((2 * channels, rows), bf16),
        ],
        out_shape=[jax.ShapeDtypeStruct((cells, channels, slots), f32)] * count,
        compiler_params=params(),
        cost_estimate=pl.CostEstimate(
            flops=6 * rows * count * cells * slots * channels,
            bytes_accessed=4 * rows * count * cells * slots, transcendentals=0,
        ),
        name="potentials",
    )(*held, *waves)


def message_kernel(
    basis, sources, table, together, once, last, first, own_source, step_ref, mix_ref, value_ref, *refs
):
    blocks, refs = refs[:sources], refs[sources:]
    own_ref = blocks[own_source]
    if last:
        before, refs = refs[:last], refs[last:]
        out_ref, cell_ref, at_ref, own_col_ref, acc_ref, mixed_ref, wide_ref = refs[:7]
    else:
        out_ref, cell_ref, at_ref, own_col_ref, acc_ref = refs[:5]
    left_ref = refs[-1]
    count = step_ref.shape[1]
    cells = acc_ref.shape[0]
    slots = own_ref.shape[-1]
    along, planes = len(table[0]), len(table[0][0])
    channels = value_ref.shape[0]

    for x, columns in enumerate(table):
        for y, column in enumerate(columns):
            for z, choices in enumerate(column):
                n = (x * along + y) * planes + z
                (_, source, index), others = choices[0], choices[1:]
                block = blocks[source][index]
                for condition, source, index in others:
                    block = jnp.where(condition(), blocks[source][index], block)
                high, low = split(block[:channels])
                cell_ref[n, :channels, :] = high
                cell_ref[n, channels:, :] = low
                at_ref[n] = block[channels:]
    for b in range(basis) if last else ():
        high, low = split(value_ref[...] * (mix_ref[b : b + 1, :] * math.exp(-b * b)))
        mixed_ref[b * channels : (b + 1) * channels, :channels] = high
        mixed_ref[b * channels : (b + 1) * channels, channels:] = low
    for cell in range(cells):
        columns = own_ref[first + cell, channels : channels + 8, :].T
        for axis in range(3):
            own_col_ref[cell, axis] = jnp.broadcast_to(columns[:, axis : axis + 1], (slots, slots))

    def fill(step, visit, move):
        place_x = step_ref[0, step] + 1 + (move - 1)
        place_y = step_ref[1, step]
        plane = plane_of(step)
        shift_z = step_ref[3, step].astype(f32)
        own = step_ref[4, step]
        near = []
        for n in range(3):
            number = (place_x * along + place_y + n) * planes + plane
            at = at_ref[number]
            near.append((at[0:1] + float(move - 1), at[1:2] + float(n - 1), at[2:3] + shift_z))
        tile = 32
        for m in range(slots // tile):
            at = m * tile
            own_x = own_col_ref[own, 0, at : at + tile, :]
            own_y = own_col_ref[own, 1, at : at + tile, :]
            own_z = own_col_ref[own, 2, at : at + tile, :]
            for n in range(3):
                dx = near[n][0] - own_x
                dy = near[n][1] - own_y
                dz = near[n][2] - own_z
                squared = dx * dx + dy * dy + dz * dz
                distance = squared * lax.rsqrt(jnp.maximum(squared, 1e-30))
                envelope = jnp.maximum(1.0 - squared, 0.0)
                term = envelope * envelope * jnp.exp2(squared * (-float((basis - 1) ** 2) * LOG2E))
                ratio = jnp.exp2(distance * (2.0 * (basis - 1) * LOG2E))
                if not last and move == 1 and n == 1:
                    i = lax.broadcasted_iota(jnp.int32, (tile, slots), 0) + at
                    j = lax.broadcasted_iota(jnp.int32, (tile, slots), 1)
                    same = jnp.logical_and(i == j, step_ref[3, step] == 0)
                    term = jnp.where(same, 0.0, term)
                for b in range(basis):
                    if b > 0:
                        term = term * ratio
                    high, low = split(term)
                    row = b * slots + at
                    here = 9 * visit + 3 * move + n
                    left_ref[row : row + tile, here * slots : (here + 1) * slots] = high
                    here += 9 * together
                    left_ref[row : row + tile, here * slots : (here + 1) * slots] = low

    def plane_of(step):
        plane = step_ref[2, step]
        return jnp.where(is_even("gz"), plane, 1 - plane) if last else plane

    def near_of(step):
        held = []
        for n in range(together):
            x, y = step_ref[0, step + n], step_ref[1, step + n]
            plane = plane_of(step + n)
            held += [
                cell_ref[((x + over_x) * along + y + over_y) * planes + plane]
                for over_x in range(3)
                for over_y in range(3)
            ]
        return jnp.concatenate(held + held, axis=1)

    def product(step):
        return lax.dot_general(
            left_ref[...], near_of(step), (((1,), (1,)), ((), ())), preferred_element_type=f32
        )

    def visit(group, carry):
        step = group * together
        own = step_ref[4, step]
        for n in range(together):
            for move in range(3):
                fill(step + n, n, move)
        if once:
            acc_ref[own] = product(step)
        else:
            fresh = step_ref[5, step] == 1
            acc_ref[own] = jnp.where(fresh, 0.0, acc_ref[own]) + product(step)
        return carry

    lax.fori_loop(0, count // together, visit, 0)
    wide = basis * channels
    for cell in range(cells):
        gathered = acc_ref[cell, :, :channels] + acc_ref[cell, :, channels:]
        if not last:
            out_ref[cell] = gathered
            continue
        per = cells // last
        high, low = split(gathered + before[cell // per][cell % per])
        here = slice(cell * slots, (cell + 1) * slots)
        for b in range(basis):
            wide_ref[here, b * channels : (b + 1) * channels] = high[b * slots : (b + 1) * slots]
            wide_ref[here, wide + b * channels : wide + (b + 1) * channels] = low[b * slots : (b + 1) * slots]
    if last:
        both = jnp.dot(wide_ref[:, :wide], mixed_ref[...], preferred_element_type=f32)
        both = both + jnp.dot(wide_ref[:, wide:], mixed_ref[...], preferred_element_type=f32)
        for cell in range(cells):
            part = both[cell * slots : (cell + 1) * slots]
            out_ref[cell] = (part[:, :channels] + part[:, channels:]).T


def pair_messages(steps, own, blocks, table, mix, w_value, cells, first, before=()):
    slots = blocks[own].shape[-1]
    basis, channels = mix.shape
    around = len(table) * len(table[0]) * len(table[0][0])
    count = steps.shape[1]
    per_cell = np.bincount(steps[4], minlength=cells)
    once = bool(np.all(per_cell == per_cell[0]))
    together = int(per_cell[0]) if once else 1
    last = len(before)
    sums = (cells, basis * slots, channels)
    closing = [
        pltpu.VMEM((basis * channels, 2 * channels), bf16),
        pltpu.VMEM((cells * slots, 2 * basis * channels), bf16),
    ]
    return pl.pallas_call(
        functools.partial(
            message_kernel, basis, len(blocks), table, together, once, last, first, own
        ),
        in_specs=[pl.BlockSpec(memory_space=pltpu.SMEM)] + [whole()] * (2 + len(blocks) + last),
        out_specs=whole(),
        scratch_shapes=[
            pltpu.VMEM((around, 2 * channels, slots), bf16),
            pltpu.VMEM((around, 8, slots), f32),
            pltpu.VMEM((cells, 3, slots, slots), f32),
            pltpu.VMEM((cells, basis * slots, 2 * channels), f32),
        ]
        + closing * bool(last)
        + [pltpu.VMEM((basis * slots, 18 * together * slots), bf16)],
        out_shape=jax.ShapeDtypeStruct((cells, channels, slots) if last else sums, f32),
        compiler_params=params(),
        cost_estimate=pl.CostEstimate(
            flops=count * 8 * basis * slots * 9 * slots * channels, bytes_accessed=1 << 20,
            transcendentals=0,
        ),
        name="messages",
    )(jnp.asarray(steps), mix, w_value, *blocks, *before)


def visits(cells_x, cells_y, cells_z, inside, first=0, end=None):
    table = []
    for x in range(cells_x):
        for y in range(cells_y):
            for z in range(cells_z):
                own = (x * cells_y + y) * cells_z + z
                if not first <= own < (cells_x * cells_y * cells_z if end is None else end):
                    continue
                for shift in (-1, 0, 1):
                    plane = z + shift
                    if (0 <= plane < cells_z) != inside:
                        continue
                    if not inside:
                        plane = 0 if shift > 0 else 1
                    table.append([x - first // (cells_y * cells_z), y, plane, shift, own - first, 1, 1])
    for one, after in zip(table, table[1:]):
        if one[4] == after[4]:
            one[6] = after[5] = 0
    return np.array(table, np.int32).T.copy()


def mlp_kernel(count, shape, *refs):
    counts_ref, feature_ref = refs[:2]
    message_ref = refs[2]
    potentials = refs[3 : 3 + count]
    hidden_ref, back_ref, out_ref = refs[3 + count :]
    cells, channels, slots = feature_ref.shape
    columns = []
    for cell in range(cells):
        mixed = feature_ref[cell] + message_scale * message_ref[cell]
        for potential in potentials:
            mixed = mixed + potential[cell]
        columns.append(mixed)
    mixed = jnp.concatenate(columns, axis=1)
    inner = lax.dot_general(
        hidden_ref[...], mixed, (((0,), (0,)), ((), ())), precision=HIGH, preferred_element_type=f32
    )
    hidden = inner * jax.nn.sigmoid(inner)
    updated = mixed + lax.dot_general(
        back_ref[...], hidden, (((0,), (0,)), ((), ())), precision=HIGH, preferred_element_type=f32
    )
    slot = lax.broadcasted_iota(jnp.int32, (channels, slots), 1)
    for cell in range(cells):
        part = updated[:, cell * slots : (cell + 1) * slots]
        x, y, z = place_of(cell, shape)
        out_ref[cell] = jnp.where(slot < counts_ref[x, z, y], part, 0.0)


def atom_mlp(shape, counts, features, messages, potentials, w_hidden, w_out):
    return pl.pallas_call(
        functools.partial(mlp_kernel, len(potentials), shape),
        in_specs=[pl.BlockSpec(memory_space=pltpu.SMEM)]
        + [whole()] * (4 + len(potentials)),
        out_specs=whole(),
        out_shape=jax.ShapeDtypeStruct(features.shape, f32),
        compiler_params=params(),
        name="atom_mlp",
    )(counts, features, messages, *potentials, w_hidden, w_out)


def next_in_x(block, shape):
    size = lax.axis_size("gx")
    if size == 2:
        other = exchange(block, "gx", 1)
        return (other, shape[0] - 1), (other, 0)
    wide = block.reshape(shape + block.shape[1:])
    below, above = below_above(wide[:1], wide[-1:], "gx")
    return tuple((side.reshape((-1,) + block.shape[1:]), 0) for side in (below, above))


class Sources:
    def __init__(self):
        self.arrays = []

    def add(self, array):
        for n, held in enumerate(self.arrays):
            if held is array:
                return n
        self.arrays.append(array)
        return len(self.arrays) - 1

    def columns(self, block, shape):
        below, above = next_in_x(block, shape)
        inside = [(self.add(block), x) for x in range(shape[0])]
        return [(self.add(below[0]), below[1])] + inside + [(self.add(above[0]), above[1])]


def always():
    return True


def shards(
    features, positions, counts, waves, filter_table, w_value, w_charge, radial_mix, w_hidden, w_out
):
    shape = cells_x, cells_y, cells_z = features.shape[:3]
    channels, slots = features.shape[3:]
    total_waves = waves.shape[1]
    size_x, size_y, size_z = (lax.axis_size(a) for a in ("gx", "gy", "gz"))
    at_x, at_y, at_z = (lax.axis_index(a) for a in ("gx", "gy", "gz"))
    grid = (cells_x * size_x, cells_y * size_y, cells_z * size_z)
    cells = cells_x * cells_y * cells_z
    some_counts = jnp.transpose(counts, (0, 2, 1))
    flat_features = features.reshape(cells, channels, slots)

    share = total_waves // size_y
    own = pack(shape, grid, some_counts, flat_features, positions.reshape(cells * 3, 1, slots))
    rows = own.shape[1]
    packed = own.reshape(shape + (rows, slots))

    gathered = [own]
    for s in range(1, size_y):
        high = 1 << (s.bit_length() - 1)
        gathered.append(exchange(gathered[s - high], "gy", high))
    if cells_z == 1:
        sides = neighbours(own, own, "gz", same=True)
    else:
        flat = (cells_x * cells_y, rows, slots)
        sides = neighbours(packed[:, :, 0].reshape(flat), packed[:, :, -1].reshape(flat), "gz")

    half = 2 * share // size_x
    piece = half // size_z
    chunk = min(piece, share // size_x)
    most = min(2, size_y)
    *parts, table, columns = partial_factors(waves, share, chunk, gathered[:most], (), size_x)
    tables = [table]
    for block in gathered[most:]:
        *parts, table = partial_factors(columns, share, chunk, [block], parts, size_x)
        tables.append(table)

    summed = parts[0]
    for s in range(1, size_x):
        other = partner(at_x, s, size_x)
        to = parts[1]
        for n in range(2, size_x):
            to = jnp.where(lax.rem(other - at_x + size_x, size_x) == n, parts[n], to)
        summed = summed + exchange(to, "gx", s)
    low, high = (
        jnp.concatenate(
            [side[n : n + 1] for n in range(y, cells_x * cells_y, cells_y) for side in sides], axis=0
        )
        for y in (0, cells_y - 1)
    )
    edges = neighbours(low, high, "gy")
    value_near, summed = lax.optimization_barrier((w_value, summed))
    pieces = [lax.dynamic_slice_in_dim(summed, at_z * piece, piece, 0)]
    for s in range(1, size_z):
        other = partner(at_z, s, size_z)
        pieces.append(exchange(lax.dynamic_slice_in_dim(summed, other * piece, piece, 0), "gz", s))

    sources = Sources()

    def reaches(step, rank):
        return any(partner(i, step, size_y) == (i + rank) % size_y for i in range(size_y))

    columns = {
        step: sources.columns(block, shape)
        for step, block in enumerate(gathered)
        if any(reaches(step, rank) for rank in (-1, 0, 1))
    }

    def at_rank(step, rank):
        def condition():
            at = lax.axis_index("gy")
            return partner(at, step, size_y) == (at + rank) % size_y

        return condition

    def choices(x, y, z):
        rank = -1 if y < 0 else 1 if y == cells_y else 0
        y = y % cells_y
        found = []
        for step in columns:
            if reaches(step, rank):
                source, from_x = columns[step][x + 1]
                found.append((at_rank(step, rank), source, (from_x * cells_y + y) * cells_z + z))
        return found

    table = [
        [[choices(x, y, z) for z in range(cells_z)] for y in range(-1, cells_y + 1)]
        for x in range(-1, cells_x + 1)
    ]
    layer = cells_y * cells_z
    at_once = (cells_x + 1) // 2
    near = []

    def near_messages(begin, value):
        end = min(begin + at_once, cells_x)
        inner = visits(cells_x, cells_y, cells_z, True, begin * layer, end * layer)
        return pair_messages(
            inner, sources.add(own), sources.arrays, table[begin : end + 2], radial_mix, value,
            (end - begin) * layer, begin * layer,
        )

    near.append(near_messages(0, value_near))

    scale = 1.0 / math.sqrt(grid[0] * grid[1] * grid[2] * slots) / math.sqrt(total_waves)
    rank = at_x * size_z + at_z
    block = at_y * (share // chunk) + (rank * piece) // (2 * chunk)
    charge, near[0] = lax.optimization_barrier((w_charge, near[0]))
    filtered = filtered_piece(scale, block.reshape(1), chunk, pieces, charge, filter_table)

    value_near, filtered = lax.optimization_barrier((w_value, filtered))
    if cells_x > 1:
        near.append(near_messages(at_once, value_near))
    held_z = jnp.concatenate(
        [filtered] + [exchange(filtered, "gz", s) for s in range(1, size_z)], axis=0
    )
    held_z, *rest = lax.optimization_barrier((held_z, *near, *edges))
    near, edges = rest[:-2], rest[-2:]
    held = [held_z] + [exchange(held_z, "gx", s) for s in range(1, size_x)]

    sources = Sources()
    flat = (cells_x, cells_y, 1)
    side_columns = [sources.columns(side, flat) for side in sides]
    edge_columns = [sources.columns(edge, (cells_x, 1, 2)) for edge in edges]

    def choices(x, y, z):
        if 0 <= y < cells_y:
            source, from_x = side_columns[z][x + 1]
            return [(always, source, from_x * cells_y + y)]
        found = []
        for n, columns in enumerate(edge_columns):
            source, from_x = columns[x + 1]
            first_is_here = y == cells_y
            condition = (lambda: is_even("gy")) if (n == 0) == first_is_here else (
                lambda: jnp.logical_not(is_even("gy"))
            )
            found.append((condition, source, from_x * 2 + z))
        return found

    table = [
        [[choices(x, y, z) for z in range(2)] for y in range(-1, cells_y + 1)]
        for x in range(-1, cells_x + 1)
    ]
    found = potentials_of(held, held_z.shape[0] // piece, tables, cells, slots)
    value_far, *found = lax.optimization_barrier((w_value, *found))
    returned = [found[0]] + [exchange(found[s], "gy", s) for s in range(1, size_y)]
    outer = visits(cells_x, cells_y, cells_z, False)
    messages = pair_messages(
        outer, sources.add(own), sources.arrays, table, radial_mix, value_far, cells, 0, near
    )

    updated = atom_mlp(
        shape, some_counts, flat_features, messages, returned, w_hidden, w_out
    )
    return updated.reshape(features.shape)


def solution(mesh):
    placed = (
        P("gx", "gy", "gz", None, None),
        P("gx", "gy", "gz", None, None),
        P("gx", "gy", "gz"),
        P(),
        P(),
        P(),
        P(),
        P(),
        P(),
        P(),
    )
    return jax.shard_map(
        shards,
        mesh=mesh,
        in_specs=placed,
        out_specs=P("gx", "gy", "gz", None, None),
        check_vma=False,
    )
```
